128 devices in a mesh: ctx: 8 (over x_hi, y), head: 8 (over z, core), var: 2 (over x_lo).
Axes of the slice: x: 4 (x_hi: 2, x_lo: 2; x = x_hi * 2 + x_lo), y: 4, z: 4, core: 2. Of those that a mesh axis runs over, the one named last changes fastest.
Arguments:
- sequence: bfloat16 [4096, 1536], P('ctx', 'head'), may hold values from -8 to 8
- deletions: int32 [8, 2], P('var'), parts along dimension 0, may hold values from 0 to 4096, as said below
- conv_taps: float32 [3, 1536], P(None, 'head'), may hold values from -3 to 3
- conv_bias: float32 [1536], P('head'), may hold values from -3 to 3
- w_proj: bfloat16 [1536, 3584], P(None, 'head'), may hold values from -1 to 1
- w_out: bfloat16 [1536, 1536], P('head'), may hold values from -0.15625 to 0.15625
- w_pair: bfloat16 [1536, 256], P('head'), may hold values from -0.15625 to 0.15625
- dist_table: float32 [16, 128], replicated, may hold values from -3 to 3
Outputs:
- pair_map: bfloat16 [8, 1024, 1024, 128], P('var', 'ctx', 'head'), parts along dimension 0
The draws below stay inside these ranges and needn't reach their ends.
There are 2 independent parts, one for each index of `var`. The reference program is written for one: setup_inputs(seed, part) draws one part's arguments, and reference() takes and returns one part's arrays. A program takes and returns all parts, laid end to end along the dimension named above; an argument that names none is the same for every part. Nothing has to cross between parts.
Inputs may be any that keep to these rules, and one draw needn't show every extreme that they name: `deletions`: each variant deletes 1 to 128 consecutive tokens, some variant deletes exactly 128, and some variant's deletion ends at the last token of the locus.
All inputs are finite; a program needn't handle non-finite values.
Results may differ from the reference program's by a relative error of at most 0.025.
Values may be sent and summed in bfloat16 or wider, within the bound.
A program may use at most 128 MiB of HBM per device.

```python
import math
import jax
import jax.numpy as jnp
from jax import lax

MODEL_WIDTH = 1536
H = 8
HD = 128
VD = 192
C = 128
NB = 16
POOL = 4
VARS = 4
LOCUS_TOKENS = 4096
DILATION_STEP = 256
DEL_MAX = 128
PAIR_ROWS = 1024
N_HEAD = 8


def draw_sequence(key, part):
    return jnp.clip(jax.random.normal(key, (LOCUS_TOKENS, MODEL_WIDTH), jnp.float32), -6.0, 6.0).astype(jnp.bfloat16)


def draw_w_proj(key, part):
    first_key = jax.random.fold_in(key, 0)
    spread = 1.0 / math.sqrt(MODEL_WIDTH)
    normal_part = jnp.clip(jax.random.normal(first_key, (MODEL_WIDTH, H * (2 * HD + VD)), jnp.float32), -6.0, 6.0)
    return (normal_part * spread).astype(jnp.bfloat16)


def draw_deletions(key, part):
    first_key, second_key, third_key, fourth_key = jax.random.split(key, 4)
    starts = jax.random.randint(first_key, (VARS,), 0, LOCUS_TOKENS - DEL_MAX + 1)
    lengths = jax.random.randint(second_key, (VARS,), 1, DEL_MAX + 1)
    chosen = jax.random.randint(third_key, (), 0, VARS)
    lengths = jnp.where(jnp.arange(VARS) == chosen, DEL_MAX, lengths)
    at_end = jax.random.randint(fourth_key, (), 0, VARS)
    starts = jnp.where(jnp.arange(VARS) == at_end, LOCUS_TOKENS - lengths, starts)
    return jnp.stack([starts, starts + lengths], 1).astype(jnp.int32)


def shard_levels(rng, dims, pieces, low, high):
    def one(axis_at, blocks):
        steps = jax.random.uniform(jax.random.fold_in(jax.random.fold_in(rng, 6), axis_at), (blocks,), jnp.float32, low / len(pieces), high / len(pieces))
        return jnp.repeat(jnp.exp(steps), dims[axis_at] // blocks).reshape((-1,) + (1,) * (len(dims) - axis_at - 1))

    loudness = one(*pieces[0])
    for cut in pieces[1:]:
        loudness = loudness * one(*cut)
    return loudness


def bell_draw(rng, extent, deviation, reach, cuts=(), kind=jnp.bfloat16):
    drawn = deviation * jax.random.normal(rng, extent, jnp.float32)
    if cuts:
        drawn = drawn * shard_levels(rng, extent, cuts, -0.22, 0.18)
    return jnp.clip(drawn, -reach, reach).astype(kind)


def setup_inputs(seed: int = 0, part: int = 0) -> dict:
    splits = jax.random.split(jax.random.key(seed), 9)
    part_splits = jax.random.split(jax.random.fold_in(splits[8], part), 9)
    sequence = draw_sequence(jax.random.fold_in(splits[8], 71), part)
    deletions = draw_deletions(jax.random.fold_in(jax.random.fold_in(splits[8], part), 71), part)
    conv_taps = bell_draw(splits[2], (3, MODEL_WIDTH), 0.5, 3.0, ((1, 8),), jnp.float32)
    conv_bias = bell_draw(splits[3], (MODEL_WIDTH,), 0.5, 3.0, ((0, 8),), jnp.float32)
    w_proj = draw_w_proj(jax.random.fold_in(splits[8], 71), part)
    w_out = bell_draw(splits[5], (H * VD, MODEL_WIDTH), (H * VD) ** -0.5, 0.15625, ((0, 8),))
    w_pair = bell_draw(splits[6], (MODEL_WIDTH, 2 * C), MODEL_WIDTH ** -0.5, 0.15625, ((0, 8),))
    dist_table = bell_draw(splits[7], (NB, C), 0.5, 3.0, (), jnp.float32)
    return dict(sequence=sequence, deletions=deletions, conv_taps=conv_taps, conv_bias=conv_bias, w_proj=w_proj, w_out=w_out, w_pair=w_pair, dist_table=dist_table)


def bucket_of(distance):
    buckets = jnp.zeros(distance.shape, jnp.int32)
    for power_index in range(NB - 1):
        buckets = buckets + (distance >= 2 ** power_index).astype(jnp.int32)
    return buckets

def attend_head(operands):
    queries, key_rows, value_rows = operands
    scores = jnp.dot(queries, key_rows.T, preferred_element_type=jnp.float32) / math.sqrt(HD)
    row_max = scores.max(1, keepdims=True)
    weights = jnp.exp(scores - row_max)
    row_sum = weights.sum(1, keepdims=True)
    return jnp.dot(weights.astype(jnp.bfloat16), value_rows, preferred_element_type=jnp.float32) / row_sum

def one_variant(deletion, sequence, conv_taps, conv_bias, w_proj, w_out, w_pair, dist_table):
    positions = jnp.arange(LOCUS_TOKENS, dtype=jnp.int32)
    kept_bins = jnp.logical_or(positions < deletion[0], positions >= deletion[1])
    masked = jnp.where(kept_bins[:, None], sequence, jnp.zeros((), sequence.dtype))
    widened_rows = masked.astype(jnp.float32)
    zeroed_rows = jnp.zeros((DILATION_STEP, MODEL_WIDTH), jnp.float32)
    preceding_rows = jnp.concatenate([zeroed_rows, widened_rows[:LOCUS_TOKENS - DILATION_STEP]], 0)
    following_rows = jnp.concatenate([widened_rows[DILATION_STEP:], zeroed_rows], 0)
    convolved = conv_taps[0] * preceding_rows + conv_taps[1] * widened_rows + conv_taps[2] * following_rows + conv_bias
    trunk_out = (widened_rows + jax.nn.gelu(convolved, approximate=True)).astype(jnp.bfloat16)
    projected = jnp.dot(trunk_out, w_proj, preferred_element_type=jnp.float32).astype(jnp.bfloat16)
    projected = projected.reshape(LOCUS_TOKENS, H, 2 * HD + VD).transpose(1, 0, 2)
    head_out = lax.map(attend_head, (projected[:, :, :HD], projected[:, :, HD:2 * HD], projected[:, :, 2 * HD:]))
    head_out = head_out.transpose(1, 0, 2).reshape(LOCUS_TOKENS, H * VD).astype(jnp.bfloat16)
    group_width = H // N_HEAD * VD
    grouped = head_out.reshape(LOCUS_TOKENS, N_HEAD, group_width).transpose(1, 0, 2)
    w_groups = w_out.reshape(N_HEAD, group_width, MODEL_WIDTH)
    partial_value = jnp.einsum('gtc,gcd->gtd', grouped.astype(jnp.float32), w_groups.astype(jnp.float32)).astype(jnp.bfloat16)
    residual = trunk_out.astype(jnp.float32) + partial_value.astype(jnp.float32).sum(0)
    pooled = residual.reshape(PAIR_ROWS, POOL, MODEL_WIDTH).mean(1).astype(jnp.bfloat16)
    pair_proj = jnp.dot(pooled, w_pair, preferred_element_type=jnp.float32)
    pair_ids = jnp.arange(PAIR_ROWS, dtype=jnp.int32)
    distance = jnp.abs(pair_ids[:, None] - pair_ids[None, :])
    rel_table = dist_table[bucket_of(distance)]
    return (pair_proj[:, None, :C] + pair_proj[None, :, C:] + rel_table).astype(jnp.bfloat16)

def reference(sequence, deletions, conv_taps, conv_bias, w_proj, w_out, w_pair, dist_table):
    return lax.map(lambda deletion: one_variant(deletion, sequence, conv_taps, conv_bias, w_proj, w_out, w_pair, dist_table), deletions)
```

```python
import functools
import math

import jax
import jax.numpy as jnp
from jax import lax
from jax.experimental import pallas as pl
from jax.experimental.pallas import tpu as pltpu
from jax.sharding import PartitionSpec as P

HD = 128
VD = 192
C = 128
NB = 16
POOL = 4
DIL = 256
DEL = 128
SEGS = 3
BIG = -1e30
QSCALE = math.log2(math.e) / math.sqrt(HD)


def changed(delta, length):
    hit = jnp.logical_and(delta >= 0, delta < length)
    for shift in (-DIL, DIL):
        moved = delta + shift
        hit = jnp.logical_or(hit, jnp.logical_and(moved >= 0, moved < length))
    return hit


def attention_kernel(dels, q_ref, kv_ref, mod_ref, mix_ref, out_ref, k_aug, v_aug, m_aug, mv_aug):
    tokens = q_ref.shape[0]
    total = kv_ref.shape[0]
    variants = dels.shape[0]
    per = mod_ref.shape[0] // variants
    lane = lax.broadcasted_iota(jnp.int32, (1, 128), 1)
    first = jnp.zeros((1, 128), jnp.int32)
    length = jnp.zeros((1, 128), jnp.int32)
    for v in range(variants):
        first = jnp.where(lane == v, dels[v, 0], first)
        length = jnp.where(lane == v, dels[v, 1] - dels[v, 0], length)
    ones = jnp.where(lax.broadcasted_iota(jnp.int32, (1, 64), 1) == 0, 1.0, 0.0).astype(jnp.bfloat16)
    k_aug[:, :HD] = kv_ref[:, :HD]
    pos = lax.broadcasted_iota(jnp.int32, (total, 128), 0)
    k_aug[:, HD:] = jnp.where(changed(pos - first, length), BIG, 0.0).astype(jnp.bfloat16)
    v_aug[:, :VD] = kv_ref[:, HD:]
    v_aug[:, VD:] = jnp.broadcast_to(ones, (total, 64))
    m_aug[:, :HD] = mod_ref[:, HD : 2 * HD]
    mv_aug[:, :VD] = mod_ref[:, 2 * HD :]
    mv_aug[:, VD:] = jnp.broadcast_to(ones, (variants * per, 64))
    row = lax.broadcasted_iota(jnp.int32, (per, 128), 0)
    half = row // (per // 2)
    seg = (row % (per // 2)) // (DEL // 2)
    step = half * (DEL // 2) + row % (DEL // 2)
    for v in range(variants):
        token = dels[v, 0] + (seg - 1) * DIL + step
        valid = (step < dels[v, 1] - dels[v, 0]) & (token >= 0) & (token < total)
        m_aug[v * per : (v + 1) * per, HD:] = jnp.where(valid, 0.0, BIG).astype(jnp.bfloat16)

    start = lax.axis_index("ctx") * tokens
    col = lax.broadcasted_iota(jnp.int32, (tokens, per), 1)
    qpos = lax.broadcasted_iota(jnp.int32, (tokens, per), 0) + start
    col_half = col // (per // 2)
    col_seg = (col % (per // 2)) // (DEL // 2)
    col_step = col_half * (DEL // 2) + col % (DEL // 2)
    pool = (
        lax.broadcasted_iota(jnp.int32, (tokens // POOL, tokens), 1) // POOL
        == lax.broadcasted_iota(jnp.int32, (tokens // POOL, tokens), 0)
    ).astype(jnp.bfloat16)
    tile = 1024

    def one(v, _):
        s0 = dels[v, 0]
        ln = dels[v, 1] - s0
        place = jnp.logical_and(qpos == s0 + (col_seg - 1) * DIL + col_step, col_step < ln)
        moved = jnp.dot(
            place.astype(jnp.bfloat16),
            mod_ref[pl.ds(pl.multiple_of(v * per, per), per), :HD],
            preferred_element_type=jnp.float32,
        )
        is_mod = changed(qpos[:, :128] - s0, ln)
        queries = jnp.where(is_mod, moved, q_ref[...].astype(jnp.float32)).astype(jnp.bfloat16)
        pick = jnp.broadcast_to(jnp.where(lane == v, 1.0, 0.0), (tokens, 128)).astype(jnp.bfloat16)
        q_aug = jnp.concatenate([queries, pick], axis=1)
        top = jnp.full((tokens, 1), -3e38, jnp.float32)
        acc = jnp.zeros((tokens, 256), jnp.float32)

        def step_on(keys, values, top, acc):
            s = lax.dot_general(q_aug, keys, (((1,), (1,)), ((), ())), preferred_element_type=jnp.float32)
            new = jnp.maximum(top, s.max(1, keepdims=True))
            w = jnp.exp2(s - new).astype(jnp.bfloat16)
            acc = acc * jnp.exp2(top - new) + jnp.dot(w, values, preferred_element_type=jnp.float32)
            return new, acc

        for t in range(total // tile):
            rows = slice(t * tile, (t + 1) * tile)
            top, acc = step_on(k_aug[rows], v_aug[rows], top, acc)
        rows = pl.ds(pl.multiple_of(v * per, per), per)
        top, acc = step_on(m_aug[rows], mv_aug[rows], top, acc)
        out = (acc[:, :VD] / acc[:, VD : VD + 1]).astype(jnp.bfloat16)
        pooled = jnp.dot(pool, out, preferred_element_type=jnp.float32) * (1.0 / POOL)
        out_ref[v] = jnp.dot(pooled.astype(jnp.bfloat16), mix_ref[...], preferred_element_type=jnp.float32)
        return 0

    lax.fori_loop(0, variants, one, 0)


def attention(deletions, queries, kv, mod, mix):
    variants = deletions.shape[0]
    tokens = queries.shape[0]
    total = kv.shape[0]
    vm = pl.BlockSpec(memory_space=pltpu.VMEM)
    return pl.pallas_call(
        attention_kernel,
        out_shape=jax.ShapeDtypeStruct((variants, tokens // POOL, 2 * C), jnp.float32),
        in_specs=[pl.BlockSpec(memory_space=pltpu.SMEM), vm, vm, vm, vm],
        out_specs=vm,
        scratch_shapes=[
            pltpu.VMEM((total, 2 * HD), jnp.bfloat16),
            pltpu.VMEM((total, 256), jnp.bfloat16),
            pltpu.VMEM((mod.shape[0], 2 * HD), jnp.bfloat16),
            pltpu.VMEM((mod.shape[0], 256), jnp.bfloat16),
        ],
        compiler_params=pltpu.CompilerParams(vmem_limit_bytes=56 * 2**20),
    )(deletions, queries, kv, mod, mix)


def pair_kernel(rows_per, row_ref, col_ref, table_ref, out_ref, rel):
    step = pl.program_id(0)
    span = col_ref.shape[1]
    row_count = row_ref.shape[1]

    @pl.when(step == 0)
    def _():
        base = lax.axis_index("head") * span - lax.axis_index("ctx") * row_count - (row_count - 1)
        dist = jnp.abs(lax.broadcasted_iota(jnp.int32, rel.shape, 0) + base)
        value = jnp.broadcast_to(table_ref[0:1, :], rel.shape)
        for k in range(NB - 1):
            value = jnp.where(dist >= 2**k, table_ref[k + 1 : k + 2, :], value)
        rel[...] = value

    def one(i, _):
        row = step * rows_per + i
        shifted = rel[pl.ds(row_count - 1 - row, span), :]
        for v in range(row_ref.shape[0]):
            out_ref[v, i] = (row_ref[v, pl.ds(row, 1), :] + (col_ref[v] + shifted)).astype(out_ref.dtype)
        return 0

    lax.fori_loop(0, rows_per, one, 0)


def pair_map(row_feats, col_feats, table):
    variants, rows, _ = row_feats.shape
    cols = col_feats.shape[1]
    per = 8
    vm = pl.BlockSpec(memory_space=pltpu.VMEM)
    return pl.pallas_call(
        functools.partial(pair_kernel, per),
        grid=(rows // per,),
        out_shape=jax.ShapeDtypeStruct((variants, rows, cols, C), jnp.bfloat16),
        in_specs=[vm, vm, vm],
        out_specs=pl.BlockSpec((variants, per, cols, C), lambda i: (0, i, 0, 0)),
        scratch_shapes=[pltpu.VMEM((rows + cols, C), jnp.float32)],
        compiler_params=pltpu.CompilerParams(vmem_limit_bytes=32 * 2**20),
    )(row_feats, col_feats, table)


def local(sequence, deletions, conv_taps, conv_bias, w_proj, w_out, w_pair, dist_table):
    tokens, width = sequence.shape
    variants = deletions.shape[0]
    ctx = lax.axis_index("ctx")
    n_ctx = lax.axis_size("ctx")
    forward = [(i, i + 1) for i in range(n_ctx - 1)]
    backward = [(b, a) for a, b in forward]
    low = lax.ppermute(sequence[tokens - DIL :], "ctx", forward)
    high = lax.ppermute(sequence[:DIL], "ctx", backward)
    pair_weights = lax.all_gather(w_pair, "head", axis=0, tiled=True)
    mix = jnp.dot(w_out, pair_weights, preferred_element_type=jnp.float32).astype(jnp.bfloat16)

    ext = jnp.concatenate([low, sequence, high], 0)
    start = ctx * tokens
    pos = start - DIL + jnp.arange(tokens + 2 * DIL, dtype=jnp.int32)
    dels = jnp.concatenate([deletions, jnp.zeros((1, 2), jnp.int32)], 0)
    kept = jnp.logical_or(pos[None] < dels[:, :1], pos[None] >= dels[:, 1:])
    masked = jnp.where(kept[:, :, None], ext[None], jnp.zeros((), jnp.bfloat16)).astype(jnp.float32)
    conv = (
        conv_taps[0] * masked[:, :tokens]
        + conv_taps[1] * masked[:, DIL : DIL + tokens]
        + conv_taps[2] * masked[:, 2 * DIL :]
        + conv_bias
    )
    trunk = (masked[:, DIL : DIL + tokens] + jax.nn.gelu(conv, approximate=True)).astype(jnp.bfloat16)
    base, own = trunk[variants], trunk[:variants]
    pooled = own.astype(jnp.float32).reshape(variants, tokens // POOL, POOL, width).mean(2).astype(jnp.bfloat16)

    per = SEGS * DEL
    r = jnp.arange(per, dtype=jnp.int32)
    offset = ((r % (per // 2)) // (DEL // 2) - 1) * DIL + (r // (per // 2)) * (DEL // 2) + r % (DEL // 2)
    token = deletions[:, :1] + offset[None]
    pick = (token[:, :, None] == (start + jnp.arange(tokens, dtype=jnp.int32))[None, None]).astype(jnp.bfloat16)
    moved = jnp.einsum("vrt,vtd->vrd", pick, own, preferred_element_type=jnp.float32).astype(jnp.bfloat16)
    share = variants * per // n_ctx
    mod = lax.psum_scatter(moved.reshape(variants * per, width), "ctx", scatter_dimension=0, tiled=True)
    rows = lax.all_gather(jnp.concatenate([base, mod], 0), "head", axis=1, tiled=True)
    proj = jnp.dot(rows, w_proj, preferred_element_type=jnp.float32)
    proj = jnp.concatenate([proj[:, :HD] * QSCALE, proj[:, HD:]], 1).astype(jnp.bfloat16)
    kv = lax.all_gather(proj[:tokens, HD:], "ctx", axis=0, tiled=True)
    mod_all = lax.all_gather(proj[tokens:], "ctx", axis=0, tiled=True)
    part = attention(deletions, proj[:tokens, :HD], kv, mod_all, mix)
    part = part + jnp.einsum("vpd,dc->vpc", pooled, w_pair, preferred_element_type=jnp.float32)
    pair = lax.psum(part.astype(jnp.bfloat16), "head")
    cols = lax.all_gather(pair[:, :, C:], "ctx", axis=1, tiled=True)
    count = cols.shape[1] // lax.axis_size("head")
    cols = lax.dynamic_slice_in_dim(cols, lax.axis_index("head") * count, count, 1)
    return pair_map(pair[:, :, :C].astype(jnp.float32), cols.astype(jnp.float32), dist_table)


def solution(mesh):
    in_specs = (
        P("ctx", "head"),
        P("var", None),
        P(None, "head"),
        P("head"),
        P(None, "head"),
        P("head", None),
        P("head", None),
        P(),
    )
    out_specs = P("var", "ctx", "head", None)
    return jax.shard_map(local, mesh=mesh, in_specs=in_specs, out_specs=out_specs, check_vma=False)
```

```python
import functools
import math

import jax
import jax.numpy as jnp
from jax import lax
from jax.experimental import pallas as pl
from jax.experimental.pallas import tpu as pltpu
from jax.sharding import PartitionSpec as P

HD = 128
VD = 192
C = 128
NB = 16
POOL = 4
DIL = 256
DEL = 128
SEGS = 3
BIG = -1e30
QSCALE = math.log2(math.e) / math.sqrt(HD)


def changed(delta, length):
    hit = jnp.logical_and(delta >= 0, delta < length)
    for shift in (-DIL, DIL):
        moved = delta + shift
        hit = jnp.logical_or(hit, jnp.logical_and(moved >= 0, moved < length))
    return hit


def attention_kernel(dels, q_ref, kv_ref, mod_ref, mix_ref, pooled_ref, wp_ref, out_ref, k_aug, v_aug, m_aug, mv_aug, mq):
    tokens = q_ref.shape[0]
    blocks = kv_ref.shape[0]
    total = tokens * blocks
    variants = dels.shape[0]
    share = SEGS * DEL // 2
    per = 2 * share
    lane = lax.broadcasted_iota(jnp.int32, (1, 128), 1)
    first = jnp.zeros((1, 128), jnp.int32)
    length = jnp.zeros((1, 128), jnp.int32)
    for v in range(variants):
        first = jnp.where(lane == v, dels[v, 0], first)
        length = jnp.where(lane == v, dels[v, 1] - dels[v, 0], length)
    one_lane = jnp.where(lane == VD - 128, 1.0, 0.0).astype(jnp.bfloat16)

    def spread(tail):
        both = jnp.concatenate([tail, jnp.concatenate([tail[:, 64:], tail[:, :64]], axis=1)], axis=0)
        keep = lax.broadcasted_iota(jnp.int32, both.shape, 1) < VD - 128
        return jnp.where(keep, both, jnp.broadcast_to(one_lane, both.shape))

    for b in range(blocks):
        rows = slice(b * tokens, (b + 1) * tokens)
        k_aug[rows, :HD] = kv_ref[b, :tokens]
        v_aug[rows, :128] = kv_ref[b, tokens : 2 * tokens]
        v_aug[rows, 128:] = spread(kv_ref[b, 2 * tokens :])
        pos = lax.broadcasted_iota(jnp.int32, (tokens, 128), 0) + b * tokens
        k_aug[rows, HD:] = jnp.where(changed(pos - first, length), BIG, 0.0).astype(jnp.bfloat16)
        rows = slice(b * share, (b + 1) * share)
        mq[rows] = mod_ref[b, :share]
        m_aug[rows, :HD] = mod_ref[b, share : 2 * share]
        mv_aug[rows, :128] = mod_ref[b, 2 * share : 3 * share]
        mv_aug[rows, 128:] = spread(mod_ref[b, 3 * share :])
    row = lax.broadcasted_iota(jnp.int32, (per, 128), 0)
    half = row // (per // 2)
    seg = (row % (per // 2)) // (DEL // 2)
    step = half * (DEL // 2) + row % (DEL // 2)
    for v in range(variants):
        token = dels[v, 0] + (seg - 1) * DIL + step
        valid = (step < dels[v, 1] - dels[v, 0]) & (token >= 0) & (token < total)
        m_aug[v * per : (v + 1) * per, HD:] = jnp.where(valid, 0.0, BIG).astype(jnp.bfloat16)

    start = lax.axis_index("ctx") * tokens
    col = lax.broadcasted_iota(jnp.int32, (tokens, per), 1)
    qpos = lax.broadcasted_iota(jnp.int32, (tokens, per), 0) + start
    col_half = col // (per // 2)
    col_seg = (col % (per // 2)) // (DEL // 2)
    col_step = col_half * (DEL // 2) + col % (DEL // 2)
    pool = (
        lax.broadcasted_iota(jnp.int32, (tokens // POOL, tokens), 1) // POOL
        == lax.broadcasted_iota(jnp.int32, (tokens // POOL, tokens), 0)
    ).astype(jnp.bfloat16)
    tile = 1024

    def one(v, _):
        s0 = dels[v, 0]
        ln = dels[v, 1] - s0
        place = jnp.logical_and(qpos == s0 + (col_seg - 1) * DIL + col_step, col_step < ln)
        moved = jnp.dot(
            place.astype(jnp.bfloat16),
            mq[pl.ds(pl.multiple_of(v * per, per), per), :],
            preferred_element_type=jnp.float32,
        )
        is_mod = changed(qpos[:, :128] - s0, ln)
        queries = jnp.where(is_mod, moved, q_ref[...].astype(jnp.float32)).astype(jnp.bfloat16)
        pick = jnp.broadcast_to(jnp.where(lane == v, 1.0, 0.0), (tokens, 128)).astype(jnp.bfloat16)
        q_aug = jnp.concatenate([queries, pick], axis=1)
        top = jnp.full((tokens, 1), -3e38, jnp.float32)
        acc = jnp.zeros((tokens, 256), jnp.float32)

        def step_on(keys, values, top, acc):
            s = lax.dot_general(q_aug, keys, (((1,), (1,)), ((), ())), preferred_element_type=jnp.float32)
            new = jnp.maximum(top, s.max(1, keepdims=True))
            w = jnp.exp2(s - new).astype(jnp.bfloat16)
            acc = acc * jnp.exp2(top - new) + jnp.dot(w, values, preferred_element_type=jnp.float32)
            return new, acc

        for t in range(total // tile):
            rows = slice(t * tile, (t + 1) * tile)
            top, acc = step_on(k_aug[rows], v_aug[rows], top, acc)
        rows = pl.ds(pl.multiple_of(v * per, per), per)
        top, acc = step_on(m_aug[rows], mv_aug[rows], top, acc)
        out = (acc[:, :VD] / acc[:, VD : VD + 1]).astype(jnp.bfloat16)
        pooled = jnp.dot(pool, out, preferred_element_type=jnp.float32) * (1.0 / POOL)
        out_ref[v] = jnp.dot(
            pooled.astype(jnp.bfloat16), mix_ref[...], preferred_element_type=jnp.float32
        ) + jnp.dot(pooled_ref[v], wp_ref[...], preferred_element_type=jnp.float32)
        return 0

    lax.fori_loop(0, variants, one, 0)


def attention(deletions, queries, kv, mod, mix, pooled, w_pair):
    variants = deletions.shape[0]
    tokens = queries.shape[0]
    total = kv.shape[0] * tokens
    changed_rows = variants * SEGS * DEL
    vm = pl.BlockSpec(memory_space=pltpu.VMEM)
    return pl.pallas_call(
        attention_kernel,
        out_shape=jax.ShapeDtypeStruct((variants, tokens // POOL, 2 * C), jnp.float32),
        in_specs=[pl.BlockSpec(memory_space=pltpu.SMEM)] + [vm] * 6,
        out_specs=vm,
        scratch_shapes=[
            pltpu.VMEM((total, 2 * HD), jnp.bfloat16),
            pltpu.VMEM((total, 256), jnp.bfloat16),
            pltpu.VMEM((changed_rows, 2 * HD), jnp.bfloat16),
            pltpu.VMEM((changed_rows, 256), jnp.bfloat16),
            pltpu.VMEM((changed_rows, HD), jnp.bfloat16),
        ],
        compiler_params=pltpu.CompilerParams(vmem_limit_bytes=56 * 2**20),
    )(deletions, queries, kv, mod, mix, pooled, w_pair)


def pair_kernel(rows_per, row_ref, col_ref, table_ref, out_ref, rel):
    step = pl.program_id(0)
    span = col_ref.shape[1]
    row_count = row_ref.shape[1]

    @pl.when(step == 0)
    def _():
        base = lax.axis_index("head") * span - lax.axis_index("ctx") * row_count - (row_count - 1)
        dist = jnp.abs(lax.broadcasted_iota(jnp.int32, rel.shape, 0) + base)
        value = jnp.broadcast_to(table_ref[0:1, :], rel.shape)
        for k in range(NB - 1):
            value = jnp.where(dist >= 2**k, table_ref[k + 1 : k + 2, :], value)
        rel[...] = value

    def one(i, _):
        row = step * rows_per + i
        shifted = rel[pl.ds(row_count - 1 - row, span), :]
        for v in range(row_ref.shape[0]):
            out_ref[v, i] = (row_ref[v, pl.ds(row, 1), :] + (col_ref[v] + shifted)).astype(out_ref.dtype)
        return 0

    lax.fori_loop(0, rows_per, one, 0)


def pair_map(row_feats, col_feats, table):
    variants, rows, _ = row_feats.shape
    cols = col_feats.shape[1]
    per = 8
    vm = pl.BlockSpec(memory_space=pltpu.VMEM)
    return pl.pallas_call(
        functools.partial(pair_kernel, per),
        grid=(rows // per,),
        out_shape=jax.ShapeDtypeStruct((variants, rows, cols, C), jnp.bfloat16),
        in_specs=[vm, vm, vm],
        out_specs=pl.BlockSpec((variants, per, cols, C), lambda i: (0, i, 0, 0)),
        scratch_shapes=[pltpu.VMEM((rows + cols, C), jnp.float32)],
        compiler_params=pltpu.CompilerParams(vmem_limit_bytes=32 * 2**20),
    )(row_feats, col_feats, table)


MESH = pl.DeviceIdType.MESH


def pack(x):
    half = x.shape[0] // 2
    tail = jnp.concatenate([x[:half, 128:], x[half:, 128:]], axis=1)
    return jnp.concatenate([x[:, :128], tail], axis=0)


class Ring:
    def __init__(self, make, buf, rows, base, me, dn, up, far, mate, mate_of, to_dn, to_up, to_mate):
        half = rows // 2
        self.full, self.lo, self.hi = pl.ds(0, rows), pl.ds(0, half), pl.ds(half, half)
        self.make, self.buf, self.base = make, buf, base
        self.me, self.dn, self.up, self.far, self.mate, self.mate_of = me, dn, up, far, mate, mate_of
        self.to_dn, self.to_up, self.to_mate = to_dn, to_up, to_mate
        self.sent = []

    def copy(self, slot, rows, index, target):
        ref = self.buf.at[slot, rows]
        return self.make(ref, ref, self.base + index, target)

    def send(self, slot, rows, index, target):
        made = self.copy(slot, rows, index, target)
        made.start()
        self.sent.append(made)

    def got(self, slot, rows, index):
        self.copy(slot, rows, index, self.to_up).wait_recv()


class HeadRing(Ring):
    def begin(self):
        self.send(self.me, self.full, 0, self.to_up)
        self.send(self.me, self.full, 1, self.to_dn)
        self.send(self.me, self.full, 2, self.to_mate)

    def relay(self):
        self.got(self.dn, self.full, 0)
        self.send(self.dn, self.lo, 3, self.to_up)
        self.send(self.dn, self.full, 4, self.to_mate)
        self.got(self.up, self.full, 1)
        self.send(self.up, self.hi, 5, self.to_dn)
        self.send(self.up, self.full, 6, self.to_mate)

    def end(self):
        self.got(self.far, self.lo, 3)
        self.send(self.far, self.lo, 7, self.to_mate)
        self.got(self.far, self.hi, 5)
        self.send(self.far, self.hi, 8, self.to_mate)
        self.got(self.mate, self.full, 2)
        self.got(self.mate_of(self.dn), self.full, 4)
        self.got(self.mate_of(self.up), self.full, 6)
        self.got(self.mate_of(self.far), self.lo, 7)
        self.got(self.mate_of(self.far), self.hi, 8)

    def drain(self):
        for made in self.sent:
            made.wait_send()


class TokenRing(Ring):
    def begin(self):
        self.send(self.me, self.full, 2, self.to_mate)
        self.send(self.me, self.full, 0, self.to_up)
        self.send(self.me, self.full, 1, self.to_dn)

    def cross(self):
        self.got(self.mate, self.full, 2)
        self.send(self.mate, self.full, 4, self.to_up)
        self.send(self.mate, self.full, 6, self.to_dn)

    def relay(self):
        self.got(self.dn, self.full, 0)
        self.send(self.dn, self.lo, 3, self.to_up)
        self.got(self.up, self.full, 1)
        self.send(self.up, self.hi, 5, self.to_dn)

    def relay_mate(self):
        dn, up = self.mate_of(self.dn), self.mate_of(self.up)
        self.got(dn, self.full, 4)
        self.send(dn, self.lo, 7, self.to_up)
        self.got(up, self.full, 6)
        self.send(up, self.hi, 8, self.to_dn)

    def end(self):
        self.got(self.far, self.lo, 3)
        self.got(self.far, self.hi, 5)
        self.got(self.mate_of(self.far), self.lo, 7)
        self.got(self.mate_of(self.far), self.hi, 8)

    def drain(self):
        for made in self.sent:
            made.wait_send()


def rows_kernel(dels, seq, taps, bias, w_ref, wo_ref, wp_ref,
                q_out, kv_out, mod_out, pooled_out, mix_out,
                low, high, gb, gm, wp, moved, landed, kv, mod, wb1, wb2, proj, projm, send, recv):
    tokens, width = seq.shape
    variants = dels.shape[0]
    c, h, g = lax.axis_index("ctx"), lax.axis_index("head"), lax.axis_index("var")
    n = 8
    dn_h, up_h, far_h = lax.rem(h + 6, n), lax.rem(h + 2, n), lax.rem(h + 4, n)
    sib = h + 1 - 2 * lax.rem(h, 2)
    x0, y0 = c // 4 * 4, lax.rem(c, 4)
    up_c, dn_c, far_c = x0 + lax.rem(y0 + 1, 4), x0 + lax.rem(y0 + 3, 4), x0 + lax.rem(y0 + 2, 4)
    xp = lax.rem(c + 4, n)
    other = lambda t: lax.rem(t + 4, n)
    sib_of = lambda t: t + 1 - 2 * lax.rem(t, 2)

    barrier = pltpu.get_barrier_semaphore()
    peers = [{"ctx": lax.rem(c + k, n)} for k in range(1, n)]
    peers += [{"head": dn_h}, {"head": up_h}, {"head": sib}, {"ctx": xp, "var": 1 - g}]
    for peer in peers:
        pl.semaphore_signal(barrier, inc=1, device_id=peer, device_id_type=MESH)
    pl.semaphore_wait(barrier, len(peers))

    def make(src, dst, index, target):
        return pltpu.make_async_remote_copy(
            src_ref=src, dst_ref=dst, send_sem=send.at[index], recv_sem=recv.at[index],
            device_id=target, device_id_type=MESH,
        )

    right, left = {"ctx": lax.rem(c + 1, n)}, {"ctx": lax.rem(c + 7, n)}
    halo_low = make(seq.at[pl.ds(tokens - DIL, DIL)], low, 0, right)
    halo_high = make(seq.at[pl.ds(0, DIL)], high, 1, left)
    halo_low.start()
    halo_high.start()

    def head_ring(buf, rows, base):
        return HeadRing(make, buf, rows, base, h, dn_h, up_h, far_h, sib, sib_of,
                        {"head": dn_h}, {"head": up_h}, {"head": sib})

    def token_ring(buf, rows, base, to_mate):
        return TokenRing(make, buf, rows, base, c, dn_c, up_c, far_c, xp, other,
                         {"ctx": dn_c}, {"ctx": up_c}, to_mate)

    ring_b = head_ring(gb, gb.shape[1], 10)
    ring_m = head_ring(gm, gm.shape[1], 20)
    ring_p = head_ring(wp, wp.shape[1], 30)
    ring_k = token_ring(kv, kv.shape[1], 40, {"ctx": xp, "var": 1 - g})
    ring_o = token_ring(mod, mod.shape[1], 50, {"ctx": xp})

    wp[h] = wp_ref[...]

    zero = jnp.zeros((64, w_ref.shape[1]), jnp.bfloat16)
    for k in range(n):
        part = w_ref[k * 192 + 128 : k * 192 + 192, :]
        wb1[k * 128 : k * 128 + 64, :] = part
        wb1[k * 128 + 64 : k * 128 + 128, :] = zero
        wb2[k * 128 : k * 128 + 64, :] = zero
        wb2[k * 128 + 64 : k * 128 + 128, :] = part

    halo_low.wait()
    halo_high.wait()
    pos = lax.broadcasted_iota(jnp.int32, (tokens, width), 0) + c * tokens
    tap0, tap1, tap2 = taps[0:1, :], taps[1:2, :], taps[2:3, :]

    def row_block(first, length, lo, hi):
        def masked(ref, begin, shift):
            x = ref[begin : begin + DIL].astype(jnp.float32)
            d = pos[lo:hi] + shift - first
            return jnp.where((d >= 0) & (d < length), 0.0, x)

        if lo == 0:
            before = jnp.where(c == 0, 0.0, masked(low, 0, -DIL))
            after = masked(seq, DIL, DIL)
        else:
            before = masked(seq, 0, -DIL)
            after = jnp.where(c == n - 1, 0.0, masked(high, 0, DIL))
        here = masked(seq, lo, 0)
        conv = tap0 * before + tap1 * here + tap2 * after + bias[...]
        return (here + jax.nn.gelu(conv, approximate=True)).astype(jnp.bfloat16)

    def trunk(first, length):
        return jnp.concatenate([row_block(first, length, 0, DIL), row_block(first, length, DIL, 2 * DIL)], axis=0)

    gb[h] = pack(trunk(0, 0))
    ring_b.begin()

    share = SEGS * DEL // 2
    r = lax.broadcasted_iota(jnp.int32, (share, tokens), 0)
    offset = (r // (DEL // 2) - 1) * DIL + r % (DEL // 2)
    here = lax.broadcasted_iota(jnp.int32, (share, tokens), 1) + c * tokens
    pool = (
        lax.broadcasted_iota(jnp.int32, (tokens // POOL, tokens), 1) // POOL
        == lax.broadcasted_iota(jnp.int32, (tokens // POOL, tokens), 0)
    ).astype(jnp.bfloat16)

    def variant(v, _):
        first = dels[v, 0]
        own = trunk(first, dels[v, 1] - first)
        for half in range(2):
            pick = (here == offset + (first + half * (DEL // 2))).astype(jnp.bfloat16)
            moved[2 * v + half] = pack(jnp.dot(pick, own, preferred_element_type=jnp.float32).astype(jnp.bfloat16))
        pooled_out[v] = (jnp.dot(pool, own, preferred_element_type=jnp.float32) * (1.0 / POOL)).astype(jnp.bfloat16)
        return 0

    lax.fori_loop(0, variants, variant, 0)
    shared = []
    for k in range(1, n):
        to = lax.rem(c + k, n)
        made = make(moved.at[to], landed.at[k - 1], 1 + k, {"ctx": to})
        made.start()
        shared.append(made)
    ring_p.begin()
    ring_b.relay()
    total = moved[c]
    for k in range(1, n):
        shared[k - 1].wait_recv()
        total = total + landed[k - 1]
    gm[h] = total
    ring_m.begin()
    ring_b.end()

    def project(buf, rows, out):
        half = rows // 2
        for k in range(0, n, 2):
            a = jnp.concatenate([buf[k, :rows, :], buf[k + 1, :rows, :]], axis=1)
            wa = jnp.concatenate([w_ref[k * 192 : k * 192 + 128, :], w_ref[k * 192 + 192 : k * 192 + 320, :]], axis=0)
            part = jnp.dot(a, wa, preferred_element_type=jnp.float32)
            b = jnp.concatenate([buf[k, rows : rows + half, :], buf[k + 1, rows : rows + half, :]], axis=1)
            top = jnp.dot(b, wb1[k * 128 : k * 128 + 256, :], preferred_element_type=jnp.float32)
            bot = jnp.dot(b, wb2[k * 128 : k * 128 + 256, :], preferred_element_type=jnp.float32)
            part = part + jnp.concatenate([top, bot], axis=0)
            if k == 0:
                out[...] = part
            else:
                out[...] += part

    project(gb, tokens, proj)
    kv[c, :tokens] = proj[:, HD : 2 * HD].astype(jnp.bfloat16)
    kv[c, tokens:] = pack(proj[:, 2 * HD :].astype(jnp.bfloat16))
    ring_k.begin()
    q_out[...] = (proj[:, :HD] * QSCALE).astype(jnp.bfloat16)
    ring_m.relay()
    ring_p.relay()
    ring_m.end()
    project(gm, share, projm)
    mod[c, :share] = (projm[:, :HD] * QSCALE).astype(jnp.bfloat16)
    mod[c, share : 2 * share] = projm[:, HD : 2 * HD].astype(jnp.bfloat16)
    mod[c, 2 * share :] = pack(projm[:, 2 * HD :].astype(jnp.bfloat16))
    ring_o.begin()
    ring_p.end()
    mix = jnp.zeros((wo_ref.shape[0], 2 * C), jnp.float32)
    for k in range(0, n, 2):
        wide = jnp.concatenate([wp[k], wp[k + 1]], axis=0)
        mix = mix + jnp.dot(wo_ref[:, k * 192 : k * 192 + 384], wide, preferred_element_type=jnp.float32)
    mix_out[...] = mix.astype(jnp.bfloat16)
    ring_k.cross()
    ring_k.relay()
    ring_o.cross()
    ring_o.relay()
    ring_k.relay_mate()
    ring_o.relay_mate()
    ring_k.end()
    ring_o.end()
    for ring in (ring_b, ring_m, ring_p, ring_k, ring_o):
        ring.drain()
    for made in shared:
        made.wait_send()
    kv_out[...] = kv[...]
    mod_out[...] = mod[...]


def project_rows(sequence, deletions, conv_taps, conv_bias, w_proj, w_out, w_pair):
    tokens, width = sequence.shape
    variants = deletions.shape[0]
    n = 8
    share = SEGS * DEL // 2
    vm = pl.BlockSpec(memory_space=pltpu.VMEM)
    bf = jnp.bfloat16
    kv_rows, mod_rows = tokens * 5 // 2, share * 7 // 2
    return pl.pallas_call(
        rows_kernel,
        out_shape=(
            jax.ShapeDtypeStruct((tokens, HD), bf),
            jax.ShapeDtypeStruct((n, kv_rows, 128), bf),
            jax.ShapeDtypeStruct((n, mod_rows, 128), bf),
            jax.ShapeDtypeStruct((variants, tokens // POOL, width), bf),
            jax.ShapeDtypeStruct((w_out.shape[0], 2 * C), bf),
        ),
        in_specs=[pl.BlockSpec(memory_space=pltpu.SMEM)] + [vm] * 6,
        out_specs=(vm,) * 5,
        scratch_shapes=[
            pltpu.VMEM((DIL, width), bf),
            pltpu.VMEM((DIL, width), bf),
            pltpu.VMEM((n, tokens * 3 // 2, 128), bf),
            pltpu.VMEM((n, share * 3 // 2, 128), bf),
            pltpu.VMEM((n, width, 2 * C), bf),
            pltpu.VMEM((n, share * 3 // 2, 128), bf),
            pltpu.VMEM((n - 1, share * 3 // 2, 128), bf),
            pltpu.VMEM((n, kv_rows, 128), bf),
            pltpu.VMEM((n, mod_rows, 128), bf),
            pltpu.VMEM((n * 128, w_proj.shape[1]), bf),
            pltpu.VMEM((n * 128, w_proj.shape[1]), bf),
            pltpu.VMEM((tokens, w_proj.shape[1]), jnp.float32),
            pltpu.VMEM((share, w_proj.shape[1]), jnp.float32),
            pltpu.SemaphoreType.DMA((60,)),
            pltpu.SemaphoreType.DMA((60,)),
        ],
        compiler_params=pltpu.CompilerParams(
            collective_id=0, has_side_effects=True, vmem_limit_bytes=56 * 2**20
        ),
    )(deletions, sequence, conv_taps, conv_bias.reshape(1, width), w_proj, w_out, w_pair)


def sum_kernel(part, row_out, col_out, mine, landed, rows_buf, cols_buf, feats, send, recv):
    c, h = lax.axis_index("ctx"), lax.axis_index("head")
    n = 8
    count = part.shape[0] // n
    on_diag = (c == h).astype(jnp.int32)
    barrier = pltpu.get_barrier_semaphore()
    for k in range(1, n):
        pl.semaphore_signal(barrier, inc=1, device_id={"head": lax.rem(h + k, n)}, device_id_type=MESH)
    for k in range(n):
        source = lax.rem(h + k, n)

        @pl.when(jnp.logical_or(c != h, k != 0))
        def _():
            pl.semaphore_signal(barrier, inc=1, device_id={"ctx": h, "head": source}, device_id_type=MESH)

    pl.semaphore_wait(barrier, (n - 1) + n - on_diag)

    def make(src, dst, index, target, arrival=None):
        return pltpu.make_async_remote_copy(
            src_ref=src, dst_ref=dst, send_sem=send.at[index],
            recv_sem=recv.at[index if arrival is None else arrival],
            device_id=target, device_id_type=MESH,
        )

    mine[...] = part[...].astype(jnp.bfloat16)
    first = []
    for k in range(1, n):
        to = lax.rem(h + k, n)
        made = make(mine.at[pl.ds(pl.multiple_of(to * count, count), count)], landed.at[k - 1], k, {"head": to})
        made.start()
        first.append(made)
    total = part[pl.ds(pl.multiple_of(h * count, count), count), :]
    for k in range(1, n):
        first[k - 1].wait_recv()
        total = total + landed[k - 1].astype(jnp.float32)
    feats[0] = total[:, :C].astype(jnp.bfloat16)
    feats[1] = total[:, C:].astype(jnp.bfloat16)
    rows_buf[h] = feats[0]
    for k in range(1, n):
        to = lax.rem(h + k, n)
        make(feats.at[0], rows_buf.at[h], n + k, {"head": to}).start()
    for k in range(n):
        to = lax.rem(c + k, n)

        @pl.when(jnp.logical_or(c != h, k != 0))
        def _():
            make(feats.at[1], cols_buf.at[h], 2 * n + k, {"ctx": to, "head": c}, 2 * n + h).start()

        @pl.when(jnp.logical_and(c == h, k == 0))
        def _():
            cols_buf[h] = feats[1]

    for k in range(1, n):
        source = lax.rem(h + n - k, n)
        made = make(feats.at[0], rows_buf.at[source], n + k, {"head": lax.rem(h + k, n)})
        made.wait_recv()
        made.wait_send()
    for k in range(n):
        @pl.when(jnp.logical_or(c != h, k != h))
        def _():
            make(feats.at[1], cols_buf.at[k], 2 * n + k, {"head": lax.rem(h + 1, n)}).wait_recv()

        @pl.when(jnp.logical_or(c != h, k != 0))
        def _():
            make(feats.at[1], cols_buf.at[h], 2 * n + k, {"head": lax.rem(h + 1, n)}).wait_send()
    for made in first:
        made.wait_send()
    for k in range(n):
        row_out[k * count : (k + 1) * count] = rows_buf[k].astype(jnp.float32)
        col_out[k * count : (k + 1) * count] = cols_buf[k].astype(jnp.float32)


def sum_heads(part):
    rows = part.shape[0]
    n = 8
    count = rows // n
    vm = pl.BlockSpec(memory_space=pltpu.VMEM)
    return pl.pallas_call(
        sum_kernel,
        out_shape=(jax.ShapeDtypeStruct((rows, C), jnp.float32),) * 2,
        in_specs=[vm],
        out_specs=(vm, vm),
        scratch_shapes=[
            pltpu.VMEM((rows, 2 * C), jnp.bfloat16),
            pltpu.VMEM((n - 1, count, 2 * C), jnp.bfloat16),
            pltpu.VMEM((n, count, C), jnp.bfloat16),
            pltpu.VMEM((n, count, C), jnp.bfloat16),
            pltpu.VMEM((2, count, C), jnp.bfloat16),
            pltpu.SemaphoreType.DMA((3 * n,)),
            pltpu.SemaphoreType.DMA((3 * n,)),
        ],
        compiler_params=pltpu.CompilerParams(collective_id=1, has_side_effects=True),
    )(part)


def local(sequence, deletions, conv_taps, conv_bias, w_proj, w_out, w_pair, dist_table):
    queries, kv, mod, pooled, mix = project_rows(
        sequence, deletions, conv_taps, conv_bias, w_proj, w_out, w_pair
    )
    part = attention(deletions, queries, kv, mod, mix, pooled, w_pair)
    variants, rows, _ = part.shape
    row_feats, col_feats = sum_heads(part.reshape(variants * rows, 2 * C))
    return pair_map(row_feats.reshape(variants, rows, C), col_feats.reshape(variants, rows, C), dist_table)


def solution(mesh):
    in_specs = (
        P("ctx", "head"),
        P("var", None),
        P(None, "head"),
        P("head"),
        P(None, "head"),
        P("head", None),
        P("head", None),
        P(),
    )
    out_specs = P("var", "ctx", "head", None)
    return jax.shard_map(local, mesh=mesh, in_specs=in_specs, out_specs=out_specs, check_vma=False)
```

```python
import functools
import math

import jax
import jax.numpy as jnp
from jax import lax
from jax.experimental import pallas as pl
from jax.experimental.pallas import tpu as pltpu
from jax.sharding import PartitionSpec as P

HD = 128
VD = 192
C = 128
NB = 16
POOL = 4
DIL = 256
DEL = 128
SEGS = 3
BIG = -1e30
QSCALE = math.log2(math.e) / math.sqrt(HD)


def changed(delta, length):
    hit = jnp.logical_and(delta >= 0, delta < length)
    for shift in (-DIL, DIL):
        moved = delta + shift
        hit = jnp.logical_or(hit, jnp.logical_and(moved >= 0, moved < length))
    return hit


def pair_kernel(rows_per, row_ref, col_ref, table_ref, out_ref, rel, rows, cols):
    step = pl.program_id(0)
    span = col_ref.shape[1]
    row_count = row_ref.shape[1]

    @pl.when(step == 0)
    def _():
        base = lax.axis_index("head") * span - lax.axis_index("ctx") * row_count - (row_count - 1)
        dist = jnp.abs(lax.broadcasted_iota(jnp.int32, rel.shape, 0) + base)
        value = jnp.broadcast_to(table_ref[0:1, :], rel.shape)
        for k in range(NB - 1):
            value = jnp.where(dist >= 2**k, table_ref[k + 1 : k + 2, :], value)
        rel[...] = value
        rows[...] = row_ref[...].astype(jnp.float32)
        cols[...] = col_ref[...].astype(jnp.float32)

    def one(i, _):
        row = step * rows_per + i
        shifted = rel[pl.ds(row_count - 1 - row, span), :]
        for v in range(row_ref.shape[0]):
            out_ref[v, i] = (rows[v, pl.ds(row, 1), :] + (cols[v] + shifted)).astype(out_ref.dtype)
        return 0

    lax.fori_loop(0, rows_per, one, 0)


def pair_map(row_feats, col_feats, table):
    variants, rows, _ = row_feats.shape
    cols = col_feats.shape[1]
    per = 8
    vm = pl.BlockSpec(memory_space=pltpu.VMEM)
    return pl.pallas_call(
        functools.partial(pair_kernel, per),
        grid=(rows // per,),
        out_shape=jax.ShapeDtypeStruct((variants, rows, cols, C), jnp.bfloat16),
        in_specs=[vm, vm, vm],
        out_specs=pl.BlockSpec((variants, per, cols, C), lambda i: (0, i, 0, 0)),
        scratch_shapes=[
            pltpu.VMEM((rows + cols, C), jnp.float32),
            pltpu.VMEM((variants, rows, C), jnp.float32),
            pltpu.VMEM((variants, cols, C), jnp.float32),
        ],
        compiler_params=pltpu.CompilerParams(vmem_limit_bytes=32 * 2**20),
    )(row_feats, col_feats, table)


MESH = pl.DeviceIdType.MESH


def pack(x):
    half = x.shape[0] // 2
    tail = jnp.concatenate([x[:half, 128:], x[half:, 128:]], axis=1)
    return jnp.concatenate([x[:, :128], tail], axis=0)


class Ring:
    def __init__(self, make, buf, rows, base, me, dn, up, far, mate, mate_of, to_dn, to_up, to_mate):
        half = rows // 2
        self.full, self.lo, self.hi = pl.ds(0, rows), pl.ds(0, half), pl.ds(half, half)
        self.make, self.buf, self.base = make, buf, base
        self.me, self.dn, self.up, self.far, self.mate, self.mate_of = me, dn, up, far, mate, mate_of
        self.to_dn, self.to_up, self.to_mate = to_dn, to_up, to_mate
        self.sent = []

    def copy(self, slot, rows, index, target):
        ref = self.buf.at[slot, rows]
        return self.make(ref, ref, self.base + index, target)

    def send(self, slot, rows, index, target):
        made = self.copy(slot, rows, index, target)
        made.start()
        self.sent.append(made)

    def got(self, slot, rows, index):
        self.copy(slot, rows, index, self.to_up).wait_recv()


class HeadRing(Ring):
    def begin(self):
        self.send(self.me, self.full, 0, self.to_up)
        self.send(self.me, self.full, 1, self.to_dn)
        self.send(self.me, self.full, 2, self.to_mate)

    def relay(self):
        self.got(self.dn, self.full, 0)
        self.send(self.dn, self.lo, 3, self.to_up)
        self.send(self.dn, self.full, 4, self.to_mate)
        self.got(self.up, self.full, 1)
        self.send(self.up, self.hi, 5, self.to_dn)
        self.send(self.up, self.full, 6, self.to_mate)

    def end(self):
        self.got(self.far, self.lo, 3)
        self.send(self.far, self.lo, 7, self.to_mate)
        self.got(self.far, self.hi, 5)
        self.send(self.far, self.hi, 8, self.to_mate)
        self.got(self.mate, self.full, 2)
        self.got(self.mate_of(self.dn), self.full, 4)
        self.got(self.mate_of(self.up), self.full, 6)
        self.got(self.mate_of(self.far), self.lo, 7)
        self.got(self.mate_of(self.far), self.hi, 8)

    def drain(self):
        for made in self.sent:
            made.wait_send()


class TokenRing(Ring):
    def begin(self):
        self.send(self.me, self.full, 2, self.to_mate)
        self.send(self.me, self.full, 0, self.to_up)
        self.send(self.me, self.full, 1, self.to_dn)

    def cross(self):
        self.got(self.mate, self.full, 2)
        self.send(self.mate, self.full, 4, self.to_up)
        self.send(self.mate, self.full, 6, self.to_dn)

    def relay(self):
        self.got(self.dn, self.full, 0)
        self.send(self.dn, self.lo, 3, self.to_up)
        self.got(self.up, self.full, 1)
        self.send(self.up, self.hi, 5, self.to_dn)

    def relay_mate(self):
        dn, up = self.mate_of(self.dn), self.mate_of(self.up)
        self.got(dn, self.full, 4)
        self.send(dn, self.lo, 7, self.to_up)
        self.got(up, self.full, 6)
        self.send(up, self.hi, 8, self.to_dn)

    def end(self):
        self.got(self.far, self.lo, 3)
        self.got(self.far, self.hi, 5)
        self.got(self.mate_of(self.far), self.lo, 7)
        self.got(self.mate_of(self.far), self.hi, 8)

    def drain(self):
        for made in self.sent:
            made.wait_send()


def swap_lanes(x):
    return jnp.concatenate([x[:, 64:], x[:, :64]], axis=1)


def unpack_tail(tail, fill):
    both = jnp.concatenate([tail, swap_lanes(tail)], axis=0)
    keep = lax.broadcasted_iota(jnp.int32, both.shape, 1) < 64
    return jnp.where(keep, both, jnp.broadcast_to(fill, both.shape))


def features_kernel(dels, seq, taps, bias, w_ref, wo_ref, wp_ref, row_out, col_out,
                    low, high, cols, gb0, gb1, gm, wp, moved, landed, flat, kv0, kv1, mq, mkv,
                    queries, q_aug, top, acc, ka, va, pooled, mix, mine, arrived, rows_buf, cols_buf, feats,
                    send, recv):
    width, tokens = seq.shape
    variants = dels.shape[0]
    share = SEGS * DEL // 2
    per = 2 * share
    n = 8
    bf = jnp.bfloat16
    c, h, g = lax.axis_index("ctx"), lax.axis_index("head"), lax.axis_index("var")
    dn_h, up_h, far_h = lax.rem(h + 6, n), lax.rem(h + 2, n), lax.rem(h + 4, n)
    sib = h + 1 - 2 * lax.rem(h, 2)
    x0, y0 = c // 4 * 4, lax.rem(c, 4)
    up_c, dn_c, far_c = x0 + lax.rem(y0 + 1, 4), x0 + lax.rem(y0 + 3, 4), x0 + lax.rem(y0 + 2, 4)
    other = lambda t: lax.rem(t + 4, n)
    xp = other(c)
    sib_of = lambda t: t + 1 - 2 * lax.rem(t, 2)

    barrier = pltpu.get_barrier_semaphore()
    peers = [{"ctx": lax.rem(c + k, n)} for k in range(1, n)]
    peers += [{"head": lax.rem(h + k, n)} for k in range(1, n)]
    peers += [{"ctx": xp, "var": 1 - g}]
    for peer in peers:
        pl.semaphore_signal(barrier, inc=1, device_id=peer, device_id_type=MESH)
    for k in range(n):
        source = lax.rem(h + k, n)

        @pl.when(jnp.logical_or(c != h, k != 0))
        def _():
            pl.semaphore_signal(barrier, inc=1, device_id={"ctx": h, "head": source}, device_id_type=MESH)

    for k in range(4):
        line = bias[...] if k == 3 else taps[k : k + 1, :]
        cols[k] = jnp.broadcast_to(line, (128, width)).T
    wp[h] = wp_ref[...]
    pl.semaphore_wait(barrier, len(peers) + n - (c == h).astype(jnp.int32))

    def make(src, dst, index, target, arrival=None):
        return pltpu.make_async_remote_copy(
            src_ref=src, dst_ref=dst, send_sem=send.at[index],
            recv_sem=recv.at[index if arrival is None else arrival],
            device_id=target, device_id_type=MESH,
        )

    halo_low = make(seq.at[:, pl.ds(tokens - DIL, DIL)], low, 0, {"ctx": lax.rem(c + 1, n)})
    halo_high = make(seq.at[:, pl.ds(0, DIL)], high, 1, {"ctx": lax.rem(c + 7, n)})
    halo_low.start()
    halo_high.start()

    def head_ring(buf, base):
        return HeadRing(make, buf, buf.shape[1], base, h, dn_h, up_h, far_h, sib, sib_of,
                        {"head": dn_h}, {"head": up_h}, {"head": sib})

    def token_ring(buf, base, to_mate):
        return TokenRing(make, buf, buf.shape[1], base, c, dn_c, up_c, far_c, xp, other,
                         {"ctx": dn_c}, {"ctx": up_c}, to_mate)

    ring_b0, ring_b1, ring_m, ring_p = (head_ring(buf, 10 + 9 * i) for i, buf in enumerate((gb0, gb1, gm, wp)))
    cross = {"ctx": xp, "var": 1 - g}
    ring_k0, ring_k1 = token_ring(kv0, 46, cross), token_ring(kv1, 55, cross)
    ring_q, ring_o = token_ring(mq, 64, {"ctx": xp}), token_ring(mkv, 73, {"ctx": xp})

    at = lax.broadcasted_iota(jnp.int32, (1, DIL), 1) + c * tokens
    wide = lambda k: jnp.concatenate([cols[k], cols[k]], axis=1)

    def trunk(half, first, length):
        def kept(x, shift, inside=None):
            d = at + (half * DIL + shift) - first
            keep = jnp.logical_or(d < 0, d >= length)
            if inside is not None:
                keep = jnp.logical_and(keep, inside)
            return jnp.where(keep, x.astype(jnp.float32), 0.0)

        here = kept(seq[:, half * DIL : (half + 1) * DIL], 0)
        if half == 0:
            before, after = kept(low[...], -DIL, c != 0), kept(seq[:, DIL:], DIL)
        else:
            before, after = kept(seq[:, :DIL], -DIL), kept(high[...], DIL, c != n - 1)
        conv = wide(0) * before + wide(1) * here + wide(2) * after + wide(3)
        return (here + jax.nn.gelu(conv, approximate=True)).astype(bf)

    halo_low.wait()
    gb0[h] = trunk(0, 0, 0)
    ring_b0.begin()
    halo_high.wait()
    gb1[h] = trunk(1, 0, 0)
    ring_b1.begin()

    r = lax.broadcasted_iota(jnp.int32, (tokens, share), 1)
    offset = (r // (DEL // 2) - 1) * DIL + r % (DEL // 2)
    here = lax.broadcasted_iota(jnp.int32, (tokens, share), 0) + c * tokens - offset
    pool = (
        lax.broadcasted_iota(jnp.int32, (tokens // POOL, tokens), 1) // POOL
        == lax.broadcasted_iota(jnp.int32, (tokens // POOL, tokens), 0)
    ).astype(bf)

    def variant(v, _):
        first = dels[v, 0]
        length = dels[v, 1] - first
        own = jnp.concatenate([trunk(0, first, length), trunk(1, first, length)], axis=1)
        for half in range(2):
            pick = (here == first + half * (DEL // 2)).astype(bf)
            moved[2 * v + half] = pack(jnp.dot(own, pick, preferred_element_type=jnp.float32).astype(bf))
        mean = lax.dot_general(pool, own, (((1,), (1,)), ((), ())), preferred_element_type=jnp.float32)
        pooled[v] = (mean * (1.0 / POOL)).astype(bf)
        return 0

    lax.fori_loop(0, variants, variant, 0)
    shared = []
    for k in range(1, n):
        to = lax.rem(c + k, n)
        made = make(moved.at[to], landed.at[k - 1], 1 + k, {"ctx": to})
        made.start()
        shared.append(made)
    ring_b0.relay()
    total = moved[c]
    for k in range(1, n):
        shared[k - 1].wait_recv()
        total = total + landed[k - 1]
    gm[h] = total
    ring_m.begin()
    ring_b0.end()

    def project(x):
        return jnp.dot(w_ref[...], x, preferred_element_type=jnp.float32).T

    def place(kv, x, count):
        kv[c, :count] = x[:count, HD : 2 * HD].astype(bf)
        kv[c, count:] = pack(x[:count, 2 * HD :].astype(bf))

    x = project(gb0[...].reshape(n * width, DIL))
    place(kv0, x, DIL)
    ring_k0.begin()
    queries[:DIL] = (x[:, :HD] * QSCALE).astype(bf)
    ring_m.relay()
    ring_b1.relay()
    ring_p.begin()
    ring_m.end()
    zero = jnp.zeros((1, 128), bf)
    for k in range(n):
        flat[k * width : (k + 1) * width, :128] = gm[k, :width]
        flat[k * width : (k + 1) * width, 128:] = unpack_tail(gm[k, width:], zero)
    x = project(flat[...])
    mq[c] = (x[:share, :HD] * QSCALE).astype(bf)
    ring_q.begin()
    place(mkv, x, share)
    ring_b1.end()
    x = project(gb1[...].reshape(n * width, DIL))
    place(kv1, x, DIL)
    ring_k1.begin()
    ring_o.begin()
    queries[DIL:] = (x[:, :HD] * QSCALE).astype(bf)
    ring_k0.cross()
    ring_k0.relay()
    ring_q.cross()
    ring_q.relay()
    ring_p.relay()
    ring_p.end()
    total = jnp.zeros((wo_ref.shape[0], 2 * C), jnp.float32)
    for k in range(0, n, 2):
        two = jnp.concatenate([wp[k], wp[k + 1]], axis=0)
        total = total + jnp.dot(wo_ref[:, k * width : (k + 2) * width], two, preferred_element_type=jnp.float32)
    mix[...] = total.astype(bf)
    ring_q.relay_mate()
    ring_q.end()

    lane = lax.broadcasted_iota(jnp.int32, (1, 128), 1)
    first = jnp.zeros((1, 128), jnp.int32)
    length = jnp.zeros((1, 128), jnp.int32)
    for v in range(variants):
        first = jnp.where(lane == v, dels[v, 0], first)
        length = jnp.where(lane == v, dels[v, 1] - dels[v, 0], length)
    col = lax.broadcasted_iota(jnp.int32, (tokens, per), 1)
    col_step = col // share * (DEL // 2) + col % (DEL // 2)
    col_offset = (col % share // (DEL // 2) - 1) * DIL + col_step
    qpos = lax.broadcasted_iota(jnp.int32, (tokens, per), 0) + c * tokens

    def aim(v, _):
        s0 = dels[v, 0]
        count = dels[v, 1] - s0
        spot = jnp.logical_and(qpos - col_offset == s0, col_step < count).astype(bf)
        source = jnp.concatenate([mq[2 * v], mq[2 * v + 1]], axis=0)
        moved_q = jnp.dot(spot, source, preferred_element_type=jnp.float32)
        is_mod = changed(qpos[:, :128] - s0, count)
        q_aug[v, :, :HD] = jnp.where(is_mod, moved_q, queries[...].astype(jnp.float32)).astype(bf)
        q_aug[v, :, HD:] = jnp.broadcast_to(jnp.where(lane == v, 1.0, 0.0), (tokens, 128)).astype(bf)
        top[v] = jnp.full((tokens, 1), -3e38, jnp.float32)
        acc[v] = jnp.zeros((tokens, 256), jnp.float32)
        return 0

    lax.fori_loop(0, variants, aim, 0)
    ones = jnp.where(lane == VD - 128, 1.0, 0.0).astype(bf)

    def unit(v, keys, values):
        s = lax.dot_general(q_aug[v], keys, (((1,), (1,)), ((), ())), preferred_element_type=jnp.float32)
        old = top[v]
        new = jnp.maximum(old, s.max(1, keepdims=True))
        w = jnp.exp2(s - new).astype(bf)
        top[v] = new
        acc[v] = acc[v] * jnp.exp2(old - new) + jnp.dot(w, values, preferred_element_type=jnp.float32)

    def attend(block):
        for i, kv in enumerate((kv0, kv1)):
            rows = slice(i * DIL, (i + 1) * DIL)
            ka[rows, :HD] = kv[block, :DIL]
            pos = lax.broadcasted_iota(jnp.int32, (DIL, 128), 0) + (block * tokens + i * DIL)
            ka[rows, HD:] = jnp.where(changed(pos - first, length), BIG, 0.0).astype(bf)
            va[rows, :128] = kv[block, DIL : 2 * DIL]
            va[rows, 128:] = unpack_tail(kv[block, 2 * DIL :], ones)

        def one(v, _):
            unit(v, ka[...], va[...])
            return 0

        lax.fori_loop(0, variants, one, 0)

    ring_k1.cross()
    ring_k1.relay()
    attend(c)
    ring_k0.relay_mate()
    ring_o.cross()
    ring_o.relay()
    attend(dn_c)
    ring_k1.relay_mate()
    attend(up_c)
    ring_o.relay_mate()
    attend(xp)
    ring_k0.end()
    ring_k1.end()
    attend(far_c)
    attend(other(dn_c))
    attend(other(up_c))
    attend(other(far_c))
    ring_o.end()

    row = lax.broadcasted_iota(jnp.int32, (per, 128), 0)
    step = row // share * (DEL // 2) + row % (DEL // 2)
    row_offset = (row % share // (DEL // 2) - 1) * DIL + step
    count = tokens // POOL // 2
    first_sent = []
    for v in range(variants):
        token = dels[v, 0] + row_offset
        valid = (step < dels[v, 1] - dels[v, 0]) & (token >= 0) & (token < n * tokens)
        ka[:per, HD:] = jnp.where(valid, 0.0, BIG).astype(bf)
        for i in range(2):
            rows = slice(i * share, (i + 1) * share)
            ka[rows, :HD] = mkv[2 * v + i, :share]
            va[rows, :128] = mkv[2 * v + i, share : 2 * share]
            va[rows, 128:] = unpack_tail(mkv[2 * v + i, 2 * share :], ones)
        unit(v, ka[:per], va[:per])
        out = (acc[v, :, :VD] / acc[v, :, VD : VD + 1]).astype(bf)
        mean = jnp.dot(pool, out, preferred_element_type=jnp.float32) * (1.0 / POOL)
        part = jnp.dot(mean.astype(bf), mix[...], preferred_element_type=jnp.float32) + jnp.dot(
            pooled[v], wp_ref[...], preferred_element_type=jnp.float32
        )
        for i in range(2):
            to = 2 * v + i
            mine[to] = part[i * count : (i + 1) * count].astype(bf)
            made = make(mine.at[to], arrived.at[h], 82 + to, {"head": to}, 82 + h)
            first_sent.append(made)

            @pl.when(h != to)
            def _():
                made.start()

            @pl.when(h == to)
            def _():
                arrived[h] = mine[to]

    for k in range(n):
        @pl.when(h != k)
        def _():
            make(mine.at[k], arrived.at[k], 82 + k, {"head": k}).wait_recv()

    total = arrived[0].astype(jnp.float32)
    for k in range(1, n):
        total = total + arrived[k].astype(jnp.float32)
    feats[0] = total[:, :C].astype(bf)
    feats[1] = total[:, C:].astype(bf)
    rows_buf[h] = feats[0]
    for k in range(n):
        to = lax.rem(c + k, n)

        @pl.when(jnp.logical_or(c != h, k != 0))
        def _():
            make(feats.at[1], cols_buf.at[h], 98 + k, {"ctx": to, "head": c}, 98 + h).start()

        @pl.when(jnp.logical_and(c == h, k == 0))
        def _():
            cols_buf[h] = feats[1]

    for k in range(1, n):
        make(feats.at[0], rows_buf.at[h], 90 + k, {"head": lax.rem(h + k, n)}).start()
    for ring in (ring_b0, ring_b1, ring_m, ring_p, ring_k0, ring_k1, ring_q, ring_o):
        ring.drain()
    for made in shared:
        made.wait_send()
    for k, made in enumerate(first_sent):
        @pl.when(h != k)
        def _():
            made.wait_send()

    for k in range(1, n):
        source = lax.rem(h + n - k, n)
        made = make(feats.at[0], rows_buf.at[source], 90 + k, {"head": lax.rem(h + k, n)})
        made.wait_recv()
        made.wait_send()
    for k in range(n):
        @pl.when(jnp.logical_or(c != h, k != h))
        def _():
            make(feats.at[1], cols_buf.at[k], 98 + k, {"head": lax.rem(h + 1, n)}).wait_recv()

        @pl.when(jnp.logical_or(c != h, k != 0))
        def _():
            make(feats.at[1], cols_buf.at[h], 98 + k, {"head": lax.rem(h + 1, n)}).wait_send()
    row_out[...] = rows_buf[...]
    col_out[...] = cols_buf[...]


def features(sequence, deletions, conv_taps, conv_bias, w_proj, w_out, w_pair):
    tokens, width = sequence.shape
    variants = deletions.shape[0]
    n = 8
    share = SEGS * DEL // 2
    vm = pl.BlockSpec(memory_space=pltpu.VMEM)
    bf, f32 = jnp.bfloat16, jnp.float32
    part = variants * tokens // POOL // n
    scratch = [
        ((width, DIL), bf),
        ((width, DIL), bf),
        ((4, width, 128), f32),
        ((n, width, DIL), bf),
        ((n, width, DIL), bf),
        ((n, share * 3 // 2, 128), bf),
        ((n, width, 2 * C), bf),
        ((n, share * 3 // 2, 128), bf),
        ((n - 1, share * 3 // 2, 128), bf),
        ((n * width, 256), bf),
        ((n, DIL * 5 // 2, 128), bf),
        ((n, DIL * 5 // 2, 128), bf),
        ((n, share, 128), bf),
        ((n, share * 5 // 2, 128), bf),
        ((tokens, HD), bf),
        ((variants, tokens, 256), bf),
        ((variants, tokens, 1), f32),
        ((variants, tokens, 256), f32),
        ((tokens, 256), bf),
        ((tokens, 256), bf),
        ((variants, tokens // POOL, width), bf),
        ((w_out.shape[0], 2 * C), bf),
        ((n, part, 2 * C), bf),
        ((n, part, 2 * C), bf),
        ((n, part, C), bf),
        ((n, part, C), bf),
        ((2, part, C), bf),
    ]
    return pl.pallas_call(
        features_kernel,
        out_shape=(jax.ShapeDtypeStruct((n, part, C), bf),) * 2,
        in_specs=[pl.BlockSpec(memory_space=pltpu.SMEM)] + [vm] * 6,
        out_specs=(vm, vm),
        scratch_shapes=[pltpu.VMEM(shape, kind) for shape, kind in scratch]
        + [pltpu.SemaphoreType.DMA((106,)), pltpu.SemaphoreType.DMA((106,))],
        compiler_params=pltpu.CompilerParams(
            collective_id=0, has_side_effects=True, vmem_limit_bytes=56 * 2**20
        ),
    )(deletions, sequence.T, conv_taps, conv_bias.reshape(1, width), w_proj.T, w_out, w_pair)


def local(sequence, deletions, conv_taps, conv_bias, w_proj, w_out, w_pair, dist_table):
    variants = deletions.shape[0]
    row_feats, col_feats = features(sequence, deletions, conv_taps, conv_bias, w_proj, w_out, w_pair)
    shape = (variants, sequence.shape[0] // POOL, C)
    return pair_map(row_feats.reshape(shape), col_feats.reshape(shape), dist_table)


def solution(mesh):
    in_specs = (
        P("ctx", "head"),
        P("var", None),
        P(None, "head"),
        P("head"),
        P(None, "head"),
        P("head", None),
        P("head", None),
        P(),
    )
    out_specs = P("var", "ctx", "head", None)
    return jax.shard_map(local, mesh=mesh, in_specs=in_specs, out_specs=out_specs, check_vma=False)
```

```python
import functools
import math

import jax
import jax.numpy as jnp
from jax import lax
from jax.experimental import pallas as pl
from jax.experimental.pallas import tpu as pltpu
from jax.sharding import PartitionSpec as P

HD = 128
VD = 192
C = 128
NB = 16
POOL = 4
DIL = 256
DEL = 128
SEGS = 3
BIG = -1e30
QSCALE = math.log2(math.e) / math.sqrt(HD)


def changed(delta, length):
    hit = jnp.logical_and(delta >= 0, delta < length)
    for shift in (-DIL, DIL):
        moved = delta + shift
        hit = jnp.logical_or(hit, jnp.logical_and(moved >= 0, moved < length))
    return hit


def pair_kernel(rows_per, row_ref, col_ref, table_ref, out_ref, rel, rows, cols):
    step = pl.program_id(0)
    span = col_ref.shape[1]
    row_count = row_ref.shape[1]

    @pl.when(step == 0)
    def _():
        base = lax.axis_index("head") * span - lax.axis_index("ctx") * row_count - (row_count - 1)
        dist = jnp.abs(lax.broadcasted_iota(jnp.int32, rel.shape, 0) + base)
        value = jnp.broadcast_to(table_ref[0:1, :], rel.shape)
        for k in range(NB - 1):
            value = jnp.where(dist >= 2**k, table_ref[k + 1 : k + 2, :], value)
        rel[...] = value
        rows[...] = row_ref[...].astype(jnp.float32)
        cols[...] = col_ref[...].astype(jnp.float32)

    def one(i, _):
        row = step * rows_per + i
        shifted = rel[pl.ds(row_count - 1 - row, span), :]
        for v in range(row_ref.shape[0]):
            out_ref[v, i] = (rows[v, pl.ds(row, 1), :] + (cols[v] + shifted)).astype(out_ref.dtype)
        return 0

    lax.fori_loop(0, rows_per, one, 0)


def pair_map(row_feats, col_feats, table):
    variants, rows, _ = row_feats.shape
    cols = col_feats.shape[1]
    per = 8
    vm = pl.BlockSpec(memory_space=pltpu.VMEM)
    return pl.pallas_call(
        functools.partial(pair_kernel, per),
        grid=(rows // per,),
        out_shape=jax.ShapeDtypeStruct((variants, rows, cols, C), jnp.bfloat16),
        in_specs=[vm, vm, vm],
        out_specs=pl.BlockSpec((variants, per, cols, C), lambda i: (0, i, 0, 0)),
        scratch_shapes=[
            pltpu.VMEM((rows + cols, C), jnp.float32),
            pltpu.VMEM((variants, rows, C), jnp.float32),
            pltpu.VMEM((variants, cols, C), jnp.float32),
        ],
        compiler_params=pltpu.CompilerParams(vmem_limit_bytes=32 * 2**20),
    )(row_feats, col_feats, table)


MESH = pl.DeviceIdType.MESH


def pack(x):
    half = x.shape[0] // 2
    tail = jnp.concatenate([x[:half, 128:], x[half:, 128:]], axis=1)
    return jnp.concatenate([x[:, :128], tail], axis=0)


class Ring:
    def __init__(self, make, buf, rows, base, me, dn, up, far, mate, mate_of, to_dn, to_up, to_mate):
        half = rows // 2
        self.full, self.lo, self.hi = pl.ds(0, rows), pl.ds(0, half), pl.ds(half, half)
        self.make, self.buf, self.base = make, buf, base
        self.me, self.dn, self.up, self.far, self.mate, self.mate_of = me, dn, up, far, mate, mate_of
        self.to_dn, self.to_up, self.to_mate = to_dn, to_up, to_mate
        self.sent = []

    def copy(self, slot, rows, index, target):
        ref = self.buf.at[slot, rows]
        return self.make(ref, ref, self.base + index, target)

    def send(self, slot, rows, index, target):
        made = self.copy(slot, rows, index, target)
        made.start()
        self.sent.append(made)

    def got(self, slot, rows, index):
        self.copy(slot, rows, index, self.to_up).wait_recv()


class HeadRing(Ring):
    def begin(self):
        self.send(self.me, self.full, 0, self.to_up)
        self.send(self.me, self.full, 1, self.to_dn)
        self.send(self.me, self.full, 2, self.to_mate)

    def relay(self):
        self.got(self.dn, self.full, 0)
        self.send(self.dn, self.lo, 3, self.to_up)
        self.send(self.dn, self.full, 4, self.to_mate)
        self.got(self.up, self.full, 1)
        self.send(self.up, self.hi, 5, self.to_dn)
        self.send(self.up, self.full, 6, self.to_mate)

    def end(self):
        self.got(self.far, self.lo, 3)
        self.send(self.far, self.lo, 7, self.to_mate)
        self.got(self.far, self.hi, 5)
        self.send(self.far, self.hi, 8, self.to_mate)
        self.got(self.mate, self.full, 2)
        self.got(self.mate_of(self.dn), self.full, 4)
        self.got(self.mate_of(self.up), self.full, 6)
        self.got(self.mate_of(self.far), self.lo, 7)
        self.got(self.mate_of(self.far), self.hi, 8)

    def drain(self):
        for made in self.sent:
            made.wait_send()


class TokenRing(Ring):
    def begin(self):
        self.send(self.me, self.full, 2, self.to_mate)
        self.send(self.me, self.full, 0, self.to_up)
        self.send(self.me, self.full, 1, self.to_dn)

    def cross(self):
        self.got(self.mate, self.full, 2)
        self.send(self.mate, self.full, 4, self.to_up)
        self.send(self.mate, self.full, 6, self.to_dn)

    def relay(self):
        self.got(self.dn, self.full, 0)
        self.send(self.dn, self.lo, 3, self.to_up)
        self.got(self.up, self.full, 1)
        self.send(self.up, self.hi, 5, self.to_dn)

    def far_block(self):
        self.got(self.far, self.lo, 3)
        self.send(self.far, self.lo, 7, self.to_mate)
        self.got(self.far, self.hi, 5)
        self.send(self.far, self.hi, 8, self.to_mate)

    def end(self):
        self.got(self.mate_of(self.dn), self.full, 4)
        self.got(self.mate_of(self.up), self.full, 6)
        self.got(self.mate_of(self.far), self.lo, 7)
        self.got(self.mate_of(self.far), self.hi, 8)

    def drain(self):
        for made in self.sent:
            made.wait_send()


def swap_lanes(x):
    return jnp.concatenate([x[:, 64:], x[:, :64]], axis=1)


def unpack_tail(tail, fill):
    both = jnp.concatenate([tail, swap_lanes(tail)], axis=0)
    keep = lax.broadcasted_iota(jnp.int32, both.shape, 1) < 64
    return jnp.where(keep, both, jnp.broadcast_to(fill, both.shape))


def features_kernel(dels, seq, taps, bias, w_ref, wo_ref, wp_ref, row_out, col_out,
                    low, high, cols, gb0, gb1, gm, wp, moved, landed, flat, kv0, kv1, mq, mkv,
                    queries, q_aug, top, acc, ka, va, pooled, mix, mine, arrived, rows_buf, cols_buf, feats,
                    send, recv):
    width, tokens = seq.shape
    variants = dels.shape[0]
    share = SEGS * DEL // 2
    per = 2 * share
    n = 8
    bf = jnp.bfloat16
    c, h, g = lax.axis_index("ctx"), lax.axis_index("head"), lax.axis_index("var")
    dn_h, up_h, far_h = lax.rem(h + 6, n), lax.rem(h + 2, n), lax.rem(h + 4, n)
    sib = h + 1 - 2 * lax.rem(h, 2)
    x0, y0 = c // 4 * 4, lax.rem(c, 4)
    up_c, dn_c, far_c = x0 + lax.rem(y0 + 1, 4), x0 + lax.rem(y0 + 3, 4), x0 + lax.rem(y0 + 2, 4)
    other = lambda t: lax.rem(t + 4, n)
    xp = other(c)
    sib_of = lambda t: t + 1 - 2 * lax.rem(t, 2)

    barrier = pltpu.get_barrier_semaphore()
    peers = [{"ctx": lax.rem(c + k, n)} for k in range(1, n)]
    peers += [{"head": lax.rem(h + k, n)} for k in range(1, n)]
    peers += [{"ctx": xp, "var": 1 - g}]
    for peer in peers:
        pl.semaphore_signal(barrier, inc=1, device_id=peer, device_id_type=MESH)
    for k in range(n):
        source = lax.rem(h + k, n)

        @pl.when(jnp.logical_or(c != h, k != 0))
        def _():
            pl.semaphore_signal(barrier, inc=1, device_id={"ctx": h, "head": source}, device_id_type=MESH)

    for k in range(4):
        line = bias[...] if k == 3 else taps[k : k + 1, :]
        cols[k] = jnp.broadcast_to(line, (128, width)).T
    wp[h] = wp_ref[...]
    pl.semaphore_wait(barrier, len(peers) + n - (c == h).astype(jnp.int32))

    def make(src, dst, index, target, arrival=None):
        return pltpu.make_async_remote_copy(
            src_ref=src, dst_ref=dst, send_sem=send.at[index],
            recv_sem=recv.at[index if arrival is None else arrival],
            device_id=(target.get("ctx", c), target.get("head", h), target.get("var", g)), device_id_type=MESH,
        )

    halo_low = make(seq.at[:, pl.ds(tokens - DIL, DIL)], low, 0, {"ctx": lax.rem(c + 1, n)})
    halo_high = make(seq.at[:, pl.ds(0, DIL)], high, 1, {"ctx": lax.rem(c + 7, n)})
    halo_low.start()
    halo_high.start()

    def head_ring(buf, base):
        return HeadRing(make, buf, buf.shape[1], base, h, dn_h, up_h, far_h, sib, sib_of,
                        {"head": dn_h}, {"head": up_h}, {"head": sib})

    def token_ring(buf, base, to_mate):
        return TokenRing(make, buf, buf.shape[1], base, c, dn_c, up_c, far_c, xp, other,
                         {"ctx": dn_c}, {"ctx": up_c}, to_mate)

    ring_b0, ring_b1, ring_m, ring_p = (head_ring(buf, 10 + 9 * i) for i, buf in enumerate((gb0, gb1, gm, wp)))
    cross = {"ctx": xp, "var": 1 - g}
    ring_k0, ring_k1 = token_ring(kv0, 46, cross), token_ring(kv1, 55, cross)
    ring_q, ring_o = token_ring(mq, 64, {"ctx": xp}), token_ring(mkv, 73, {"ctx": xp})

    at = lax.broadcasted_iota(jnp.int32, (1, DIL), 1) + c * tokens
    wide = lambda k: jnp.concatenate([cols[k], cols[k]], axis=1)

    def trunk(half, first, length):
        def kept(x, shift, inside=None):
            d = at + (half * DIL + shift) - first
            keep = jnp.logical_or(d < 0, d >= length)
            if inside is not None:
                keep = jnp.logical_and(keep, inside)
            return jnp.where(keep, x.astype(jnp.float32), 0.0)

        here = kept(seq[:, half * DIL : (half + 1) * DIL], 0)
        if half == 0:
            before, after = kept(low[...], -DIL, c != 0), kept(seq[:, DIL:], DIL)
        else:
            before, after = kept(seq[:, :DIL], -DIL), kept(high[...], DIL, c != n - 1)
        conv = wide(0) * before + wide(1) * here + wide(2) * after + wide(3)
        return (here + jax.nn.gelu(conv, approximate=True)).astype(bf)

    ring_p.begin()
    halo_low.wait()
    gb0[h] = trunk(0, 0, 0)
    ring_b0.begin()
    halo_high.wait()
    gb1[h] = trunk(1, 0, 0)
    ring_b1.begin()

    r = lax.broadcasted_iota(jnp.int32, (tokens, share), 1)
    offset = (r // (DEL // 2) - 1) * DIL + r % (DEL // 2)
    here = lax.broadcasted_iota(jnp.int32, (tokens, share), 0) + c * tokens - offset
    pool = (
        lax.broadcasted_iota(jnp.int32, (tokens // POOL, tokens), 1) // POOL
        == lax.broadcasted_iota(jnp.int32, (tokens // POOL, tokens), 0)
    ).astype(bf)

    def variant(v, _):
        first = dels[v, 0]
        length = dels[v, 1] - first
        own = jnp.concatenate([trunk(0, first, length), trunk(1, first, length)], axis=1)
        for half in range(2):
            pick = (here == first + half * (DEL // 2)).astype(bf)
            moved[2 * v + half] = pack(jnp.dot(own, pick, preferred_element_type=jnp.float32).astype(bf))
        mean = lax.dot_general(pool, own, (((1,), (1,)), ((), ())), preferred_element_type=jnp.float32)
        pooled[v] = (mean * (1.0 / POOL)).astype(bf)
        return 0

    ring_p.relay()
    lax.fori_loop(0, variants, variant, 0)
    shared = []
    for k in range(1, n):
        to = lax.rem(c + k, n)
        made = make(moved.at[to], landed.at[k - 1], 1 + k, {"ctx": to})
        made.start()
        shared.append(made)
    ring_b0.relay()
    total = moved[c]
    for k in range(1, n):
        shared[k - 1].wait_recv()
        total = total + landed[k - 1]
    gm[h] = total
    ring_m.begin()
    ring_b0.end()

    def project(x):
        return jnp.dot(w_ref[...], x, preferred_element_type=jnp.float32).T

    def place(kv, x, count):
        kv[c, :count] = x[:count, HD : 2 * HD].astype(bf)
        kv[c, count:] = pack(x[:count, 2 * HD :].astype(bf))

    x = project(gb0[...].reshape(n * width, DIL))
    place(kv0, x, DIL)
    ring_k0.begin()
    queries[:DIL] = (x[:, :HD] * QSCALE).astype(bf)
    ring_m.relay()
    ring_b1.relay()
    ring_p.end()
    ring_m.end()
    zero = jnp.zeros((1, 128), bf)
    for k in range(n):
        flat[k * width : (k + 1) * width, :128] = gm[k, :width]
        flat[k * width : (k + 1) * width, 128:] = unpack_tail(gm[k, width:], zero)
    x = project(flat[...])
    mq[c] = (x[:share, :HD] * QSCALE).astype(bf)
    ring_q.begin()
    place(mkv, x, share)
    ring_b1.end()
    x = project(gb1[...].reshape(n * width, DIL))
    place(kv1, x, DIL)
    ring_k1.begin()
    ring_o.begin()
    queries[DIL:] = (x[:, :HD] * QSCALE).astype(bf)
    ring_k0.cross()
    ring_k0.relay()
    ring_q.cross()
    ring_q.relay()
    total = jnp.zeros((wo_ref.shape[0], 2 * C), jnp.float32)
    for k in range(0, n, 2):
        two = jnp.concatenate([wp[k], wp[k + 1]], axis=0)
        total = total + jnp.dot(wo_ref[:, k * width : (k + 2) * width], two, preferred_element_type=jnp.float32)
    mix[...] = total.astype(bf)
    ring_q.far_block()
    ring_q.end()

    lane = lax.broadcasted_iota(jnp.int32, (1, 128), 1)
    first = jnp.zeros((1, 128), jnp.int32)
    length = jnp.zeros((1, 128), jnp.int32)
    for v in range(variants):
        first = jnp.where(lane == v, dels[v, 0], first)
        length = jnp.where(lane == v, dels[v, 1] - dels[v, 0], length)
    col = lax.broadcasted_iota(jnp.int32, (tokens, per), 1)
    col_step = col // share * (DEL // 2) + col % (DEL // 2)
    col_offset = (col % share // (DEL // 2) - 1) * DIL + col_step
    qpos = lax.broadcasted_iota(jnp.int32, (tokens, per), 0) + c * tokens

    def aim(v, _):
        s0 = dels[v, 0]
        count = dels[v, 1] - s0
        spot = jnp.logical_and(qpos - col_offset == s0, col_step < count).astype(bf)
        source = jnp.concatenate([mq[2 * v], mq[2 * v + 1]], axis=0)
        moved_q = jnp.dot(spot, source, preferred_element_type=jnp.float32)
        is_mod = changed(qpos[:, :128] - s0, count)
        q_aug[v, :, :HD] = jnp.where(is_mod, moved_q, queries[...].astype(jnp.float32)).astype(bf)
        q_aug[v, :, HD:] = jnp.broadcast_to(jnp.where(lane == v, 1.0, 0.0), (tokens, 128)).astype(bf)
        top[v] = jnp.full((tokens, 128), -3e38, jnp.float32)
        acc[v] = jnp.zeros((tokens, 256), jnp.float32)
        return 0

    lax.fori_loop(0, variants, aim, 0)
    ones = jnp.where(lane == VD - 128, 1.0, 0.0).astype(bf)

    def unit(v, keys, values):
        s = lax.dot_general(q_aug[v], keys, (((1,), (1,)), ((), ())), preferred_element_type=jnp.float32)
        old = top[v]
        new = jnp.maximum(old, jnp.broadcast_to(s.max(1, keepdims=True), old.shape))
        w = jnp.exp2(s - jnp.concatenate([new] * (keys.shape[0] // 128), axis=1)).astype(bf)
        shrink = jnp.exp2(old - new)
        top[v] = new
        acc[v] = acc[v] * jnp.concatenate([shrink, shrink], axis=1) + jnp.dot(
            w, values, preferred_element_type=jnp.float32
        )

    ring_k1.cross()
    ring_k1.relay()

    def attend(step, _):
        look = lambda table: sum((step == i).astype(jnp.int32) * t for i, t in enumerate(table) if t)
        away = look((0, 3, 1, 0, 2, 3, 1, 2))
        across = look((0, 0, 0, 1, 0, 1, 1, 1))
        side = x0 + across * (4 - 2 * x0)
        block = side + lax.rem(y0 + away, 4)
        for i, kv in enumerate((kv0, kv1)):
            rows = slice(i * DIL, (i + 1) * DIL)
            ka[rows, :HD] = kv[block, :DIL]
            pos = lax.broadcasted_iota(jnp.int32, (DIL, 128), 0) + (block * tokens + i * DIL)
            ka[rows, HD:] = jnp.where(changed(pos - first, length), BIG, 0.0).astype(bf)
            va[rows, :128] = kv[block, DIL : 2 * DIL]
            va[rows, 128:] = unpack_tail(kv[block, 2 * DIL :], ones)
        for v in range(variants):
            unit(v, ka[...], va[...])
        return 0

    lax.fori_loop(0, 2, attend, 0)
    ring_k0.far_block()
    ring_k1.far_block()
    ring_o.cross()
    ring_o.relay()
    lax.fori_loop(2, 5, attend, 0)
    ring_k0.end()
    ring_k1.end()
    ring_o.far_block()
    lax.fori_loop(5, n, attend, 0)
    ring_o.end()

    row = lax.broadcasted_iota(jnp.int32, (per, 128), 0)
    step = row // share * (DEL // 2) + row % (DEL // 2)
    row_offset = (row % share // (DEL // 2) - 1) * DIL + step
    count = tokens // POOL // 2
    first_sent = []
    for v in range(variants):
        token = dels[v, 0] + row_offset
        valid = (step < dels[v, 1] - dels[v, 0]) & (token >= 0) & (token < n * tokens)
        ka[:per, HD:] = jnp.where(valid, 0.0, BIG).astype(bf)
        for i in range(2):
            rows = slice(i * share, (i + 1) * share)
            ka[rows, :HD] = mkv[2 * v + i, :share]
            va[rows, :128] = mkv[2 * v + i, share : 2 * share]
            va[rows, 128:] = unpack_tail(mkv[2 * v + i, 2 * share :], ones)
        unit(v, ka[:per], va[:per])
        out = (acc[v, :, :VD] / acc[v, :, VD : VD + 1]).astype(bf)
        mean = jnp.dot(pool, out, preferred_element_type=jnp.float32) * (1.0 / POOL)
        part = jnp.dot(mean.astype(bf), mix[...], preferred_element_type=jnp.float32) + jnp.dot(
            pooled[v], wp_ref[...], preferred_element_type=jnp.float32
        )
        for i in range(2):
            to = 2 * v + i
            mine[to] = part[i * count : (i + 1) * count].astype(bf)
            made = make(mine.at[to], arrived.at[h], 82 + to, {"head": to}, 82 + h)
            first_sent.append(made)

            @pl.when(h != to)
            def _():
                made.start()

            @pl.when(h == to)
            def _():
                arrived[h] = mine[to]

    for k in range(n):
        @pl.when(h != k)
        def _():
            make(mine.at[k], arrived.at[k], 82 + k, {"head": k}).wait_recv()

    total = arrived[0].astype(jnp.float32)
    for k in range(1, n):
        total = total + arrived[k].astype(jnp.float32)
    feats[0] = total[:, :C].astype(bf)
    feats[1] = total[:, C:].astype(bf)
    rows_buf[h] = feats[0]
    for k in range(n):
        to = lax.rem(c + k, n)

        @pl.when(jnp.logical_or(c != h, k != 0))
        def _():
            make(feats.at[1], cols_buf.at[h], 98 + k, {"ctx": to, "head": c}, 98 + h).start()

        @pl.when(jnp.logical_and(c == h, k == 0))
        def _():
            cols_buf[h] = feats[1]

    for k in range(1, n):
        make(feats.at[0], rows_buf.at[h], 90 + k, {"head": lax.rem(h + k, n)}).start()
    for ring in (ring_b0, ring_b1, ring_m, ring_p, ring_k0, ring_k1, ring_q, ring_o):
        ring.drain()
    for made in shared:
        made.wait_send()
    for k, made in enumerate(first_sent):
        @pl.when(h != k)
        def _():
            made.wait_send()

    for k in range(1, n):
        source = lax.rem(h + n - k, n)
        made = make(feats.at[0], rows_buf.at[source], 90 + k, {"head": lax.rem(h + k, n)})
        made.wait_recv()
        made.wait_send()
    for k in range(n):
        @pl.when(jnp.logical_or(c != h, k != h))
        def _():
            make(feats.at[1], cols_buf.at[k], 98 + k, {"head": lax.rem(h + 1, n)}).wait_recv()

        @pl.when(jnp.logical_or(c != h, k != 0))
        def _():
            make(feats.at[1], cols_buf.at[h], 98 + k, {"head": lax.rem(h + 1, n)}).wait_send()
    row_out[...] = rows_buf[...]
    col_out[...] = cols_buf[...]


def features(sequence, deletions, conv_taps, conv_bias, w_proj, w_out, w_pair):
    tokens, width = sequence.shape
    variants = deletions.shape[0]
    n = 8
    share = SEGS * DEL // 2
    vm = pl.BlockSpec(memory_space=pltpu.VMEM)
    bf, f32 = jnp.bfloat16, jnp.float32
    part = variants * tokens // POOL // n
    scratch = [
        ((width, DIL), bf),
        ((width, DIL), bf),
        ((4, width, 128), f32),
        ((n, width, DIL), bf),
        ((n, width, DIL), bf),
        ((n, share * 3 // 2, 128), bf),
        ((n, width, 2 * C), bf),
        ((n, share * 3 // 2, 128), bf),
        ((n - 1, share * 3 // 2, 128), bf),
        ((n * width, 256), bf),
        ((n, DIL * 5 // 2, 128), bf),
        ((n, DIL * 5 // 2, 128), bf),
        ((n, share, 128), bf),
        ((n, share * 5 // 2, 128), bf),
        ((tokens, HD), bf),
        ((variants, tokens, 256), bf),
        ((variants, tokens, 128), f32),
        ((variants, tokens, 256), f32),
        ((tokens, 256), bf),
        ((tokens, 256), bf),
        ((variants, tokens // POOL, width), bf),
        ((w_out.shape[0], 2 * C), bf),
        ((n, part, 2 * C), bf),
        ((n, part, 2 * C), bf),
        ((n, part, C), bf),
        ((n, part, C), bf),
        ((2, part, C), bf),
    ]
    return pl.pallas_call(
        features_kernel,
        out_shape=(jax.ShapeDtypeStruct((n, part, C), bf),) * 2,
        in_specs=[pl.BlockSpec(memory_space=pltpu.SMEM)] + [vm] * 6,
        out_specs=(vm, vm),
        scratch_shapes=[pltpu.VMEM(shape, kind) for shape, kind in scratch]
        + [pltpu.SemaphoreType.DMA((106,)), pltpu.SemaphoreType.DMA((106,))],
        compiler_params=pltpu.CompilerParams(
            collective_id=0, has_side_effects=True, vmem_limit_bytes=56 * 2**20
        ),
    )(deletions, sequence.T, conv_taps, conv_bias.reshape(1, width), w_proj.T, w_out, w_pair)


def local(sequence, deletions, conv_taps, conv_bias, w_proj, w_out, w_pair, dist_table):
    variants = deletions.shape[0]
    row_feats, col_feats = features(sequence, deletions, conv_taps, conv_bias, w_proj, w_out, w_pair)
    shape = (variants, sequence.shape[0] // POOL, C)
    return pair_map(row_feats.reshape(shape), col_feats.reshape(shape), dist_table)


def solution(mesh):
    in_specs = (
        P("ctx", "head"),
        P("var", None),
        P(None, "head"),
        P("head"),
        P(None, "head"),
        P("head", None),
        P("head", None),
        P(),
    )
    out_specs = P("var", "ctx", "head", None)
    return jax.shard_map(local, mesh=mesh, in_specs=in_specs, out_specs=out_specs, check_vma=False)
```

```python
import functools
import math

import jax
import jax.numpy as jnp
from jax import lax
from jax.experimental import pallas as pl
from jax.experimental.pallas import tpu as pltpu
from jax.sharding import PartitionSpec as P

HD = 128
VD = 192
C = 128
NB = 16
POOL = 4
DIL = 256
DEL = 128
SEGS = 3
BIG = -1e30
QSCALE = math.log2(math.e) / math.sqrt(HD)


def changed(delta, length):
    hit = jnp.logical_and(delta >= 0, delta < length)
    for shift in (-DIL, DIL):
        moved = delta + shift
        hit = jnp.logical_or(hit, jnp.logical_and(moved >= 0, moved < length))
    return hit


def pair_kernel(rows_per, row_ref, col_ref, table_ref, out_ref, rel, rows, cols):
    step = pl.program_id(0)
    span = col_ref.shape[1]
    row_count = row_ref.shape[1]

    @pl.when(step == 0)
    def _():
        base = lax.axis_index("head") * span - lax.axis_index("ctx") * row_count - (row_count - 1)
        dist = jnp.abs(lax.broadcasted_iota(jnp.int32, rel.shape, 0) + base)
        value = jnp.broadcast_to(table_ref[0:1, :], rel.shape)
        for k in range(NB - 1):
            value = jnp.where(dist >= 2**k, table_ref[k + 1 : k + 2, :], value)
        rel[...] = value
        rows[...] = row_ref[...].astype(jnp.float32)
        cols[...] = col_ref[...].astype(jnp.float32)

    def one(i, _):
        row = step * rows_per + i
        shifted = rel[pl.ds(row_count - 1 - row, span), :]
        for v in range(row_ref.shape[0]):
            out_ref[v, i] = (rows[v, pl.ds(row, 1), :] + (cols[v] + shifted)).astype(out_ref.dtype)
        return 0

    lax.fori_loop(0, rows_per, one, 0)


def pair_map(row_feats, col_feats, table):
    variants, rows, _ = row_feats.shape
    cols = col_feats.shape[1]
    per = 8
    vm = pl.BlockSpec(memory_space=pltpu.VMEM)
    return pl.pallas_call(
        functools.partial(pair_kernel, per),
        grid=(rows // per,),
        out_shape=jax.ShapeDtypeStruct((variants, rows, cols, C), jnp.bfloat16),
        in_specs=[vm, vm, vm],
        out_specs=pl.BlockSpec((variants, per, cols, C), lambda i: (0, i, 0, 0)),
        scratch_shapes=[
            pltpu.VMEM((rows + cols, C), jnp.float32),
            pltpu.VMEM((variants, rows, C), jnp.float32),
            pltpu.VMEM((variants, cols, C), jnp.float32),
        ],
        compiler_params=pltpu.CompilerParams(vmem_limit_bytes=60 * 2**20),
    )(row_feats, col_feats, table)


MESH = pl.DeviceIdType.MESH


def pack(x):
    half = x.shape[0] // 2
    tail = jnp.concatenate([x[:half, 128:], x[half:, 128:]], axis=1)
    return jnp.concatenate([x[:, :128], tail], axis=0)


class Ring:
    def __init__(self, make, buf, rows, base, me, dn, up, far, mate, mate_of, to_dn, to_up, to_mate):
        half = rows // 2
        self.full, self.lo, self.hi = pl.ds(0, rows), pl.ds(0, half), pl.ds(half, half)
        self.make, self.buf, self.base = make, buf, base
        self.me, self.dn, self.up, self.far, self.mate, self.mate_of = me, dn, up, far, mate, mate_of
        self.to_dn, self.to_up, self.to_mate = to_dn, to_up, to_mate
        self.sent = []

    def copy(self, slot, rows, index, target):
        ref = self.buf.at[slot, rows]
        return self.make(ref, ref, self.base + index, target)

    def send(self, slot, rows, index, target):
        made = self.copy(slot, rows, index, target)
        made.start()
        self.sent.append(made)

    def got(self, slot, rows, index):
        self.copy(slot, rows, index, self.to_up).wait_recv()


class HeadRing(Ring):
    def begin(self):
        self.send(self.me, self.full, 0, self.to_up)
        self.send(self.me, self.full, 1, self.to_dn)
        self.send(self.me, self.full, 2, self.to_mate)

    def relay(self):
        self.got(self.dn, self.full, 0)
        self.send(self.dn, self.lo, 3, self.to_up)
        self.send(self.dn, self.full, 4, self.to_mate)
        self.got(self.up, self.full, 1)
        self.send(self.up, self.hi, 5, self.to_dn)
        self.send(self.up, self.full, 6, self.to_mate)

    def end(self):
        self.got(self.far, self.lo, 3)
        self.send(self.far, self.lo, 7, self.to_mate)
        self.got(self.far, self.hi, 5)
        self.send(self.far, self.hi, 8, self.to_mate)
        self.got(self.mate, self.full, 2)
        self.got(self.mate_of(self.dn), self.full, 4)
        self.got(self.mate_of(self.up), self.full, 6)
        self.got(self.mate_of(self.far), self.lo, 7)
        self.got(self.mate_of(self.far), self.hi, 8)

    def drain(self):
        for made in self.sent:
            made.wait_send()


class TokenRing(Ring):
    def begin(self):
        self.send(self.me, self.full, 2, self.to_mate)
        self.send(self.me, self.full, 0, self.to_up)
        self.send(self.me, self.full, 1, self.to_dn)

    def cross(self):
        self.got(self.mate, self.full, 2)
        self.send(self.mate, self.full, 4, self.to_up)
        self.send(self.mate, self.full, 6, self.to_dn)

    def relay(self):
        self.got(self.dn, self.full, 0)
        self.send(self.dn, self.lo, 3, self.to_up)
        self.got(self.up, self.full, 1)
        self.send(self.up, self.hi, 5, self.to_dn)

    def far_block(self):
        self.got(self.far, self.lo, 3)
        self.send(self.far, self.lo, 7, self.to_mate)
        self.got(self.far, self.hi, 5)
        self.send(self.far, self.hi, 8, self.to_mate)

    def end(self):
        self.got(self.mate_of(self.dn), self.full, 4)
        self.got(self.mate_of(self.up), self.full, 6)
        self.got(self.mate_of(self.far), self.lo, 7)
        self.got(self.mate_of(self.far), self.hi, 8)

    def drain(self):
        for made in self.sent:
            made.wait_send()


def swap_lanes(x):
    return jnp.concatenate([x[:, 64:], x[:, :64]], axis=1)


def unpack_tail(tail, fill):
    both = jnp.concatenate([tail, swap_lanes(tail)], axis=0)
    keep = lax.broadcasted_iota(jnp.int32, both.shape, 1) < 64
    return jnp.where(keep, both, jnp.broadcast_to(fill, both.shape))


def features_kernel(dels, seq, taps, bias, w_ref, wo_ref, wp_ref, row_out, col_out,
                    low, high, cols, gb0, gb1, gm, wp, moved, landed, flat, kv0, kv1, mq, mkv,
                    queries, q_aug, top, acc, ka, va, pooled, mix, mine, arrived, rows_buf, cols_buf, feats,
                    send, recv):
    width, tokens = seq.shape
    variants = dels.shape[1]
    share = SEGS * DEL // 2
    per = 2 * share
    n = 8
    bf = jnp.bfloat16
    c, h, g = lax.axis_index("ctx"), lax.axis_index("head"), lax.axis_index("var")
    dn_h, up_h, far_h = lax.rem(h + 6, n), lax.rem(h + 2, n), lax.rem(h + 4, n)
    sib = h + 1 - 2 * lax.rem(h, 2)
    x0, y0 = c // 4 * 4, lax.rem(c, 4)
    up_c, dn_c, far_c = x0 + lax.rem(y0 + 1, 4), x0 + lax.rem(y0 + 3, 4), x0 + lax.rem(y0 + 2, 4)
    other = lambda t: lax.rem(t + 4, n)
    xp = other(c)
    sib_of = lambda t: t + 1 - 2 * lax.rem(t, 2)

    barrier = pltpu.get_barrier_semaphore()
    peers = [{"ctx": lax.rem(c + k, n)} for k in range(1, n)]
    peers += [{"head": lax.rem(h + k, n)} for k in range(1, n)]
    peers += [{"ctx": xp, "var": 1 - g}]
    for peer in peers:
        pl.semaphore_signal(barrier, inc=1, device_id=peer, device_id_type=MESH)
    for k in range(n):
        source = lax.rem(h + k, n)

        @pl.when(jnp.logical_or(c != h, k != 0))
        def _():
            pl.semaphore_signal(barrier, inc=1, device_id={"ctx": h, "head": source}, device_id_type=MESH)

    for k in range(4):
        line = bias[...] if k == 3 else taps[k : k + 1, :]
        cols[k] = jnp.broadcast_to(line, (128, width)).T
    wp[h] = wp_ref[...]
    run = DEL // 2
    r = lax.broadcasted_iota(jnp.int32, (tokens, 4 * run), 1)
    offset = (r // run - 2) * DIL + (r // (2 * run)) * DIL + r % run
    local_token = lax.broadcasted_iota(jnp.int32, (tokens, 4 * run), 0) + c * tokens - offset

    def gather_runs(v, _):
        for half in range(2):
            pick = (local_token == dels[0, v] + half * run).astype(bf)
            moved[2 * v + half] = jnp.dot(seq[...], pick, preferred_element_type=jnp.float32).astype(bf)
        return 0

    lax.fori_loop(0, variants, gather_runs, 0)
    pl.semaphore_wait(barrier, len(peers) + n - (c == h).astype(jnp.int32))

    def make(src, dst, index, target, arrival=None):
        return pltpu.make_async_remote_copy(
            src_ref=src, dst_ref=dst, send_sem=send.at[index],
            recv_sem=recv.at[index if arrival is None else arrival],
            device_id=(target.get("ctx", c), target.get("head", h), target.get("var", g)), device_id_type=MESH,
        )

    halo_low = make(seq.at[:, pl.ds(tokens - DIL, DIL)], low, 0, {"ctx": lax.rem(c + 1, n)})
    halo_high = make(seq.at[:, pl.ds(0, DIL)], high, 1, {"ctx": lax.rem(c + 7, n)})
    halo_low.start()
    halo_high.start()
    shared = []
    for k in (4, 3, 5, 2, 6, 1, 7):
        to = lax.rem(c + k, n)
        made = make(moved.at[to], landed.at[k - 1], 1 + k, {"ctx": to})
        made.start()
        shared.append(made)

    def head_ring(buf, base):
        return HeadRing(make, buf, buf.shape[1], base, h, dn_h, up_h, far_h, sib, sib_of,
                        {"head": dn_h}, {"head": up_h}, {"head": sib})

    def token_ring(buf, base, to_mate):
        return TokenRing(make, buf, buf.shape[1], base, c, dn_c, up_c, far_c, xp, other,
                         {"ctx": dn_c}, {"ctx": up_c}, to_mate)

    ring_b0, ring_b1, ring_m, ring_p = (head_ring(buf, 10 + 9 * i) for i, buf in enumerate((gb0, gb1, gm, wp)))
    cross = {"ctx": xp, "var": 1 - g}
    ring_k0, ring_k1 = token_ring(kv0, 46, cross), token_ring(kv1, 55, cross)
    ring_q, ring_o = token_ring(mq, 64, {"ctx": xp}), token_ring(mkv, 73, {"ctx": xp})

    at = lax.broadcasted_iota(jnp.int32, (1, DIL), 1) + c * tokens
    wide = lambda k: jnp.concatenate([cols[k], cols[k]], axis=1)

    def trunk(half, first, length):
        def kept(x, shift, inside=None):
            d = at + (half * DIL + shift) - first
            keep = jnp.logical_or(d < 0, d >= length)
            if inside is not None:
                keep = jnp.logical_and(keep, inside)
            return jnp.where(keep, x.astype(jnp.float32), 0.0)

        here = kept(seq[:, half * DIL : (half + 1) * DIL], 0)
        if half == 0:
            before, after = kept(low[...], -DIL, c != 0), kept(seq[:, DIL:], DIL)
        else:
            before, after = kept(seq[:, :DIL], -DIL), kept(high[...], DIL, c != n - 1)
        conv = wide(0) * before + wide(1) * here + wide(2) * after + wide(3)
        return (here + jax.nn.gelu(conv, approximate=True)).astype(bf)

    ring_p.begin()
    halo_low.wait()
    gb0[h] = trunk(0, 0, 0)
    ring_b0.begin()
    halo_high.wait()
    gb1[h] = trunk(1, 0, 0)
    ring_b1.begin()

    pool = (
        lax.broadcasted_iota(jnp.int32, (tokens // POOL, tokens), 1) // POOL
        == lax.broadcasted_iota(jnp.int32, (tokens // POOL, tokens), 0)
    ).astype(bf)

    def project(x):
        return jnp.dot(w_ref[...], x, preferred_element_type=jnp.float32).T

    def place(kv, x, count):
        kv[c, :count] = x[:count, HD : 2 * HD].astype(bf)
        kv[c, count:] = pack(x[:count, 2 * HD :].astype(bf))

    ring_b0.relay()
    ring_p.relay()
    ring_b0.end()
    x = project(gb0[...].reshape(n * width, DIL))
    place(kv0, x, DIL)
    ring_k0.begin()
    queries[:DIL] = (x[:, :HD] * QSCALE).astype(bf)
    ring_b1.relay()

    total = moved[c].astype(jnp.float32)
    for made in shared:
        made.wait_recv()
    for k in range(1, n):
        total = total + landed[k - 1].astype(jnp.float32)
    runs = [total[:, i * run : (i + 1) * run] for i in range(4)]
    nil = jnp.zeros((width, run), jnp.float32)
    t0, t1, t2, t3 = (cols[k, :, :run] for k in range(4))
    made_rows = []
    for before, here, after in ((runs[0], runs[1], nil), (runs[1], nil, runs[2]), (nil, runs[2], runs[3])):
        conv = t0 * before + t1 * here + t2 * after + t3
        made_rows.append((here + jax.nn.gelu(conv, approximate=True)).astype(bf))
    tail = made_rows[2]
    gm[h, :width] = jnp.concatenate(made_rows[:2], axis=1)
    gm[h, width:] = jnp.concatenate([tail[: width // 2], tail[width // 2 :]], axis=1)
    ring_m.begin()
    ring_b1.end()
    x = project(gb1[...].reshape(n * width, DIL))
    place(kv1, x, DIL)
    ring_k1.begin()
    queries[DIL:] = (x[:, :HD] * QSCALE).astype(bf)
    ring_m.relay()
    ring_p.end()
    ring_m.end()
    zero = jnp.zeros((1, 128), bf)
    for k in range(n):
        flat[k * width : (k + 1) * width, :128] = gm[k, :width]
        flat[k * width : (k + 1) * width, 128:] = unpack_tail(gm[k, width:], zero)
    x = project(flat[...])
    mq[c] = (x[:share, :HD] * QSCALE).astype(bf)
    ring_q.begin()
    place(mkv, x, share)
    ring_o.begin()
    ring_k0.cross()
    ring_k0.relay()

    def variant(v, _):
        first = dels[0, v]
        length = dels[1, v] - first
        own = jnp.concatenate([trunk(0, first, length), trunk(1, first, length)], axis=1)
        mean = lax.dot_general(pool, own, (((1,), (1,)), ((), ())), preferred_element_type=jnp.float32)
        pooled[v] = (mean * (1.0 / POOL)).astype(bf)
        return 0

    lax.fori_loop(0, variants, variant, 0)
    ring_k1.cross()
    ring_k1.relay()
    ring_q.cross()
    ring_q.relay()
    total = jnp.zeros((wo_ref.shape[0], 2 * C), jnp.float32)
    for k in range(0, n, 2):
        two = jnp.concatenate([wp[k], wp[k + 1]], axis=0)
        total = total + jnp.dot(wo_ref[:, k * width : (k + 2) * width], two, preferred_element_type=jnp.float32)
    mix[...] = total.astype(bf)
    ring_q.far_block()
    ring_q.end()

    lane = lax.broadcasted_iota(jnp.int32, (1, 128), 1)
    first = jnp.zeros((1, 128), jnp.int32)
    length = jnp.zeros((1, 128), jnp.int32)
    for v in range(variants):
        first = jnp.where(lane == v, dels[0, v], first)
        length = jnp.where(lane == v, dels[1, v] - dels[0, v], length)
    col = lax.broadcasted_iota(jnp.int32, (tokens, per), 1)
    col_step = col // share * (DEL // 2) + col % (DEL // 2)
    col_offset = (col % share // (DEL // 2) - 1) * DIL + col_step
    qpos = lax.broadcasted_iota(jnp.int32, (tokens, per), 0) + c * tokens

    def aim(v, _):
        s0 = dels[0, v]
        count = dels[1, v] - s0
        spot = jnp.logical_and(qpos - col_offset == s0, col_step < count).astype(bf)
        source = jnp.concatenate([mq[2 * v], mq[2 * v + 1]], axis=0)
        moved_q = jnp.dot(spot, source, preferred_element_type=jnp.float32)
        is_mod = changed(qpos[:, :128] - s0, count)
        q_aug[v, :, :HD] = jnp.where(is_mod, moved_q, queries[...].astype(jnp.float32)).astype(bf)
        q_aug[v, :, HD:] = jnp.broadcast_to(jnp.where(lane == v, 1.0, 0.0), (tokens, 128)).astype(bf)
        top[v] = jnp.full((tokens, 128), -3e38, jnp.float32)
        acc[v] = jnp.zeros((tokens, 256), jnp.float32)
        return 0

    lax.fori_loop(0, variants, aim, 0)
    ones = jnp.where(lane == VD - 128, 1.0, 0.0).astype(bf)

    def unit(v, keys, values):
        s = lax.dot_general(q_aug[v], keys, (((1,), (1,)), ((), ())), preferred_element_type=jnp.float32)
        old = top[v]
        new = jnp.maximum(old, jnp.broadcast_to(s.max(1, keepdims=True), old.shape))
        w = jnp.exp2(s - jnp.concatenate([new] * (keys.shape[0] // 128), axis=1)).astype(bf)
        shrink = jnp.exp2(old - new)
        top[v] = new
        acc[v] = acc[v] * jnp.concatenate([shrink, shrink], axis=1) + jnp.dot(
            w, values, preferred_element_type=jnp.float32
        )

    def attend(step, _):
        look = lambda table: sum((step == i).astype(jnp.int32) * t for i, t in enumerate(table) if t)
        away = look((0, 3, 1, 0, 2, 3, 1, 2))
        across = look((0, 0, 0, 1, 0, 1, 1, 1))
        side = x0 + across * (4 - 2 * x0)
        block = side + lax.rem(y0 + away, 4)
        for i, kv in enumerate((kv0, kv1)):
            rows = slice(i * DIL, (i + 1) * DIL)
            ka[rows, :HD] = kv[block, :DIL]
            pos = lax.broadcasted_iota(jnp.int32, (DIL, 128), 0) + (block * tokens + i * DIL)
            ka[rows, HD:] = jnp.where(changed(pos - first, length), BIG, 0.0).astype(bf)
            va[rows, :128] = kv[block, DIL : 2 * DIL]
            va[rows, 128:] = unpack_tail(kv[block, 2 * DIL :], ones)
        for v in range(variants):
            unit(v, ka[...], va[...])
        return 0

    lax.fori_loop(0, 2, attend, 0)
    ring_k0.far_block()
    ring_k1.far_block()
    ring_o.cross()
    ring_o.relay()
    lax.fori_loop(2, 5, attend, 0)
    ring_k0.end()
    ring_k1.end()
    ring_o.far_block()
    lax.fori_loop(5, n, attend, 0)
    ring_o.end()

    row = lax.broadcasted_iota(jnp.int32, (per, 128), 0)
    step = row // share * (DEL // 2) + row % (DEL // 2)
    row_offset = (row % share // (DEL // 2) - 1) * DIL + step
    count = tokens // POOL // 2
    first_sent = []
    for v in range(variants):
        token = dels[0, v] + row_offset
        valid = (step < dels[1, v] - dels[0, v]) & (token >= 0) & (token < n * tokens)
        ka[:per, HD:] = jnp.where(valid, 0.0, BIG).astype(bf)
        for i in range(2):
            rows = slice(i * share, (i + 1) * share)
            ka[rows, :HD] = mkv[2 * v + i, :share]
            va[rows, :128] = mkv[2 * v + i, share : 2 * share]
            va[rows, 128:] = unpack_tail(mkv[2 * v + i, 2 * share :], ones)
        unit(v, ka[:per], va[:per])
        out = (acc[v, :, :VD] / acc[v, :, VD : VD + 1]).astype(bf)
        mean = jnp.dot(pool, out, preferred_element_type=jnp.float32) * (1.0 / POOL)
        part = jnp.dot(mean.astype(bf), mix[...], preferred_element_type=jnp.float32) + jnp.dot(
            pooled[v], wp_ref[...], preferred_element_type=jnp.float32
        )
        for i in range(2):
            to = 2 * v + i
            mine[to] = part[i * count : (i + 1) * count].astype(bf)
            made = make(mine.at[to], arrived.at[h], 82 + to, {"head": to}, 82 + h)
            first_sent.append(made)

            @pl.when(h != to)
            def _():
                made.start()

            @pl.when(h == to)
            def _():
                arrived[h] = mine[to]

    for k in range(n):
        @pl.when(h != k)
        def _():
            make(mine.at[k], arrived.at[k], 82 + k, {"head": k}).wait_recv()

    total = arrived[0].astype(jnp.float32)
    for k in range(1, n):
        total = total + arrived[k].astype(jnp.float32)
    feats[0] = total[:, :C].astype(bf)
    feats[1] = total[:, C:].astype(bf)
    rows_buf[h] = feats[0]
    for k in range(n):
        to = lax.rem(c + k, n)

        @pl.when(jnp.logical_or(c != h, k != 0))
        def _():
            make(feats.at[1], cols_buf.at[h], 98 + k, {"ctx": to, "head": c}, 98 + h).start()

        @pl.when(jnp.logical_and(c == h, k == 0))
        def _():
            cols_buf[h] = feats[1]

    for k in range(1, n):
        make(feats.at[0], rows_buf.at[h], 90 + k, {"head": lax.rem(h + k, n)}).start()
    for ring in (ring_b0, ring_b1, ring_m, ring_p, ring_k0, ring_k1, ring_q, ring_o):
        ring.drain()
    for made in shared:
        made.wait_send()
    for k, made in enumerate(first_sent):
        @pl.when(h != k)
        def _():
            made.wait_send()

    for k in range(1, n):
        source = lax.rem(h + n - k, n)
        made = make(feats.at[0], rows_buf.at[source], 90 + k, {"head": lax.rem(h + k, n)})
        made.wait_recv()
        made.wait_send()
    for k in range(n):
        @pl.when(jnp.logical_or(c != h, k != h))
        def _():
            make(feats.at[1], cols_buf.at[k], 98 + k, {"head": lax.rem(h + 1, n)}).wait_recv()

        @pl.when(jnp.logical_or(c != h, k != 0))
        def _():
            make(feats.at[1], cols_buf.at[h], 98 + k, {"head": lax.rem(h + 1, n)}).wait_send()
    row_out[...] = rows_buf[...]
    col_out[...] = cols_buf[...]


def features(sequence, deletions, conv_taps, conv_bias, w_proj, w_out, w_pair):
    tokens, width = sequence.shape
    variants = deletions.shape[0]
    n = 8
    share = SEGS * DEL // 2
    vm = pl.BlockSpec(memory_space=pltpu.VMEM)
    bf, f32 = jnp.bfloat16, jnp.float32
    part = variants * tokens // POOL // n
    scratch = [
        ((width, DIL), bf),
        ((width, DIL), bf),
        ((4, width, 128), f32),
        ((n, width, DIL), bf),
        ((n, width, DIL), bf),
        ((n, share * 3 // 2, 128), bf),
        ((n, width, 2 * C), bf),
        ((n, width, 2 * DEL), bf),
        ((n - 1, width, 2 * DEL), bf),
        ((n * width, 256), bf),
        ((n, DIL * 5 // 2, 128), bf),
        ((n, DIL * 5 // 2, 128), bf),
        ((n, share, 128), bf),
        ((n, share * 5 // 2, 128), bf),
        ((tokens, HD), bf),
        ((variants, tokens, 256), bf),
        ((variants, tokens, 128), f32),
        ((variants, tokens, 256), f32),
        ((tokens, 256), bf),
        ((tokens, 256), bf),
        ((variants, tokens // POOL, width), bf),
        ((w_out.shape[0], 2 * C), bf),
        ((n, part, 2 * C), bf),
        ((n, part, 2 * C), bf),
        ((n, part, C), bf),
        ((n, part, C), bf),
        ((2, part, C), bf),
    ]
    return pl.pallas_call(
        features_kernel,
        out_shape=(jax.ShapeDtypeStruct((n, part, C), bf),) * 2,
        in_specs=[pl.BlockSpec(memory_space=pltpu.SMEM)] + [vm] * 6,
        out_specs=(vm, vm),
        scratch_shapes=[pltpu.VMEM(shape, kind) for shape, kind in scratch]
        + [pltpu.SemaphoreType.DMA((106,)), pltpu.SemaphoreType.DMA((106,))],
        compiler_params=pltpu.CompilerParams(
            collective_id=0, has_side_effects=True, vmem_limit_bytes=56 * 2**20
        ),
    )(deletions.T, sequence.T, conv_taps, conv_bias.reshape(1, width), w_proj.T, w_out, w_pair)


def local(sequence, deletions, conv_taps, conv_bias, w_proj, w_out, w_pair, dist_table):
    variants = deletions.shape[0]
    row_feats, col_feats = features(sequence, deletions, conv_taps, conv_bias, w_proj, w_out, w_pair)
    shape = (variants, sequence.shape[0] // POOL, C)
    return pair_map(row_feats.reshape(shape), col_feats.reshape(shape), dist_table)


def solution(mesh):
    in_specs = (
        P("ctx", "head"),
        P("var", None),
        P(None, "head"),
        P("head"),
        P(None, "head"),
        P("head", None),
        P("head", None),
        P(),
    )
    out_specs = P("var", "ctx", "head", None)
    return jax.shard_map(local, mesh=mesh, in_specs=in_specs, out_specs=out_specs, check_vma=False)
```

```python
import functools
import math

import jax
import jax.numpy as jnp
from jax import lax
from jax.experimental import pallas as pl
from jax.experimental.pallas import tpu as pltpu
from jax.sharding import PartitionSpec as P

HD = 128
VD = 192
C = 128
NB = 16
POOL = 4
DIL = 256
DEL = 128
SEGS = 3
BIG = -1e30
QSCALE = math.log2(math.e) / math.sqrt(HD)


def changed(delta, length):
    hit = jnp.logical_and(delta >= 0, delta < length)
    for shift in (-DIL, DIL):
        moved = delta + shift
        hit = jnp.logical_or(hit, jnp.logical_and(moved >= 0, moved < length))
    return hit


def pair_kernel(rows_per, row_ref, col_ref, table_ref, out_ref, rel, rows, cols):
    step = pl.program_id(0)
    span = col_ref.shape[1]
    row_count = row_ref.shape[1]

    @pl.when(step == 0)
    def _():
        base = lax.axis_index("head") * span - lax.axis_index("ctx") * row_count - (row_count - 1)
        dist = jnp.abs(lax.broadcasted_iota(jnp.int32, rel.shape, 0) + base)
        value = jnp.broadcast_to(table_ref[0:1, :], rel.shape)
        for k in range(NB - 1):
            value = jnp.where(dist >= 2**k, table_ref[k + 1 : k + 2, :], value)
        rel[...] = value
        rows[...] = row_ref[...].astype(jnp.float32)
        cols[...] = col_ref[...].astype(jnp.float32)

    def one(i, _):
        row = step * rows_per + i
        shifted = rel[pl.ds(row_count - 1 - row, span), :]
        for v in range(row_ref.shape[0]):
            out_ref[v, i] = (rows[v, pl.ds(row, 1), :] + (cols[v] + shifted)).astype(out_ref.dtype)
        return 0

    lax.fori_loop(0, rows_per, one, 0)


def pair_map(row_feats, col_feats, table):
    variants, rows, _ = row_feats.shape
    cols = col_feats.shape[1]
    per = 8
    vm = pl.BlockSpec(memory_space=pltpu.VMEM)
    return pl.pallas_call(
        functools.partial(pair_kernel, per),
        grid=(rows // per,),
        out_shape=jax.ShapeDtypeStruct((variants, rows, cols, C), jnp.bfloat16),
        in_specs=[vm, vm, vm],
        out_specs=pl.BlockSpec((variants, per, cols, C), lambda i: (0, i, 0, 0)),
        scratch_shapes=[
            pltpu.VMEM((rows + cols, C), jnp.float32),
            pltpu.VMEM((variants, rows, C), jnp.float32),
            pltpu.VMEM((variants, cols, C), jnp.float32),
        ],
        compiler_params=pltpu.CompilerParams(vmem_limit_bytes=60 * 2**20),
    )(row_feats, col_feats, table)


MESH = pl.DeviceIdType.MESH


def pack(x):
    half = x.shape[0] // 2
    tail = jnp.concatenate([x[:half, 128:], x[half:, 128:]], axis=1)
    return jnp.concatenate([x[:, :128], tail], axis=0)


class Ring:
    def __init__(self, make, buf, rows, base, me, dn, up, far, mate, mate_of, to_dn, to_up, to_mate):
        half = rows // 2
        self.full, self.lo, self.hi = pl.ds(0, rows), pl.ds(0, half), pl.ds(half, half)
        self.make, self.buf, self.base = make, buf, base
        self.me, self.dn, self.up, self.far, self.mate, self.mate_of = me, dn, up, far, mate, mate_of
        self.to_dn, self.to_up, self.to_mate = to_dn, to_up, to_mate
        self.sent = []

    def copy(self, slot, rows, index, target):
        ref = self.buf.at[slot, rows]
        return self.make(ref, ref, self.base + index, target)

    def send(self, slot, rows, index, target):
        made = self.copy(slot, rows, index, target)
        made.start()
        self.sent.append(made)

    def got(self, slot, rows, index):
        self.copy(slot, rows, index, self.to_up).wait_recv()


class HeadRing(Ring):
    def begin(self):
        self.send(self.me, self.full, 0, self.to_up)
        self.send(self.me, self.full, 1, self.to_dn)
        self.send(self.me, self.full, 2, self.to_mate)

    def relay(self):
        self.got(self.dn, self.full, 0)
        self.send(self.dn, self.lo, 3, self.to_up)
        self.send(self.dn, self.full, 4, self.to_mate)
        self.got(self.up, self.full, 1)
        self.send(self.up, self.hi, 5, self.to_dn)
        self.send(self.up, self.full, 6, self.to_mate)

    def end(self):
        self.got(self.far, self.lo, 3)
        self.send(self.far, self.lo, 7, self.to_mate)
        self.got(self.far, self.hi, 5)
        self.send(self.far, self.hi, 8, self.to_mate)
        self.got(self.mate, self.full, 2)
        self.got(self.mate_of(self.dn), self.full, 4)
        self.got(self.mate_of(self.up), self.full, 6)
        self.got(self.mate_of(self.far), self.lo, 7)
        self.got(self.mate_of(self.far), self.hi, 8)

    def drain(self):
        for made in self.sent:
            made.wait_send()


class TokenRing(Ring):
    def begin(self):
        self.send(self.me, self.full, 2, self.to_mate)
        self.send(self.me, self.full, 0, self.to_up)
        self.send(self.me, self.full, 1, self.to_dn)

    def cross(self):
        self.got(self.mate, self.full, 2)
        self.send(self.mate, self.full, 4, self.to_up)
        self.send(self.mate, self.full, 6, self.to_dn)

    def relay(self):
        self.got(self.dn, self.full, 0)
        self.send(self.dn, self.lo, 3, self.to_up)
        self.got(self.up, self.full, 1)
        self.send(self.up, self.hi, 5, self.to_dn)

    def far_block(self):
        self.got(self.far, self.lo, 3)
        self.send(self.far, self.lo, 7, self.to_mate)
        self.got(self.far, self.hi, 5)
        self.send(self.far, self.hi, 8, self.to_mate)

    def end(self):
        self.got(self.mate_of(self.dn), self.full, 4)
        self.got(self.mate_of(self.up), self.full, 6)
        self.got(self.mate_of(self.far), self.lo, 7)
        self.got(self.mate_of(self.far), self.hi, 8)

    def drain(self):
        for made in self.sent:
            made.wait_send()


def swap_lanes(x):
    return jnp.concatenate([x[:, 64:], x[:, :64]], axis=1)


def unpack_tail(tail, fill):
    both = jnp.concatenate([tail, swap_lanes(tail)], axis=0)
    keep = lax.broadcasted_iota(jnp.int32, both.shape, 1) < 64
    return jnp.where(keep, both, jnp.broadcast_to(fill, both.shape))


def features_kernel(dels, seq, taps, bias, w_ref, wo_ref, wp_ref, row_out, col_out,
                    low, high, cols, gb0, gb1, gm, wp, moved, landed, flat, kv0, kv1, mq, mkv,
                    queries, q_aug, top, acc, ka, va, pooled, mix, mine, arrived, rows_buf, cols_buf, feats,
                    send, recv):
    width, tokens = seq.shape
    variants = dels.shape[1]
    share = SEGS * DEL // 2
    per = 2 * share
    n = 8
    bf = jnp.bfloat16
    c, h, g = lax.axis_index("ctx"), lax.axis_index("head"), lax.axis_index("var")
    dn_h, up_h, far_h = lax.rem(h + 6, n), lax.rem(h + 2, n), lax.rem(h + 4, n)
    sib = h + 1 - 2 * lax.rem(h, 2)
    x0, y0 = c // 4 * 4, lax.rem(c, 4)
    up_c, dn_c, far_c = x0 + lax.rem(y0 + 1, 4), x0 + lax.rem(y0 + 3, 4), x0 + lax.rem(y0 + 2, 4)
    other = lambda t: lax.rem(t + 4, n)
    xp = other(c)
    sib_of = lambda t: t + 1 - 2 * lax.rem(t, 2)

    barrier = pltpu.get_barrier_semaphore()
    peers = [{"ctx": lax.rem(c + k, n)} for k in range(1, n)]
    peers += [{"head": lax.rem(h + k, n)} for k in range(1, n)]
    peers += [{"ctx": xp, "var": 1 - g}]
    for peer in peers:
        pl.semaphore_signal(barrier, inc=1, device_id=peer, device_id_type=MESH)
    for k in range(n):
        source = lax.rem(h + k, n)

        @pl.when(jnp.logical_or(c != h, k != 0))
        def _():
            pl.semaphore_signal(barrier, inc=1, device_id={"ctx": h, "head": source}, device_id_type=MESH)

    for k in range(4):
        line = bias[...] if k == 3 else taps[k : k + 1, :]
        cols[k] = jnp.broadcast_to(line, (128, width)).T
    wp[h] = wp_ref[...]
    run = DEL // 2
    r = lax.broadcasted_iota(jnp.int32, (tokens, 4 * run), 1)
    offset = (r // run - 2) * DIL + (r // (2 * run)) * DIL + r % run
    local_token = lax.broadcasted_iota(jnp.int32, (tokens, 4 * run), 0) + c * tokens - offset

    def gather_runs(v, _):
        for half in range(2):
            pick = (local_token == dels[0, v] + half * run).astype(bf)
            moved[2 * v + half] = jnp.dot(seq[...], pick, preferred_element_type=jnp.float32).astype(bf)
        return 0

    lax.fori_loop(0, variants, gather_runs, 0)
    pl.semaphore_wait(barrier, len(peers) + n - (c == h).astype(jnp.int32))

    def make(src, dst, index, target, arrival=None):
        return pltpu.make_async_remote_copy(
            src_ref=src, dst_ref=dst, send_sem=send.at[index],
            recv_sem=recv.at[index if arrival is None else arrival],
            device_id=(target.get("ctx", c), target.get("head", h), target.get("var", g)), device_id_type=MESH,
        )

    halo_low = make(seq.at[:, pl.ds(tokens - DIL, DIL)], low, 0, {"ctx": lax.rem(c + 1, n)})
    halo_high = make(seq.at[:, pl.ds(0, DIL)], high, 1, {"ctx": lax.rem(c + 7, n)})
    halo_low.start()
    halo_high.start()
    shared = []
    for k in (4, 3, 5, 2, 6, 1, 7):
        to = lax.rem(c + k, n)
        made = make(moved.at[to], landed.at[k - 1], 1 + k, {"ctx": to})
        made.start()
        shared.append(made)

    def head_ring(buf, base):
        return HeadRing(make, buf, buf.shape[1], base, h, dn_h, up_h, far_h, sib, sib_of,
                        {"head": dn_h}, {"head": up_h}, {"head": sib})

    def token_ring(buf, base, to_mate):
        return TokenRing(make, buf, buf.shape[1], base, c, dn_c, up_c, far_c, xp, other,
                         {"ctx": dn_c}, {"ctx": up_c}, to_mate)

    ring_b0, ring_b1, ring_m, ring_p = (head_ring(buf, 10 + 9 * i) for i, buf in enumerate((gb0, gb1, gm, wp)))
    cross = {"ctx": xp, "var": 1 - g}
    ring_k0, ring_k1 = token_ring(kv0, 46, cross), token_ring(kv1, 55, cross)
    ring_o = token_ring(mkv, 73, {"ctx": xp})

    at = lax.broadcasted_iota(jnp.int32, (1, DIL), 1) + c * tokens
    wide = lambda k: jnp.concatenate([cols[k], cols[k]], axis=1)

    def trunk(half, first, length):
        def kept(x, shift, inside=None):
            d = at + (half * DIL + shift) - first
            keep = jnp.logical_or(d < 0, d >= length)
            if inside is not None:
                keep = jnp.logical_and(keep, inside)
            return jnp.where(keep, x.astype(jnp.float32), 0.0)

        here = kept(seq[:, half * DIL : (half + 1) * DIL], 0)
        if half == 0:
            before, after = kept(low[...], -DIL, c != 0), kept(seq[:, DIL:], DIL)
        else:
            before, after = kept(seq[:, :DIL], -DIL), kept(high[...], DIL, c != n - 1)
        conv = wide(0) * before + wide(1) * here + wide(2) * after + wide(3)
        return (here + jax.nn.gelu(conv, approximate=True)).astype(bf)

    ring_p.begin()
    ring_p.relay()
    halo_low.wait()
    gb0[h] = trunk(0, 0, 0)
    ring_b0.begin()
    halo_high.wait()
    gb1[h] = trunk(1, 0, 0)
    ring_b1.begin()

    pool = (
        lax.broadcasted_iota(jnp.int32, (tokens // POOL, tokens), 1) // POOL
        == lax.broadcasted_iota(jnp.int32, (tokens // POOL, tokens), 0)
    ).astype(bf)

    def project(x):
        return jnp.dot(w_ref[...], x, preferred_element_type=jnp.float32).T

    def place(kv, x, count):
        kv[c, :count] = x[:count, HD : 2 * HD].astype(bf)
        kv[c, count:] = pack(x[:count, 2 * HD :].astype(bf))

    ring_p.end()
    ring_b0.relay()
    ring_b1.relay()
    ring_b0.end()

    total = moved[c].astype(jnp.float32)
    for made in shared:
        made.wait_recv()
    for k in range(1, n):
        total = total + landed[k - 1].astype(jnp.float32)
    runs = [total[:, i * run : (i + 1) * run] for i in range(4)]
    nil = jnp.zeros((width, run), jnp.float32)
    t0, t1, t2, t3 = (cols[k, :, :run] for k in range(4))
    made_rows = []
    for before, here, after in ((runs[0], runs[1], nil), (runs[1], nil, runs[2]), (nil, runs[2], runs[3])):
        conv = t0 * before + t1 * here + t2 * after + t3
        made_rows.append((here + jax.nn.gelu(conv, approximate=True)).astype(bf))
    tail = made_rows[2]
    gm[h, :width] = jnp.concatenate(made_rows[:2], axis=1)
    gm[h, width:] = jnp.concatenate([tail[: width // 2], tail[width // 2 :]], axis=1)
    ring_m.begin()
    x = project(gb0[...].reshape(n * width, DIL))
    place(kv0, x, DIL)
    ring_k0.begin()
    queries[:DIL] = (x[:, :HD] * QSCALE).astype(bf)
    ring_b1.end()
    ring_m.relay()
    x = project(gb1[...].reshape(n * width, DIL))
    place(kv1, x, DIL)
    queries[DIL:] = (x[:, :HD] * QSCALE).astype(bf)
    ring_m.end()
    zero = jnp.zeros((1, 128), bf)
    for k in range(n):
        flat[k * width : (k + 1) * width, :128] = gm[k, :width]
        flat[k * width : (k + 1) * width, 128:] = unpack_tail(gm[k, width:], zero)
    x = project(flat[...])
    mq[c] = (x[:share, :HD] * QSCALE).astype(bf)
    asked = []
    for k in (4, 3, 5, 2, 6, 1, 7):
        made = make(mq.at[c], mq.at[c], 64 + k, {"ctx": lax.rem(c + k, n)})
        made.start()
        asked.append(made)
    ring_k1.begin()
    place(mkv, x, share)
    ring_o.begin()
    ring_k0.cross()
    ring_k0.relay()

    def variant(v, _):
        first = dels[0, v]
        length = dels[1, v] - first
        own = jnp.concatenate([trunk(0, first, length), trunk(1, first, length)], axis=1)
        mean = lax.dot_general(pool, own, (((1,), (1,)), ((), ())), preferred_element_type=jnp.float32)
        pooled[v] = (mean * (1.0 / POOL)).astype(bf)
        return 0

    lax.fori_loop(0, variants, variant, 0)
    total = jnp.zeros((wo_ref.shape[0], 2 * C), jnp.float32)
    for k in range(0, n, 2):
        two = jnp.concatenate([wp[k], wp[k + 1]], axis=0)
        total = total + jnp.dot(wo_ref[:, k * width : (k + 2) * width], two, preferred_element_type=jnp.float32)
    mix[...] = total.astype(bf)
    ring_k1.cross()
    ring_k1.relay()
    for k in range(1, n):
        source = lax.rem(c + n - k, n)
        make(mq.at[source], mq.at[source], 64 + k, {"ctx": lax.rem(c + k, n)}).wait_recv()

    lane = lax.broadcasted_iota(jnp.int32, (1, 128), 1)
    first = jnp.zeros((1, 128), jnp.int32)
    length = jnp.zeros((1, 128), jnp.int32)
    for v in range(variants):
        first = jnp.where(lane == v, dels[0, v], first)
        length = jnp.where(lane == v, dels[1, v] - dels[0, v], length)
    col = lax.broadcasted_iota(jnp.int32, (tokens, per), 1)
    col_step = col // share * (DEL // 2) + col % (DEL // 2)
    col_offset = (col % share // (DEL // 2) - 1) * DIL + col_step
    qpos = lax.broadcasted_iota(jnp.int32, (tokens, per), 0) + c * tokens

    def aim(v, _):
        s0 = dels[0, v]
        count = dels[1, v] - s0
        spot = jnp.logical_and(qpos - col_offset == s0, col_step < count).astype(bf)
        source = jnp.concatenate([mq[2 * v], mq[2 * v + 1]], axis=0)
        moved_q = jnp.dot(spot, source, preferred_element_type=jnp.float32)
        is_mod = changed(qpos[:, :128] - s0, count)
        q_aug[v, :, :HD] = jnp.where(is_mod, moved_q, queries[...].astype(jnp.float32)).astype(bf)
        q_aug[v, :, HD:] = jnp.broadcast_to(jnp.where(lane == v, 1.0, 0.0), (tokens, 128)).astype(bf)
        top[v] = jnp.full((tokens, 128), -3e38, jnp.float32)
        acc[v] = jnp.zeros((tokens, 256), jnp.float32)
        return 0

    lax.fori_loop(0, variants, aim, 0)
    ones = jnp.where(lane == VD - 128, 1.0, 0.0).astype(bf)

    def unit(v, keys, values):
        s = lax.dot_general(q_aug[v], keys, (((1,), (1,)), ((), ())), preferred_element_type=jnp.float32)
        old = top[v]
        new = jnp.maximum(old, jnp.broadcast_to(s.max(1, keepdims=True), old.shape))
        w = jnp.exp2(s - jnp.concatenate([new] * (keys.shape[0] // 128), axis=1)).astype(bf)
        shrink = jnp.exp2(old - new)
        top[v] = new
        acc[v] = acc[v] * jnp.concatenate([shrink, shrink], axis=1) + jnp.dot(
            w, values, preferred_element_type=jnp.float32
        )

    def attend(step, _):
        look = lambda table: sum((step == i).astype(jnp.int32) * t for i, t in enumerate(table) if t)
        away = look((0, 3, 1, 0, 2, 3, 1, 2))
        across = look((0, 0, 0, 1, 0, 1, 1, 1))
        side = x0 + across * (4 - 2 * x0)
        block = side + lax.rem(y0 + away, 4)
        for i, kv in enumerate((kv0, kv1)):
            rows = slice(i * DIL, (i + 1) * DIL)
            ka[rows, :HD] = kv[block, :DIL]
            pos = lax.broadcasted_iota(jnp.int32, (DIL, 128), 0) + (block * tokens + i * DIL)
            ka[rows, HD:] = jnp.where(changed(pos - first, length), BIG, 0.0).astype(bf)
            va[rows, :128] = kv[block, DIL : 2 * DIL]
            va[rows, 128:] = unpack_tail(kv[block, 2 * DIL :], ones)
        for v in range(variants):
            unit(v, ka[...], va[...])
        return 0

    lax.fori_loop(0, 2, attend, 0)
    ring_k0.far_block()
    ring_k1.far_block()
    ring_o.cross()
    ring_o.relay()
    lax.fori_loop(2, 5, attend, 0)
    ring_k0.end()
    ring_k1.end()
    ring_o.far_block()
    lax.fori_loop(5, n, attend, 0)
    ring_o.end()

    row = lax.broadcasted_iota(jnp.int32, (per, 128), 0)
    step = row // share * (DEL // 2) + row % (DEL // 2)
    row_offset = (row % share // (DEL // 2) - 1) * DIL + step
    count = tokens // POOL // 2
    first_sent = []
    for v in range(variants):
        token = dels[0, v] + row_offset
        valid = (step < dels[1, v] - dels[0, v]) & (token >= 0) & (token < n * tokens)
        ka[:per, HD:] = jnp.where(valid, 0.0, BIG).astype(bf)
        for i in range(2):
            rows = slice(i * share, (i + 1) * share)
            ka[rows, :HD] = mkv[2 * v + i, :share]
            va[rows, :128] = mkv[2 * v + i, share : 2 * share]
            va[rows, 128:] = unpack_tail(mkv[2 * v + i, 2 * share :], ones)
        unit(v, ka[:per], va[:per])
        out = (acc[v, :, :VD] / acc[v, :, VD : VD + 1]).astype(bf)
        mean = jnp.dot(pool, out, preferred_element_type=jnp.float32) * (1.0 / POOL)
        part = jnp.dot(mean.astype(bf), mix[...], preferred_element_type=jnp.float32) + jnp.dot(
            pooled[v], wp_ref[...], preferred_element_type=jnp.float32
        )
        for i in range(2):
            to = 2 * v + i
            mine[to] = part[i * count : (i + 1) * count].astype(bf)
            made = make(mine.at[to], arrived.at[h], 82 + to, {"head": to}, 82 + h)
            first_sent.append(made)

            @pl.when(h != to)
            def _():
                made.start()

            @pl.when(h == to)
            def _():
                arrived[h] = mine[to]

    for k in range(n):
        @pl.when(h != k)
        def _():
            make(mine.at[k], arrived.at[k], 82 + k, {"head": k}).wait_recv()

    total = arrived[0].astype(jnp.float32)
    for k in range(1, n):
        total = total + arrived[k].astype(jnp.float32)
    feats[0] = total[:, :C].astype(bf)
    feats[1] = total[:, C:].astype(bf)
    rows_buf[h] = feats[0]
    for k in range(n):
        to = lax.rem(c + k, n)

        @pl.when(jnp.logical_or(c != h, k != 0))
        def _():
            make(feats.at[1], cols_buf.at[h], 98 + k, {"ctx": to, "head": c}, 98 + h).start()

        @pl.when(jnp.logical_and(c == h, k == 0))
        def _():
            cols_buf[h] = feats[1]

    for k in range(1, n):
        make(feats.at[0], rows_buf.at[h], 90 + k, {"head": lax.rem(h + k, n)}).start()
    for ring in (ring_b0, ring_b1, ring_m, ring_p, ring_k0, ring_k1, ring_o):
        ring.drain()
    for made in shared + asked:
        made.wait_send()
    for k, made in enumerate(first_sent):
        @pl.when(h != k)
        def _():
            made.wait_send()

    for k in range(1, n):
        source = lax.rem(h + n - k, n)
        made = make(feats.at[0], rows_buf.at[source], 90 + k, {"head": lax.rem(h + k, n)})
        made.wait_recv()
        made.wait_send()
    for k in range(n):
        @pl.when(jnp.logical_or(c != h, k != h))
        def _():
            make(feats.at[1], cols_buf.at[k], 98 + k, {"head": lax.rem(h + 1, n)}).wait_recv()

        @pl.when(jnp.logical_or(c != h, k != 0))
        def _():
            make(feats.at[1], cols_buf.at[h], 98 + k, {"head": lax.rem(h + 1, n)}).wait_send()
    row_out[...] = rows_buf[...]
    col_out[...] = cols_buf[...]


def features(sequence, deletions, conv_taps, conv_bias, w_proj, w_out, w_pair):
    tokens, width = sequence.shape
    variants = deletions.shape[0]
    n = 8
    share = SEGS * DEL // 2
    vm = pl.BlockSpec(memory_space=pltpu.VMEM)
    bf, f32 = jnp.bfloat16, jnp.float32
    part = variants * tokens // POOL // n
    scratch = [
        ((width, DIL), bf),
        ((width, DIL), bf),
        ((4, width, 128), f32),
        ((n, width, DIL), bf),
        ((n, width, DIL), bf),
        ((n, share * 3 // 2, 128), bf),
        ((n, width, 2 * C), bf),
        ((n, width, 2 * DEL), bf),
        ((n - 1, width, 2 * DEL), bf),
        ((n * width, 256), bf),
        ((n, DIL * 5 // 2, 128), bf),
        ((n, DIL * 5 // 2, 128), bf),
        ((n, share, 128), bf),
        ((n, share * 5 // 2, 128), bf),
        ((tokens, HD), bf),
        ((variants, tokens, 256), bf),
        ((variants, tokens, 128), f32),
        ((variants, tokens, 256), f32),
        ((tokens, 256), bf),
        ((tokens, 256), bf),
        ((variants, tokens // POOL, width), bf),
        ((w_out.shape[0], 2 * C), bf),
        ((n, part, 2 * C), bf),
        ((n, part, 2 * C), bf),
        ((n, part, C), bf),
        ((n, part, C), bf),
        ((2, part, C), bf),
    ]
    return pl.pallas_call(
        features_kernel,
        out_shape=(jax.ShapeDtypeStruct((n, part, C), bf),) * 2,
        in_specs=[pl.BlockSpec(memory_space=pltpu.SMEM)] + [vm] * 6,
        out_specs=(vm, vm),
        scratch_shapes=[pltpu.VMEM(shape, kind) for shape, kind in scratch]
        + [pltpu.SemaphoreType.DMA((106,)), pltpu.SemaphoreType.DMA((106,))],
        compiler_params=pltpu.CompilerParams(
            collective_id=0, has_side_effects=True, vmem_limit_bytes=56 * 2**20
        ),
    )(deletions.T, sequence.T, conv_taps, conv_bias.reshape(1, width), w_proj.T, w_out, w_pair)


def local(sequence, deletions, conv_taps, conv_bias, w_proj, w_out, w_pair, dist_table):
    variants = deletions.shape[0]
    row_feats, col_feats = features(sequence, deletions, conv_taps, conv_bias, w_proj, w_out, w_pair)
    shape = (variants, sequence.shape[0] // POOL, C)
    return pair_map(row_feats.reshape(shape), col_feats.reshape(shape), dist_table)


def solution(mesh):
    in_specs = (
        P("ctx", "head"),
        P("var", None),
        P(None, "head"),
        P("head"),
        P(None, "head"),
        P("head", None),
        P("head", None),
        P(),
    )
    out_specs = P("var", "ctx", "head", None)
    return jax.shard_map(local, mesh=mesh, in_specs=in_specs, out_specs=out_specs, check_vma=False)
```

```python
import functools
import math

import jax
import jax.numpy as jnp
from jax import lax
from jax.experimental import pallas as pl
from jax.experimental.pallas import tpu as pltpu
from jax.sharding import PartitionSpec as P

HD = 128
VD = 192
C = 128
NB = 16
POOL = 4
DIL = 256
DEL = 128
SEGS = 3
BIG = -1e30
QSCALE = math.log2(math.e) / math.sqrt(HD)


def changed(delta, length):
    hit = jnp.logical_and(delta >= 0, delta < length)
    for shift in (-DIL, DIL):
        moved = delta + shift
        hit = jnp.logical_or(hit, jnp.logical_and(moved >= 0, moved < length))
    return hit


def pair_kernel(per, row_ref, col_ref, table_ref, out_ref, rel, rows, cols, made, sem):
    span = col_ref.shape[1]
    row_count = row_ref.shape[1]
    base = lax.axis_index("head") * span - lax.axis_index("ctx") * row_count - (row_count - 1)
    dist = jnp.abs(lax.broadcasted_iota(jnp.int32, rel.shape, 0) + base)
    value = jnp.broadcast_to(table_ref[0:1, :], rel.shape)
    for k in range(NB - 1):
        value = jnp.where(dist >= 2**k, table_ref[k + 1 : k + 2, :], value)
    rel[...] = value
    rows[...] = row_ref[...].astype(jnp.float32)
    cols[...] = col_ref[...].astype(jnp.float32)

    def copy(group):
        at = pl.ds(pl.multiple_of(group * per, per), per)
        return pltpu.make_async_copy(made.at[:, at], out_ref.at[:, at], sem.at[group])

    def one_group(group, _):
        def one(i, _):
            row = group * per + i
            shifted = rel[pl.ds(row_count - 1 - row, span), :]
            for v in range(row_ref.shape[0]):
                made[v, row] = (rows[v, pl.ds(row, 1), :] + (cols[v] + shifted)).astype(made.dtype)
            return 0

        lax.fori_loop(0, per, one, 0, unroll=4)
        copy(group).start()
        return 0

    def done(group, _):
        copy(group).wait()
        return 0

    lax.fori_loop(0, row_count // per, one_group, 0)
    lax.fori_loop(0, row_count // per, done, 0)


def pair_map(row_feats, col_feats, table):
    variants, rows, _ = row_feats.shape
    cols = col_feats.shape[1]
    per = 8
    vm = pl.BlockSpec(memory_space=pltpu.VMEM)
    shape = (variants, rows, cols, C)
    return pl.pallas_call(
        functools.partial(pair_kernel, per),
        out_shape=jax.ShapeDtypeStruct(shape, jnp.bfloat16),
        in_specs=[vm, vm, vm],
        out_specs=pl.BlockSpec(memory_space=pl.ANY),
        scratch_shapes=[
            pltpu.VMEM((rows + cols, C), jnp.float32),
            pltpu.VMEM((variants, rows, C), jnp.float32),
            pltpu.VMEM((variants, cols, C), jnp.float32),
            pltpu.VMEM(shape, jnp.bfloat16),
            pltpu.SemaphoreType.DMA((rows // per,)),
        ],
        compiler_params=pltpu.CompilerParams(vmem_limit_bytes=60 * 2**20),
    )(row_feats, col_feats, table)


MESH = pl.DeviceIdType.MESH


def pack(x):
    half = x.shape[0] // 2
    tail = jnp.concatenate([x[:half, 128:], x[half:, 128:]], axis=1)
    return jnp.concatenate([x[:, :128], tail], axis=0)


class Ring:
    def __init__(self, make, buf, rows, base, me, dn, up, far, mate, mate_of, to_dn, to_up, to_mate):
        half = rows // 2
        self.full, self.lo, self.hi = pl.ds(0, rows), pl.ds(0, half), pl.ds(half, half)
        self.make, self.buf, self.base = make, buf, base
        self.me, self.dn, self.up, self.far, self.mate, self.mate_of = me, dn, up, far, mate, mate_of
        self.to_dn, self.to_up, self.to_mate = to_dn, to_up, to_mate
        self.sent = []

    def copy(self, slot, rows, index, target):
        ref = self.buf.at[slot, rows]
        return self.make(ref, ref, self.base + index, target)

    def send(self, slot, rows, index, target):
        made = self.copy(slot, rows, index, target)
        made.start()
        self.sent.append(made)

    def got(self, slot, rows, index):
        self.copy(slot, rows, index, self.to_up).wait_recv()


class HeadRing(Ring):
    def begin(self):
        self.send(self.me, self.full, 0, self.to_up)
        self.send(self.me, self.full, 1, self.to_dn)
        self.send(self.me, self.full, 2, self.to_mate)

    def relay(self):
        self.got(self.dn, self.full, 0)
        self.send(self.dn, self.lo, 3, self.to_up)
        self.send(self.dn, self.full, 4, self.to_mate)
        self.got(self.up, self.full, 1)
        self.send(self.up, self.hi, 5, self.to_dn)
        self.send(self.up, self.full, 6, self.to_mate)

    def end(self):
        self.got(self.far, self.lo, 3)
        self.send(self.far, self.lo, 7, self.to_mate)
        self.got(self.far, self.hi, 5)
        self.send(self.far, self.hi, 8, self.to_mate)
        self.got(self.mate, self.full, 2)
        self.got(self.mate_of(self.dn), self.full, 4)
        self.got(self.mate_of(self.up), self.full, 6)
        self.got(self.mate_of(self.far), self.lo, 7)
        self.got(self.mate_of(self.far), self.hi, 8)

    def drain(self):
        for made in self.sent:
            made.wait_send()


class TokenRing(Ring):
    def begin(self):
        self.send(self.me, self.full, 2, self.to_mate)
        self.send(self.me, self.full, 0, self.to_up)
        self.send(self.me, self.full, 1, self.to_dn)

    def cross(self):
        self.got(self.mate, self.full, 2)
        self.send(self.mate, self.full, 4, self.to_up)
        self.send(self.mate, self.full, 6, self.to_dn)

    def relay(self):
        self.got(self.dn, self.full, 0)
        self.send(self.dn, self.lo, 3, self.to_up)
        self.got(self.up, self.full, 1)
        self.send(self.up, self.hi, 5, self.to_dn)

    def far_block(self):
        self.got(self.far, self.lo, 3)
        self.send(self.far, self.lo, 7, self.to_mate)
        self.got(self.far, self.hi, 5)
        self.send(self.far, self.hi, 8, self.to_mate)

    def end(self):
        self.got(self.mate_of(self.dn), self.full, 4)
        self.got(self.mate_of(self.up), self.full, 6)
        self.got(self.mate_of(self.far), self.lo, 7)
        self.got(self.mate_of(self.far), self.hi, 8)

    def drain(self):
        for made in self.sent:
            made.wait_send()


def swap_lanes(x):
    return jnp.concatenate([x[:, 64:], x[:, :64]], axis=1)


def unpack_tail(tail, fill):
    both = jnp.concatenate([tail, swap_lanes(tail)], axis=0)
    keep = lax.broadcasted_iota(jnp.int32, both.shape, 1) < 64
    return jnp.where(keep, both, jnp.broadcast_to(fill, both.shape))


def features_kernel(dels, seq, taps, bias, w_ref, wo_ref, wp_ref, row_out, col_out,
                    low, high, cols, gb0, gb1, gm, wp, moved, landed, flat, kv0, kv1, mq, mkv,
                    queries, q_aug, top, acc, ka, va, pooled, mix, mine, arrived, rows_buf, cols_buf, feats,
                    send, recv):
    width, tokens = seq.shape
    variants = dels.shape[1]
    share = SEGS * DEL // 2
    per = 2 * share
    n = 8
    bf = jnp.bfloat16
    c, h, g = lax.axis_index("ctx"), lax.axis_index("head"), lax.axis_index("var")
    dn_h, up_h, far_h = lax.rem(h + 6, n), lax.rem(h + 2, n), lax.rem(h + 4, n)
    sib = h + 1 - 2 * lax.rem(h, 2)
    x0, y0 = c // 4 * 4, lax.rem(c, 4)
    up_c, dn_c, far_c = x0 + lax.rem(y0 + 1, 4), x0 + lax.rem(y0 + 3, 4), x0 + lax.rem(y0 + 2, 4)
    other = lambda t: lax.rem(t + 4, n)
    xp = other(c)
    sib_of = lambda t: t + 1 - 2 * lax.rem(t, 2)

    barrier = pltpu.get_barrier_semaphore()
    peers = [{"ctx": lax.rem(c + k, n)} for k in range(1, n)]
    peers += [{"head": lax.rem(h + k, n)} for k in range(1, n)]
    peers += [{"ctx": xp, "var": 1 - g}]
    for peer in peers:
        pl.semaphore_signal(barrier, inc=1, device_id=peer, device_id_type=MESH)
    for k in range(n):
        source = lax.rem(h + k, n)

        @pl.when(jnp.logical_or(c != h, k != 0))
        def _():
            pl.semaphore_signal(barrier, inc=1, device_id={"ctx": h, "head": source}, device_id_type=MESH)

    for k in range(4):
        line = bias[...] if k == 3 else taps[k : k + 1, :]
        cols[k] = jnp.broadcast_to(line, (128, width)).T
    wp[h] = wp_ref[...]
    run = DEL // 2
    r = lax.broadcasted_iota(jnp.int32, (tokens, 4 * run), 1)
    offset = (r // run - 2) * DIL + (r // (2 * run)) * DIL + r % run
    local_token = lax.broadcasted_iota(jnp.int32, (tokens, 4 * run), 0) + c * tokens - offset

    def gather_runs(v, _):
        for half in range(2):
            pick = (local_token == dels[0, v] + half * run).astype(bf)
            moved[2 * v + half] = jnp.dot(seq[...], pick, preferred_element_type=jnp.float32).astype(bf)
        return 0

    lax.fori_loop(0, variants, gather_runs, 0)
    pl.semaphore_wait(barrier, len(peers) + n - (c == h).astype(jnp.int32))

    def make(src, dst, index, target, arrival=None):
        return pltpu.make_async_remote_copy(
            src_ref=src, dst_ref=dst, send_sem=send.at[index],
            recv_sem=recv.at[index if arrival is None else arrival],
            device_id=(target.get("ctx", c), target.get("head", h), target.get("var", g)), device_id_type=MESH,
        )

    halo_low = make(seq.at[:, pl.ds(tokens - DIL, DIL)], low, 0, {"ctx": lax.rem(c + 1, n)})
    halo_high = make(seq.at[:, pl.ds(0, DIL)], high, 1, {"ctx": lax.rem(c + 7, n)})
    halo_low.start()
    halo_high.start()
    shared = []
    for k in (4, 3, 5, 2, 6, 1, 7):
        to = lax.rem(c + k, n)
        made = make(moved.at[to], landed.at[k - 1], 1 + k, {"ctx": to})
        made.start()
        shared.append(made)

    def head_ring(buf, base):
        return HeadRing(make, buf, buf.shape[1], base, h, dn_h, up_h, far_h, sib, sib_of,
                        {"head": dn_h}, {"head": up_h}, {"head": sib})

    def token_ring(buf, base, to_mate):
        return TokenRing(make, buf, buf.shape[1], base, c, dn_c, up_c, far_c, xp, other,
                         {"ctx": dn_c}, {"ctx": up_c}, to_mate)

    ring_b0, ring_b1, ring_m, ring_p = (head_ring(buf, 10 + 9 * i) for i, buf in enumerate((gb0, gb1, gm, wp)))
    cross = {"ctx": xp, "var": 1 - g}
    ring_k0, ring_k1 = token_ring(kv0, 46, cross), token_ring(kv1, 55, cross)
    ring_o = token_ring(mkv, 73, {"ctx": xp})

    at = lax.broadcasted_iota(jnp.int32, (1, DIL), 1) + c * tokens
    wide = lambda k: jnp.concatenate([cols[k], cols[k]], axis=1)

    def trunk(half, first, length):
        def kept(x, shift, inside=None):
            d = at + (half * DIL + shift) - first
            keep = jnp.logical_or(d < 0, d >= length)
            if inside is not None:
                keep = jnp.logical_and(keep, inside)
            return jnp.where(keep, x.astype(jnp.float32), 0.0)

        here = kept(seq[:, half * DIL : (half + 1) * DIL], 0)
        if half == 0:
            before, after = kept(low[...], -DIL, c != 0), kept(seq[:, DIL:], DIL)
        else:
            before, after = kept(seq[:, :DIL], -DIL), kept(high[...], DIL, c != n - 1)
        conv = wide(0) * before + wide(1) * here + wide(2) * after + wide(3)
        return (here + jax.nn.gelu(conv, approximate=True)).astype(bf)

    ring_p.begin()
    ring_p.relay()
    halo_low.wait()
    gb0[h] = trunk(0, 0, 0)
    ring_b0.begin()
    halo_high.wait()
    gb1[h] = trunk(1, 0, 0)
    ring_b1.begin()

    pool = (
        lax.broadcasted_iota(jnp.int32, (tokens // POOL, tokens), 1) // POOL
        == lax.broadcasted_iota(jnp.int32, (tokens // POOL, tokens), 0)
    ).astype(bf)

    def project(x):
        return jnp.dot(w_ref[...], x, preferred_element_type=jnp.float32).T

    def place(kv, x, count):
        kv[c, :count] = x[:count, HD : 2 * HD].astype(bf)
        kv[c, count:] = pack(x[:count, 2 * HD :].astype(bf))

    ring_p.end()
    ring_b0.relay()
    ring_b1.relay()
    ring_b0.end()
    x = project(gb0[...].reshape(n * width, DIL))
    place(kv0, x, DIL)
    ring_k0.begin()
    queries[:DIL] = (x[:, :HD] * QSCALE).astype(bf)
    ring_b1.end()
    x = project(gb1[...].reshape(n * width, DIL))
    place(kv1, x, DIL)
    ring_k1.begin()
    queries[DIL:] = (x[:, :HD] * QSCALE).astype(bf)

    total = moved[c].astype(jnp.float32)
    for made in shared:
        made.wait_recv()
    for k in range(1, n):
        total = total + landed[k - 1].astype(jnp.float32)
    runs = [total[:, i * run : (i + 1) * run] for i in range(4)]
    nil = jnp.zeros((width, run), jnp.float32)
    t0, t1, t2, t3 = (cols[k, :, :run] for k in range(4))
    made_rows = []
    for before, here, after in ((runs[0], runs[1], nil), (runs[1], nil, runs[2]), (nil, runs[2], runs[3])):
        conv = t0 * before + t1 * here + t2 * after + t3
        made_rows.append((here + jax.nn.gelu(conv, approximate=True)).astype(bf))
    tail = made_rows[2]
    gm[h, :width] = jnp.concatenate(made_rows[:2], axis=1)
    gm[h, width:] = jnp.concatenate([tail[: width // 2], tail[width // 2 :]], axis=1)
    ring_m.begin()
    ring_k0.cross()
    ring_k0.relay()
    ring_m.relay()
    ring_m.end()
    zero = jnp.zeros((1, 128), bf)
    for k in range(n):
        flat[k * width : (k + 1) * width, :128] = gm[k, :width]
        flat[k * width : (k + 1) * width, 128:] = unpack_tail(gm[k, width:], zero)
    x = project(flat[...])
    mq[c] = (x[:share, :HD] * QSCALE).astype(bf)
    asked = []
    for k in (4, 3, 5, 2, 6, 1, 7):
        made = make(mq.at[c], mq.at[c], 64 + k, {"ctx": lax.rem(c + k, n)})
        made.start()
        asked.append(made)
    place(mkv, x, share)
    ring_o.begin()
    ring_k1.cross()
    ring_k1.relay()

    def variant(v, _):
        first = dels[0, v]
        length = dels[1, v] - first
        own = jnp.concatenate([trunk(0, first, length), trunk(1, first, length)], axis=1)
        mean = lax.dot_general(pool, own, (((1,), (1,)), ((), ())), preferred_element_type=jnp.float32)
        pooled[v] = (mean * (1.0 / POOL)).astype(bf)
        return 0

    lax.fori_loop(0, variants, variant, 0)
    total = jnp.zeros((wo_ref.shape[0], 2 * C), jnp.float32)
    for k in range(0, n, 2):
        two = jnp.concatenate([wp[k], wp[k + 1]], axis=0)
        total = total + jnp.dot(wo_ref[:, k * width : (k + 2) * width], two, preferred_element_type=jnp.float32)
    mix[...] = total.astype(bf)
    ring_k0.far_block()
    for k in range(1, n):
        source = lax.rem(c + n - k, n)
        make(mq.at[source], mq.at[source], 64 + k, {"ctx": lax.rem(c + k, n)}).wait_recv()

    lane = lax.broadcasted_iota(jnp.int32, (1, 128), 1)
    first = jnp.zeros((1, 128), jnp.int32)
    length = jnp.zeros((1, 128), jnp.int32)
    for v in range(variants):
        first = jnp.where(lane == v, dels[0, v], first)
        length = jnp.where(lane == v, dels[1, v] - dels[0, v], length)
    col = lax.broadcasted_iota(jnp.int32, (tokens, per), 1)
    col_step = col // share * (DEL // 2) + col % (DEL // 2)
    col_offset = (col % share // (DEL // 2) - 1) * DIL + col_step
    qpos = lax.broadcasted_iota(jnp.int32, (tokens, per), 0) + c * tokens

    def aim(v, _):
        s0 = dels[0, v]
        count = dels[1, v] - s0
        spot = jnp.logical_and(qpos - col_offset == s0, col_step < count).astype(bf)
        source = jnp.concatenate([mq[2 * v], mq[2 * v + 1]], axis=0)
        moved_q = jnp.dot(spot, source, preferred_element_type=jnp.float32)
        is_mod = changed(qpos[:, :128] - s0, count)
        q_aug[v, :, :HD] = jnp.where(is_mod, moved_q, queries[...].astype(jnp.float32)).astype(bf)
        q_aug[v, :, HD:] = jnp.broadcast_to(jnp.where(lane == v, 1.0, 0.0), (tokens, 128)).astype(bf)
        top[v] = jnp.full((tokens, 128), -3e38, jnp.float32)
        acc[v] = jnp.zeros((tokens, 256), jnp.float32)
        return 0

    lax.fori_loop(0, variants, aim, 0)
    ones = jnp.where(lane == VD - 128, 1.0, 0.0).astype(bf)

    def unit(v, keys, values):
        s = lax.dot_general(q_aug[v], keys, (((1,), (1,)), ((), ())), preferred_element_type=jnp.float32)
        old = top[v]
        new = jnp.maximum(old, jnp.broadcast_to(s.max(1, keepdims=True), old.shape))
        w = jnp.exp2(s - jnp.concatenate([new] * (keys.shape[0] // 128), axis=1)).astype(bf)
        shrink = jnp.exp2(old - new)
        top[v] = new
        acc[v] = acc[v] * jnp.concatenate([shrink, shrink], axis=1) + jnp.dot(
            w, values, preferred_element_type=jnp.float32
        )

    def attend(step, _):
        look = lambda table: sum((step == i).astype(jnp.int32) * t for i, t in enumerate(table) if t)
        away = look((0, 3, 1, 0, 2, 3, 1, 2))
        across = look((0, 0, 0, 1, 0, 1, 1, 1))
        side = x0 + across * (4 - 2 * x0)
        block = side + lax.rem(y0 + away, 4)
        for i, kv in enumerate((kv0, kv1)):
            rows = slice(i * DIL, (i + 1) * DIL)
            ka[rows, :HD] = kv[block, :DIL]
            pos = lax.broadcasted_iota(jnp.int32, (DIL, 128), 0) + (block * tokens + i * DIL)
            ka[rows, HD:] = jnp.where(changed(pos - first, length), BIG, 0.0).astype(bf)
            va[rows, :128] = kv[block, DIL : 2 * DIL]
            va[rows, 128:] = unpack_tail(kv[block, 2 * DIL :], ones)
        for v in range(variants):
            unit(v, ka[...], va[...])
        return 0

    lax.fori_loop(0, 2, attend, 0)
    ring_k1.far_block()
    ring_o.cross()
    ring_o.relay()
    lax.fori_loop(2, 5, attend, 0)
    ring_k0.end()
    ring_k1.end()
    ring_o.far_block()
    lax.fori_loop(5, n, attend, 0)
    ring_o.end()

    row = lax.broadcasted_iota(jnp.int32, (per, 128), 0)
    step = row // share * (DEL // 2) + row % (DEL // 2)
    row_offset = (row % share // (DEL // 2) - 1) * DIL + step
    count = tokens // POOL // 2
    first_sent = []
    for v in range(variants):
        token = dels[0, v] + row_offset
        valid = (step < dels[1, v] - dels[0, v]) & (token >= 0) & (token < n * tokens)
        ka[:per, HD:] = jnp.where(valid, 0.0, BIG).astype(bf)
        for i in range(2):
            rows = slice(i * share, (i + 1) * share)
            ka[rows, :HD] = mkv[2 * v + i, :share]
            va[rows, :128] = mkv[2 * v + i, share : 2 * share]
            va[rows, 128:] = unpack_tail(mkv[2 * v + i, 2 * share :], ones)
        unit(v, ka[:per], va[:per])
        out = (acc[v, :, :VD] / acc[v, :, VD : VD + 1]).astype(bf)
        mean = jnp.dot(pool, out, preferred_element_type=jnp.float32) * (1.0 / POOL)
        part = jnp.dot(mean.astype(bf), mix[...], preferred_element_type=jnp.float32) + jnp.dot(
            pooled[v], wp_ref[...], preferred_element_type=jnp.float32
        )
        for i in range(2):
            to = 2 * v + i
            mine[to] = part[i * count : (i + 1) * count].astype(bf)
            made = make(mine.at[to], arrived.at[h], 82 + to, {"head": to}, 82 + h)
            first_sent.append(made)

            @pl.when(h != to)
            def _():
                made.start()

            @pl.when(h == to)
            def _():
                arrived[h] = mine[to]

    for k in range(n):
        @pl.when(h != k)
        def _():
            make(mine.at[k], arrived.at[k], 82 + k, {"head": k}).wait_recv()

    total = arrived[0].astype(jnp.float32)
    for k in range(1, n):
        total = total + arrived[k].astype(jnp.float32)
    feats[0] = total[:, :C].astype(bf)
    feats[1] = total[:, C:].astype(bf)
    rows_buf[h] = feats[0]
    for k in range(n):
        to = lax.rem(c + k, n)

        @pl.when(jnp.logical_or(c != h, k != 0))
        def _():
            make(feats.at[1], cols_buf.at[h], 98 + k, {"ctx": to, "head": c}, 98 + h).start()

        @pl.when(jnp.logical_and(c == h, k == 0))
        def _():
            cols_buf[h] = feats[1]

    for k in range(1, n):
        make(feats.at[0], rows_buf.at[h], 90 + k, {"head": lax.rem(h + k, n)}).start()
    for ring in (ring_b0, ring_b1, ring_m, ring_p, ring_k0, ring_k1, ring_o):
        ring.drain()
    for made in shared + asked:
        made.wait_send()
    for k, made in enumerate(first_sent):
        @pl.when(h != k)
        def _():
            made.wait_send()

    for k in range(1, n):
        source = lax.rem(h + n - k, n)
        made = make(feats.at[0], rows_buf.at[source], 90 + k, {"head": lax.rem(h + k, n)})
        made.wait_recv()
        made.wait_send()
    for k in range(n):
        @pl.when(jnp.logical_or(c != h, k != h))
        def _():
            make(feats.at[1], cols_buf.at[k], 98 + k, {"head": lax.rem(h + 1, n)}).wait_recv()

        @pl.when(jnp.logical_or(c != h, k != 0))
        def _():
            make(feats.at[1], cols_buf.at[h], 98 + k, {"head": lax.rem(h + 1, n)}).wait_send()
    row_out[...] = rows_buf[...]
    col_out[...] = cols_buf[...]


def features(sequence, deletions, conv_taps, conv_bias, w_proj, w_out, w_pair):
    tokens, width = sequence.shape
    variants = deletions.shape[0]
    n = 8
    share = SEGS * DEL // 2
    vm = pl.BlockSpec(memory_space=pltpu.VMEM)
    bf, f32 = jnp.bfloat16, jnp.float32
    part = variants * tokens // POOL // n
    scratch = [
        ((width, DIL), bf),
        ((width, DIL), bf),
        ((4, width, 128), f32),
        ((n, width, DIL), bf),
        ((n, width, DIL), bf),
        ((n, share * 3 // 2, 128), bf),
        ((n, width, 2 * C), bf),
        ((n, width, 2 * DEL), bf),
        ((n - 1, width, 2 * DEL), bf),
        ((n * width, 256), bf),
        ((n, DIL * 5 // 2, 128), bf),
        ((n, DIL * 5 // 2, 128), bf),
        ((n, share, 128), bf),
        ((n, share * 5 // 2, 128), bf),
        ((tokens, HD), bf),
        ((variants, tokens, 256), bf),
        ((variants, tokens, 128), f32),
        ((variants, tokens, 256), f32),
        ((tokens, 256), bf),
        ((tokens, 256), bf),
        ((variants, tokens // POOL, width), bf),
        ((w_out.shape[0], 2 * C), bf),
        ((n, part, 2 * C), bf),
        ((n, part, 2 * C), bf),
        ((n, part, C), bf),
        ((n, part, C), bf),
        ((2, part, C), bf),
    ]
    return pl.pallas_call(
        features_kernel,
        out_shape=(jax.ShapeDtypeStruct((n, part, C), bf),) * 2,
        in_specs=[pl.BlockSpec(memory_space=pltpu.SMEM)] + [vm] * 6,
        out_specs=(vm, vm),
        scratch_shapes=[pltpu.VMEM(shape, kind) for shape, kind in scratch]
        + [pltpu.SemaphoreType.DMA((106,)), pltpu.SemaphoreType.DMA((106,))],
        compiler_params=pltpu.CompilerParams(
            collective_id=0, has_side_effects=True, vmem_limit_bytes=56 * 2**20
        ),
    )(deletions.T, sequence.T, conv_taps, conv_bias.reshape(1, width), w_proj.T, w_out, w_pair)


def local(sequence, deletions, conv_taps, conv_bias, w_proj, w_out, w_pair, dist_table):
    variants = deletions.shape[0]
    row_feats, col_feats = features(sequence, deletions, conv_taps, conv_bias, w_proj, w_out, w_pair)
    shape = (variants, sequence.shape[0] // POOL, C)
    return pair_map(row_feats.reshape(shape), col_feats.reshape(shape), dist_table)


def solution(mesh):
    in_specs = (
        P("ctx", "head"),
        P("var", None),
        P(None, "head"),
        P("head"),
        P(None, "head"),
        P("head", None),
        P("head", None),
        P(),
    )
    out_specs = P("var", "ctx", "head", None)
    return jax.shard_map(local, mesh=mesh, in_specs=in_specs, out_specs=out_specs, check_vma=False)
```

```python
import functools
import math

import jax
import jax.numpy as jnp
from jax import lax
from jax.experimental import pallas as pl
from jax.experimental.pallas import tpu as pltpu
from jax.sharding import PartitionSpec as P

HD = 128
VD = 192
C = 128
NB = 16
POOL = 4
DIL = 256
DEL = 128
SEGS = 3
BIG = -1e30
QSCALE = math.log2(math.e) / math.sqrt(HD)


def changed(delta, length):
    hit = jnp.logical_and(delta >= 0, delta < length)
    for shift in (-DIL, DIL):
        moved = delta + shift
        hit = jnp.logical_or(hit, jnp.logical_and(moved >= 0, moved < length))
    return hit


def pair_kernel(per, row_ref, col_ref, table_ref, out_ref, rel, rows, cols, made, sem):
    span = col_ref.shape[1]
    row_count = row_ref.shape[1]
    base = lax.axis_index("head") * span - lax.axis_index("ctx") * row_count - (row_count - 1)
    dist = jnp.abs(lax.broadcasted_iota(jnp.int32, rel.shape, 0) + base)
    value = jnp.broadcast_to(table_ref[0:1, :], rel.shape)
    for k in range(NB - 1):
        value = jnp.where(dist >= 2**k, table_ref[k + 1 : k + 2, :], value)
    rel[...] = value
    rows[...] = row_ref[...].astype(jnp.float32)
    cols[...] = col_ref[...].astype(jnp.float32)

    def copy(group):
        at = pl.ds(pl.multiple_of(group * per, per), per)
        return pltpu.make_async_copy(made.at[:, at], out_ref.at[:, at], sem.at[group])

    def one_group(group, _):
        def one(i, _):
            row = group * per + i
            shifted = rel[pl.ds(row_count - 1 - row, span), :]
            for v in range(row_ref.shape[0]):
                made[v, row] = (rows[v, pl.ds(row, 1), :] + (cols[v] + shifted)).astype(made.dtype)
            return 0

        lax.fori_loop(0, per, one, 0, unroll=4)
        copy(group).start()
        return 0

    def done(group, _):
        copy(group).wait()
        return 0

    lax.fori_loop(0, row_count // per, one_group, 0)
    lax.fori_loop(0, row_count // per, done, 0)


def pair_map(row_feats, col_feats, table):
    variants, rows, _ = row_feats.shape
    cols = col_feats.shape[1]
    per = 8
    vm = pl.BlockSpec(memory_space=pltpu.VMEM)
    shape = (variants, rows, cols, C)
    return pl.pallas_call(
        functools.partial(pair_kernel, per),
        out_shape=jax.ShapeDtypeStruct(shape, jnp.bfloat16),
        in_specs=[vm, vm, vm],
        out_specs=pl.BlockSpec(memory_space=pl.ANY),
        scratch_shapes=[
            pltpu.VMEM((rows + cols, C), jnp.float32),
            pltpu.VMEM((variants, rows, C), jnp.float32),
            pltpu.VMEM((variants, cols, C), jnp.float32),
            pltpu.VMEM(shape, jnp.bfloat16),
            pltpu.SemaphoreType.DMA((rows // per,)),
        ],
        compiler_params=pltpu.CompilerParams(vmem_limit_bytes=60 * 2**20),
    )(row_feats, col_feats, table)


MESH = pl.DeviceIdType.MESH


def pack(x):
    half = x.shape[0] // 2
    tail = jnp.concatenate([x[:half, 128:], x[half:, 128:]], axis=1)
    return jnp.concatenate([x[:, :128], tail], axis=0)


class Ring:
    def __init__(self, make, buf, rows, base, me, dn, up, far, mate, mate_of, to_dn, to_up, to_mate):
        half = rows // 2
        self.full, self.lo, self.hi = pl.ds(0, rows), pl.ds(0, half), pl.ds(half, half)
        self.make, self.buf, self.base = make, buf, base
        self.me, self.dn, self.up, self.far, self.mate, self.mate_of = me, dn, up, far, mate, mate_of
        self.to_dn, self.to_up, self.to_mate = to_dn, to_up, to_mate
        self.sent = []

    def copy(self, slot, rows, index, target):
        ref = self.buf.at[slot, rows]
        return self.make(ref, ref, self.base + index, target)

    def send(self, slot, rows, index, target):
        made = self.copy(slot, rows, index, target)
        made.start()
        self.sent.append(made)

    def got(self, slot, rows, index):
        self.copy(slot, rows, index, self.to_up).wait_recv()


class HeadRing(Ring):
    def begin(self):
        self.send(self.me, self.full, 0, self.to_up)
        self.send(self.me, self.full, 1, self.to_dn)
        self.send(self.me, self.full, 2, self.to_mate)

    def relay(self):
        self.got(self.dn, self.full, 0)
        self.send(self.dn, self.lo, 3, self.to_up)
        self.send(self.dn, self.full, 4, self.to_mate)
        self.got(self.up, self.full, 1)
        self.send(self.up, self.hi, 5, self.to_dn)
        self.send(self.up, self.full, 6, self.to_mate)

    def end(self):
        self.got(self.far, self.lo, 3)
        self.send(self.far, self.lo, 7, self.to_mate)
        self.got(self.far, self.hi, 5)
        self.send(self.far, self.hi, 8, self.to_mate)
        self.got(self.mate, self.full, 2)
        self.got(self.mate_of(self.dn), self.full, 4)
        self.got(self.mate_of(self.up), self.full, 6)
        self.got(self.mate_of(self.far), self.lo, 7)
        self.got(self.mate_of(self.far), self.hi, 8)

    def drain(self):
        for made in self.sent:
            made.wait_send()


class TokenRing(Ring):
    near_only = False

    def begin(self):
        self.send(self.me, self.full, 2, self.to_mate)
        self.send(self.me, self.full, 0, self.to_up)
        self.send(self.me, self.full, 1, self.to_dn)

    def cross(self):
        self.got(self.mate, self.full, 2)
        self.send(self.mate, self.full, 4, self.to_up)
        self.send(self.mate, self.full, 6, self.to_dn)

    def relay(self):
        self.got(self.dn, self.full, 0)
        self.send(self.dn, self.lo, 3, self.to_up)
        self.got(self.up, self.full, 1)
        self.send(self.up, self.hi, 5, self.to_dn)

    def far_block(self):
        if self.near_only:
            dn, up = self.mate_of(self.dn), self.mate_of(self.up)
            self.got(dn, self.full, 4)
            self.send(dn, self.lo, 7, self.to_up)
            self.got(up, self.full, 6)
            self.send(up, self.hi, 8, self.to_dn)
            return
        self.got(self.far, self.lo, 3)
        self.send(self.far, self.lo, 7, self.to_mate)
        self.got(self.far, self.hi, 5)
        self.send(self.far, self.hi, 8, self.to_mate)

    def end(self):
        if self.near_only:
            self.got(self.far, self.lo, 3)
            self.got(self.far, self.hi, 5)
        else:
            self.got(self.mate_of(self.dn), self.full, 4)
            self.got(self.mate_of(self.up), self.full, 6)
        self.got(self.mate_of(self.far), self.lo, 7)
        self.got(self.mate_of(self.far), self.hi, 8)

    def drain(self):
        for made in self.sent:
            made.wait_send()


def swap_lanes(x):
    return jnp.concatenate([x[:, 64:], x[:, :64]], axis=1)


def unpack_tail(tail, fill):
    both = jnp.concatenate([tail, swap_lanes(tail)], axis=0)
    keep = lax.broadcasted_iota(jnp.int32, both.shape, 1) < 64
    return jnp.where(keep, both, jnp.broadcast_to(fill, both.shape))


def features_kernel(dels, seq, taps, bias, w_ref, wo_ref, wp_ref, row_out, col_out,
                    low, high, cols, gb0, gb1, gm, wp, moved, landed, flat, kv0, kv1, mq, mkv,
                    queries, q_aug, top, acc, ka, va, pooled, mix, mine, arrived, rows_buf, cols_buf, feats,
                    send, recv):
    width, tokens = seq.shape
    variants = dels.shape[1]
    share = SEGS * DEL // 2
    per = 2 * share
    n = 8
    bf = jnp.bfloat16
    c, h, g = lax.axis_index("ctx"), lax.axis_index("head"), lax.axis_index("var")
    dn_h, up_h, far_h = lax.rem(h + 6, n), lax.rem(h + 2, n), lax.rem(h + 4, n)
    sib = h + 1 - 2 * lax.rem(h, 2)
    x0, y0 = c // 4 * 4, lax.rem(c, 4)
    up_c, dn_c, far_c = x0 + lax.rem(y0 + 1, 4), x0 + lax.rem(y0 + 3, 4), x0 + lax.rem(y0 + 2, 4)
    other = lambda t: lax.rem(t + 4, n)
    xp = other(c)
    sib_of = lambda t: t + 1 - 2 * lax.rem(t, 2)

    barrier = pltpu.get_barrier_semaphore()
    peers = [{"ctx": lax.rem(c + k, n)} for k in range(1, n)]
    peers += [{"head": lax.rem(h + k, n)} for k in range(1, n)]
    peers += [{"ctx": xp, "var": 1 - g}]
    for peer in peers:
        pl.semaphore_signal(barrier, inc=1, device_id=peer, device_id_type=MESH)
    for k in range(n):
        source = lax.rem(h + k, n)

        @pl.when(jnp.logical_or(c != h, k != 0))
        def _():
            pl.semaphore_signal(barrier, inc=1, device_id={"ctx": h, "head": source}, device_id_type=MESH)

    for k in range(4):
        line = bias[...] if k == 3 else taps[k : k + 1, :]
        cols[k] = jnp.broadcast_to(line, (128, width)).T
    wp[h] = wp_ref[...]
    run = DEL // 2
    r = lax.broadcasted_iota(jnp.int32, (tokens, 4 * run), 1)
    offset = (r // run - 2) * DIL + (r // (2 * run)) * DIL + r % run
    local_token = lax.broadcasted_iota(jnp.int32, (tokens, 4 * run), 0) + c * tokens - offset

    def gather_runs(v, _):
        for half in range(2):
            pick = (local_token == dels[0, v] + half * run).astype(bf)
            moved[2 * v + half] = jnp.dot(seq[...], pick, preferred_element_type=jnp.float32).astype(bf)
        return 0

    lax.fori_loop(0, variants, gather_runs, 0)
    pl.semaphore_wait(barrier, len(peers) + n - (c == h).astype(jnp.int32))

    def make(src, dst, index, target, arrival=None):
        return pltpu.make_async_remote_copy(
            src_ref=src, dst_ref=dst, send_sem=send.at[index],
            recv_sem=recv.at[index if arrival is None else arrival],
            device_id=(target.get("ctx", c), target.get("head", h), target.get("var", g)), device_id_type=MESH,
        )

    halo_low = make(seq.at[:, pl.ds(tokens - DIL, DIL)], low, 0, {"ctx": lax.rem(c + 1, n)})
    halo_high = make(seq.at[:, pl.ds(0, DIL)], high, 1, {"ctx": lax.rem(c + 7, n)})
    halo_low.start()
    halo_high.start()
    shared = [make(moved.at[pl.ds(4 - x0, 4)], landed.at[pl.ds(0, 4)], 2, {"ctx": xp})]
    shared[0].start()

    def head_ring(buf, base):
        return HeadRing(make, buf, buf.shape[1], base, h, dn_h, up_h, far_h, sib, sib_of,
                        {"head": dn_h}, {"head": up_h}, {"head": sib})

    def token_ring(buf, base, to_mate):
        return TokenRing(make, buf, buf.shape[1], base, c, dn_c, up_c, far_c, xp, other,
                         {"ctx": dn_c}, {"ctx": up_c}, to_mate)

    ring_b0, ring_b1, ring_m, ring_p = (head_ring(buf, 10 + 9 * i) for i, buf in enumerate((gb0, gb1, gm, wp)))
    cross = {"ctx": xp, "var": 1 - g}
    ring_k0, ring_k1 = token_ring(kv0, 46, cross), token_ring(kv1, 55, cross)
    ring_o = token_ring(mkv, 73, {"ctx": xp})
    ring_o.near_only = True

    at = lax.broadcasted_iota(jnp.int32, (1, DIL), 1) + c * tokens
    wide = lambda k: jnp.concatenate([cols[k], cols[k]], axis=1)

    def trunk(half, first, length):
        def kept(x, shift, inside=None):
            d = at + (half * DIL + shift) - first
            keep = jnp.logical_or(d < 0, d >= length)
            if inside is not None:
                keep = jnp.logical_and(keep, inside)
            return jnp.where(keep, x.astype(jnp.float32), 0.0)

        here = kept(seq[:, half * DIL : (half + 1) * DIL], 0)
        if half == 0:
            before, after = kept(low[...], -DIL, c != 0), kept(seq[:, DIL:], DIL)
        else:
            before, after = kept(seq[:, :DIL], -DIL), kept(high[...], DIL, c != n - 1)
        conv = wide(0) * before + wide(1) * here + wide(2) * after + wide(3)
        return (here + jax.nn.gelu(conv, approximate=True)).astype(bf)

    ring_p.begin()
    ring_p.relay()
    halo_low.wait()
    gb0[h] = trunk(0, 0, 0)
    ring_b0.begin()
    halo_high.wait()
    gb1[h] = trunk(1, 0, 0)
    ring_b1.begin()

    pool = (
        lax.broadcasted_iota(jnp.int32, (tokens // POOL, tokens), 1) // POOL
        == lax.broadcasted_iota(jnp.int32, (tokens // POOL, tokens), 0)
    ).astype(bf)

    def project(x):
        return jnp.dot(w_ref[...], x, preferred_element_type=jnp.float32).T

    def place(kv, x, count):
        kv[c, :count] = x[:count, HD : 2 * HD].astype(bf)
        kv[c, count:] = pack(x[:count, 2 * HD :].astype(bf))

    ring_p.end()
    ring_b0.relay()
    ring_b1.relay()
    ring_b0.end()
    x = project(gb0[...].reshape(n * width, DIL))
    place(kv0, x, DIL)
    ring_k0.begin()
    shared[0].wait_recv()
    for k in range(4):
        moved[x0 + k] = moved[x0 + k] + landed[k]
    for k in (2, 1, 3):
        to = x0 + lax.rem(y0 + k, 4)
        made = make(moved.at[to], landed.at[3 + k], 2 + k, {"ctx": to})
        made.start()
        shared.append(made)
    queries[:DIL] = (x[:, :HD] * QSCALE).astype(bf)
    ring_b1.end()
    x = project(gb1[...].reshape(n * width, DIL))
    place(kv1, x, DIL)
    ring_k1.begin()
    queries[DIL:] = (x[:, :HD] * QSCALE).astype(bf)

    total = moved[c].astype(jnp.float32)
    for made in shared[1:]:
        made.wait_recv()
    for k in range(4, 7):
        total = total + landed[k].astype(jnp.float32)
    runs = [total[:, i * run : (i + 1) * run] for i in range(4)]
    nil = jnp.zeros((width, run), jnp.float32)
    t0, t1, t2, t3 = (cols[k, :, :run] for k in range(4))
    made_rows = []
    for before, here, after in ((runs[0], runs[1], nil), (runs[1], nil, runs[2]), (nil, runs[2], runs[3])):
        conv = t0 * before + t1 * here + t2 * after + t3
        made_rows.append((here + jax.nn.gelu(conv, approximate=True)).astype(bf))
    tail = made_rows[2]
    gm[h, :width] = jnp.concatenate(made_rows[:2], axis=1)
    gm[h, width:] = jnp.concatenate([tail[: width // 2], tail[width // 2 :]], axis=1)
    ring_m.begin()
    ring_k0.cross()
    ring_k0.relay()
    ring_m.relay()
    ring_m.end()
    zero = jnp.zeros((1, 128), bf)
    for k in range(n):
        flat[k * width : (k + 1) * width, :128] = gm[k, :width]
        flat[k * width : (k + 1) * width, 128:] = unpack_tail(gm[k, width:], zero)
    x = project(flat[...])
    mq[c] = (x[:share, :HD] * QSCALE).astype(bf)
    asked = []

    def hand_on(slot, index):
        for k in (2, 1, 3):
            made = make(mq.at[slot], mq.at[slot], index + k, {"ctx": x0 + lax.rem(y0 + k, 4)})
            made.start()
            asked.append(made)

    asked.append(make(mq.at[c], mq.at[c], 64, {"ctx": xp}))
    asked[0].start()
    hand_on(c, 64)
    place(mkv, x, share)
    ring_k1.cross()
    ring_k1.relay()
    make(mq.at[xp], mq.at[xp], 64, {"ctx": xp}).wait_recv()
    hand_on(xp, 67)
    ring_o.begin()

    def variant(v, _):
        first = dels[0, v]
        length = dels[1, v] - first
        own = jnp.concatenate([trunk(0, first, length), trunk(1, first, length)], axis=1)
        mean = lax.dot_general(pool, own, (((1,), (1,)), ((), ())), preferred_element_type=jnp.float32)
        pooled[v] = (mean * (1.0 / POOL)).astype(bf)
        return 0

    lax.fori_loop(0, variants, variant, 0)
    total = jnp.zeros((wo_ref.shape[0], 2 * C), jnp.float32)
    for k in range(0, n, 2):
        two = jnp.concatenate([wp[k], wp[k + 1]], axis=0)
        total = total + jnp.dot(wo_ref[:, k * width : (k + 2) * width], two, preferred_element_type=jnp.float32)
    mix[...] = total.astype(bf)
    ring_k0.far_block()
    for k in range(1, 4):
        near = x0 + lax.rem(y0 + 4 - k, 4)
        for source, index in ((near, 64), (other(near), 67)):
            make(mq.at[source], mq.at[source], index + k, {"ctx": near}).wait_recv()

    lane = lax.broadcasted_iota(jnp.int32, (1, 128), 1)
    first = jnp.zeros((1, 128), jnp.int32)
    length = jnp.zeros((1, 128), jnp.int32)
    for v in range(variants):
        first = jnp.where(lane == v, dels[0, v], first)
        length = jnp.where(lane == v, dels[1, v] - dels[0, v], length)
    col = lax.broadcasted_iota(jnp.int32, (tokens, per), 1)
    col_step = col // share * (DEL // 2) + col % (DEL // 2)
    col_offset = (col % share // (DEL // 2) - 1) * DIL + col_step
    qpos = lax.broadcasted_iota(jnp.int32, (tokens, per), 0) + c * tokens

    def aim(v, _):
        s0 = dels[0, v]
        count = dels[1, v] - s0
        spot = jnp.logical_and(qpos - col_offset == s0, col_step < count).astype(bf)
        source = jnp.concatenate([mq[2 * v], mq[2 * v + 1]], axis=0)
        moved_q = jnp.dot(spot, source, preferred_element_type=jnp.float32)
        is_mod = changed(qpos[:, :128] - s0, count)
        q_aug[v, :, :HD] = jnp.where(is_mod, moved_q, queries[...].astype(jnp.float32)).astype(bf)
        q_aug[v, :, HD:] = jnp.broadcast_to(jnp.where(lane == v, 1.0, 0.0), (tokens, 128)).astype(bf)
        top[v] = jnp.full((tokens, 128), -3e38, jnp.float32)
        acc[v] = jnp.zeros((tokens, 256), jnp.float32)
        return 0

    lax.fori_loop(0, variants, aim, 0)
    ones = jnp.where(lane == VD - 128, 1.0, 0.0).astype(bf)

    def unit(v, keys, values):
        s = lax.dot_general(q_aug[v], keys, (((1,), (1,)), ((), ())), preferred_element_type=jnp.float32)
        old = top[v]
        new = jnp.maximum(old, jnp.broadcast_to(s.max(1, keepdims=True), old.shape))
        w = jnp.exp2(s - jnp.concatenate([new] * (keys.shape[0] // 128), axis=1)).astype(bf)
        shrink = jnp.exp2(old - new)
        top[v] = new
        acc[v] = acc[v] * jnp.concatenate([shrink, shrink], axis=1) + jnp.dot(
            w, values, preferred_element_type=jnp.float32
        )

    def attend(step, _):
        look = lambda table: sum((step == i).astype(jnp.int32) * t for i, t in enumerate(table) if t)
        away = look((0, 3, 1, 0, 2, 3, 1, 2))
        across = look((0, 0, 0, 1, 0, 1, 1, 1))
        side = x0 + across * (4 - 2 * x0)
        block = side + lax.rem(y0 + away, 4)
        for i, kv in enumerate((kv0, kv1)):
            rows = slice(i * DIL, (i + 1) * DIL)
            ka[rows, :HD] = kv[block, :DIL]
            pos = lax.broadcasted_iota(jnp.int32, (DIL, 128), 0) + (block * tokens + i * DIL)
            ka[rows, HD:] = jnp.where(changed(pos - first, length), BIG, 0.0).astype(bf)
            va[rows, :128] = kv[block, DIL : 2 * DIL]
            va[rows, 128:] = unpack_tail(kv[block, 2 * DIL :], ones)
        for v in range(variants):
            unit(v, ka[...], va[...])
        return 0

    lax.fori_loop(0, 2, attend, 0)
    ring_k1.far_block()
    ring_o.cross()
    ring_o.relay()
    lax.fori_loop(2, 5, attend, 0)
    ring_k0.end()
    ring_k1.end()
    ring_o.far_block()
    lax.fori_loop(5, n, attend, 0)
    ring_o.end()

    row = lax.broadcasted_iota(jnp.int32, (per, 128), 0)
    step = row // share * (DEL // 2) + row % (DEL // 2)
    row_offset = (row % share // (DEL // 2) - 1) * DIL + step
    count = tokens // POOL // 2
    first_sent = []
    for v in range(variants):
        token = dels[0, v] + row_offset
        valid = (step < dels[1, v] - dels[0, v]) & (token >= 0) & (token < n * tokens)
        ka[:per, HD:] = jnp.where(valid, 0.0, BIG).astype(bf)
        for i in range(2):
            rows = slice(i * share, (i + 1) * share)
            ka[rows, :HD] = mkv[2 * v + i, :share]
            va[rows, :128] = mkv[2 * v + i, share : 2 * share]
            va[rows, 128:] = unpack_tail(mkv[2 * v + i, 2 * share :], ones)
        unit(v, ka[:per], va[:per])
        out = (acc[v, :, :VD] / acc[v, :, VD : VD + 1]).astype(bf)
        mean = jnp.dot(pool, out, preferred_element_type=jnp.float32) * (1.0 / POOL)
        part = jnp.dot(mean.astype(bf), mix[...], preferred_element_type=jnp.float32) + jnp.dot(
            pooled[v], wp_ref[...], preferred_element_type=jnp.float32
        )
        for i in range(2):
            to = 2 * v + i
            mine[to] = part[i * count : (i + 1) * count].astype(bf)
            made = make(mine.at[to], arrived.at[h], 82 + to, {"head": to}, 82 + h)
            first_sent.append(made)

            @pl.when(h != to)
            def _():
                made.start()

            @pl.when(h == to)
            def _():
                arrived[h] = mine[to]

    for k in range(n):
        @pl.when(h != k)
        def _():
            make(mine.at[k], arrived.at[k], 82 + k, {"head": k}).wait_recv()

    total = arrived[0].astype(jnp.float32)
    for k in range(1, n):
        total = total + arrived[k].astype(jnp.float32)
    feats[0] = total[:, :C].astype(bf)
    feats[1] = total[:, C:].astype(bf)
    rows_buf[h] = feats[0]
    for k in range(n):
        to = lax.rem(c + k, n)

        @pl.when(jnp.logical_or(c != h, k != 0))
        def _():
            make(feats.at[1], cols_buf.at[h], 98 + k, {"ctx": to, "head": c}, 98 + h).start()

        @pl.when(jnp.logical_and(c == h, k == 0))
        def _():
            cols_buf[h] = feats[1]

    for k in range(1, n):
        make(feats.at[0], rows_buf.at[h], 90 + k, {"head": lax.rem(h + k, n)}).start()
    for ring in (ring_b0, ring_b1, ring_m, ring_p, ring_k0, ring_k1, ring_o):
        ring.drain()
    for made in shared + asked:
        made.wait_send()
    for k, made in enumerate(first_sent):
        @pl.when(h != k)
        def _():
            made.wait_send()

    for k in range(1, n):
        source = lax.rem(h + n - k, n)
        made = make(feats.at[0], rows_buf.at[source], 90 + k, {"head": lax.rem(h + k, n)})
        made.wait_recv()
        made.wait_send()
    for k in range(n):
        @pl.when(jnp.logical_or(c != h, k != h))
        def _():
            make(feats.at[1], cols_buf.at[k], 98 + k, {"head": lax.rem(h + 1, n)}).wait_recv()

        @pl.when(jnp.logical_or(c != h, k != 0))
        def _():
            make(feats.at[1], cols_buf.at[h], 98 + k, {"head": lax.rem(h + 1, n)}).wait_send()
    row_out[...] = rows_buf[...]
    col_out[...] = cols_buf[...]


def features(sequence, deletions, conv_taps, conv_bias, w_proj, w_out, w_pair):
    tokens, width = sequence.shape
    variants = deletions.shape[0]
    n = 8
    share = SEGS * DEL // 2
    vm = pl.BlockSpec(memory_space=pltpu.VMEM)
    bf, f32 = jnp.bfloat16, jnp.float32
    part = variants * tokens // POOL // n
    scratch = [
        ((width, DIL), bf),
        ((width, DIL), bf),
        ((4, width, 128), f32),
        ((n, width, DIL), bf),
        ((n, width, DIL), bf),
        ((n, share * 3 // 2, 128), bf),
        ((n, width, 2 * C), bf),
        ((n, width, 2 * DEL), bf),
        ((n - 1, width, 2 * DEL), bf),
        ((n * width, 256), bf),
        ((n, DIL * 5 // 2, 128), bf),
        ((n, DIL * 5 // 2, 128), bf),
        ((n, share, 128), bf),
        ((n, share * 5 // 2, 128), bf),
        ((tokens, HD), bf),
        ((variants, tokens, 256), bf),
        ((variants, tokens, 128), f32),
        ((variants, tokens, 256), f32),
        ((tokens, 256), bf),
        ((tokens, 256), bf),
        ((variants, tokens // POOL, width), bf),
        ((w_out.shape[0], 2 * C), bf),
        ((n, part, 2 * C), bf),
        ((n, part, 2 * C), bf),
        ((n, part, C), bf),
        ((n, part, C), bf),
        ((2, part, C), bf),
    ]
    return pl.pallas_call(
        features_kernel,
        out_shape=(jax.ShapeDtypeStruct((n, part, C), bf),) * 2,
        in_specs=[pl.BlockSpec(memory_space=pltpu.SMEM)] + [vm] * 6,
        out_specs=(vm, vm),
        scratch_shapes=[pltpu.VMEM(shape, kind) for shape, kind in scratch]
        + [pltpu.SemaphoreType.DMA((106,)), pltpu.SemaphoreType.DMA((106,))],
        compiler_params=pltpu.CompilerParams(
            collective_id=0, has_side_effects=True, vmem_limit_bytes=56 * 2**20
        ),
    )(deletions.T, sequence.T, conv_taps, conv_bias.reshape(1, width), w_proj.T, w_out, w_pair)


def local(sequence, deletions, conv_taps, conv_bias, w_proj, w_out, w_pair, dist_table):
    variants = deletions.shape[0]
    row_feats, col_feats = features(sequence, deletions, conv_taps, conv_bias, w_proj, w_out, w_pair)
    shape = (variants, sequence.shape[0] // POOL, C)
    return pair_map(row_feats.reshape(shape), col_feats.reshape(shape), dist_table)


def solution(mesh):
    in_specs = (
        P("ctx", "head"),
        P("var", None),
        P(None, "head"),
        P("head"),
        P(None, "head"),
        P("head", None),
        P("head", None),
        P(),
    )
    out_specs = P("var", "ctx", "head", None)
    return jax.shard_map(local, mesh=mesh, in_specs=in_specs, out_specs=out_specs, check_vma=False)
```

```python
import functools
import math

import jax
import jax.numpy as jnp
from jax import lax
from jax.experimental import pallas as pl
from jax.experimental.pallas import tpu as pltpu
from jax.sharding import PartitionSpec as P

HD = 128
VD = 192
C = 128
NB = 16
POOL = 4
DIL = 256
DEL = 128
SEGS = 3
BIG = -1e30
QSCALE = math.log2(math.e) / math.sqrt(HD)


def changed(delta, length):
    hit = jnp.logical_and(delta >= 0, delta < length)
    for shift in (-DIL, DIL):
        moved = delta + shift
        hit = jnp.logical_or(hit, jnp.logical_and(moved >= 0, moved < length))
    return hit


def pair_kernel(per, row_ref, col_ref, table_ref, out_ref, rel, rows, cols, made, sem):
    span = col_ref.shape[1]
    row_count = row_ref.shape[1]
    base = lax.axis_index("head") * span - lax.axis_index("ctx") * row_count - (row_count - 1)
    dist = jnp.abs(lax.broadcasted_iota(jnp.int32, rel.shape, 0) + base)
    value = jnp.broadcast_to(table_ref[0:1, :], rel.shape)
    for k in range(NB - 1):
        value = jnp.where(dist >= 2**k, table_ref[k + 1 : k + 2, :], value)
    rel[...] = value
    rows[...] = row_ref[...].astype(jnp.float32)
    cols[...] = col_ref[...].astype(jnp.float32)

    def copy(group):
        at = pl.ds(pl.multiple_of(group * per, per), per)
        return pltpu.make_async_copy(made.at[:, at], out_ref.at[:, at], sem.at[group])

    def one_group(group, _):
        def one(i, _):
            row = group * per + i
            shifted = rel[pl.ds(row_count - 1 - row, span), :]
            for v in range(row_ref.shape[0]):
                made[v, row] = (rows[v, pl.ds(row, 1), :] + (cols[v] + shifted)).astype(made.dtype)
            return 0

        lax.fori_loop(0, per, one, 0, unroll=4)
        copy(group).start()
        return 0

    def done(group, _):
        copy(group).wait()
        return 0

    lax.fori_loop(0, row_count // per, one_group, 0)
    lax.fori_loop(0, row_count // per, done, 0)


def pair_map(row_feats, col_feats, table):
    variants, rows, _ = row_feats.shape
    cols = col_feats.shape[1]
    per = 8
    vm = pl.BlockSpec(memory_space=pltpu.VMEM)
    shape = (variants, rows, cols, C)
    return pl.pallas_call(
        functools.partial(pair_kernel, per),
        out_shape=jax.ShapeDtypeStruct(shape, jnp.bfloat16),
        in_specs=[vm, vm, vm],
        out_specs=pl.BlockSpec(memory_space=pl.ANY),
        scratch_shapes=[
            pltpu.VMEM((rows + cols, C), jnp.float32),
            pltpu.VMEM((variants, rows, C), jnp.float32),
            pltpu.VMEM((variants, cols, C), jnp.float32),
            pltpu.VMEM(shape, jnp.bfloat16),
            pltpu.SemaphoreType.DMA((rows // per,)),
        ],
        compiler_params=pltpu.CompilerParams(vmem_limit_bytes=60 * 2**20),
    )(row_feats, col_feats, table)


MESH = pl.DeviceIdType.MESH


def pack(x):
    half = x.shape[0] // 2
    tail = jnp.concatenate([x[:half, 128:], x[half:, 128:]], axis=1)
    return jnp.concatenate([x[:, :128], tail], axis=0)


class Ring:
    def __init__(self, make, buf, rows, base, me, dn, up, far, mate, mate_of, to_dn, to_up, to_mate):
        half = rows // 2
        self.full, self.lo, self.hi = pl.ds(0, rows), pl.ds(0, half), pl.ds(half, half)
        self.make, self.buf, self.base = make, buf, base
        self.me, self.dn, self.up, self.far, self.mate, self.mate_of = me, dn, up, far, mate, mate_of
        self.to_dn, self.to_up, self.to_mate = to_dn, to_up, to_mate
        self.sent = []

    def copy(self, slot, rows, index, target):
        ref = self.buf.at[slot, rows]
        return self.make(ref, ref, self.base + index, target)

    def send(self, slot, rows, index, target):
        made = self.copy(slot, rows, index, target)
        made.start()
        self.sent.append(made)

    def got(self, slot, rows, index):
        self.copy(slot, rows, index, self.to_up).wait_recv()


class HeadRing(Ring):
    def begin(self):
        self.send(self.me, self.full, 0, self.to_up)
        self.send(self.me, self.full, 1, self.to_dn)
        self.send(self.me, self.full, 2, self.to_mate)

    def relay(self):
        self.got(self.dn, self.full, 0)
        self.send(self.dn, self.lo, 3, self.to_up)
        self.send(self.dn, self.full, 4, self.to_mate)
        self.got(self.up, self.full, 1)
        self.send(self.up, self.hi, 5, self.to_dn)
        self.send(self.up, self.full, 6, self.to_mate)

    def end(self):
        self.got(self.far, self.lo, 3)
        self.send(self.far, self.lo, 7, self.to_mate)
        self.got(self.far, self.hi, 5)
        self.send(self.far, self.hi, 8, self.to_mate)
        self.got(self.mate, self.full, 2)
        self.got(self.mate_of(self.dn), self.full, 4)
        self.got(self.mate_of(self.up), self.full, 6)
        self.got(self.mate_of(self.far), self.lo, 7)
        self.got(self.mate_of(self.far), self.hi, 8)

    def drain(self):
        for made in self.sent:
            made.wait_send()


class TokenRing(Ring):
    def begin(self):
        self.send(self.me, self.full, 2, self.to_mate)
        self.send(self.me, self.full, 0, self.to_up)
        self.send(self.me, self.full, 1, self.to_dn)

    def cross(self):
        self.got(self.mate, self.full, 2)
        self.send(self.mate, self.full, 4, self.to_up)
        self.send(self.mate, self.full, 6, self.to_dn)

    def relay(self):
        self.got(self.dn, self.full, 0)
        self.send(self.dn, self.lo, 3, self.to_up)
        self.got(self.up, self.full, 1)
        self.send(self.up, self.hi, 5, self.to_dn)

    def far_block(self):
        self.got(self.far, self.lo, 3)
        self.send(self.far, self.lo, 7, self.to_mate)
        self.got(self.far, self.hi, 5)
        self.send(self.far, self.hi, 8, self.to_mate)

    def end(self):
        self.got(self.mate_of(self.dn), self.full, 4)
        self.got(self.mate_of(self.up), self.full, 6)
        self.got(self.mate_of(self.far), self.lo, 7)
        self.got(self.mate_of(self.far), self.hi, 8)

    def drain(self):
        for made in self.sent:
            made.wait_send()


def swap_lanes(x):
    return jnp.concatenate([x[:, 64:], x[:, :64]], axis=1)


def unpack_tail(tail, fill):
    both = jnp.concatenate([tail, swap_lanes(tail)], axis=0)
    keep = lax.broadcasted_iota(jnp.int32, both.shape, 1) < 64
    return jnp.where(keep, both, jnp.broadcast_to(fill, both.shape))


def features_kernel(dels, seq, taps, bias, w_hbm, wo_hbm, wp_ref, row_out, col_out,
                    low, high, cols, gb0, gb1, gm, wp, moved, landed, flat, kv0, kv1, mq, mkv,
                    queries, q_aug, top, acc, ka, va, pooled, mix, mine, arrived, rows_buf, cols_buf, feats, w_ref, wo_ref,
                    send, recv, fetched):
    width, tokens = seq.shape
    variants = dels.shape[1]
    share = SEGS * DEL // 2
    per = 2 * share
    n = 8
    bf = jnp.bfloat16
    c, h, g = lax.axis_index("ctx"), lax.axis_index("head"), lax.axis_index("var")
    dn_h, up_h, far_h = lax.rem(h + 6, n), lax.rem(h + 2, n), lax.rem(h + 4, n)
    sib = h + 1 - 2 * lax.rem(h, 2)
    x0, y0 = c // 4 * 4, lax.rem(c, 4)
    up_c, dn_c, far_c = x0 + lax.rem(y0 + 1, 4), x0 + lax.rem(y0 + 3, 4), x0 + lax.rem(y0 + 2, 4)
    other = lambda t: lax.rem(t + 4, n)
    xp = other(c)
    sib_of = lambda t: t + 1 - 2 * lax.rem(t, 2)

    fetch = [
        pltpu.make_async_copy(w_hbm, w_ref, fetched.at[0]),
        pltpu.make_async_copy(wo_hbm, wo_ref, fetched.at[1]),
    ]
    for made in fetch:
        made.start()
    barrier = pltpu.get_barrier_semaphore()
    peers = [{"ctx": lax.rem(c + k, n)} for k in range(1, n)]
    peers += [{"head": lax.rem(h + k, n)} for k in range(1, n)]
    peers += [{"ctx": xp, "var": 1 - g}]
    for peer in peers:
        pl.semaphore_signal(barrier, inc=1, device_id=peer, device_id_type=MESH)
    for k in range(n):
        source = lax.rem(h + k, n)

        @pl.when(jnp.logical_or(c != h, k != 0))
        def _():
            pl.semaphore_signal(barrier, inc=1, device_id={"ctx": h, "head": source}, device_id_type=MESH)

    for k in range(4):
        line = bias[...] if k == 3 else taps[k : k + 1, :]
        cols[k] = jnp.broadcast_to(line, (128, width)).T
    wp[h] = wp_ref[...]
    run = DEL // 2
    r = lax.broadcasted_iota(jnp.int32, (tokens, 4 * run), 1)
    offset = (r // run - 2) * DIL + (r // (2 * run)) * DIL + r % run
    local_token = lax.broadcasted_iota(jnp.int32, (tokens, 4 * run), 0) + c * tokens - offset

    def gather_runs(v, _):
        for half in range(2):
            pick = (local_token == dels[0, v] + half * run).astype(bf)
            moved[2 * v + half] = jnp.dot(seq[...], pick, preferred_element_type=jnp.float32).astype(bf)
        return 0

    lax.fori_loop(0, variants, gather_runs, 0)
    pl.semaphore_wait(barrier, len(peers) + n - (c == h).astype(jnp.int32))

    def make(src, dst, index, target, arrival=None):
        return pltpu.make_async_remote_copy(
            src_ref=src, dst_ref=dst, send_sem=send.at[index],
            recv_sem=recv.at[index if arrival is None else arrival],
            device_id=(target.get("ctx", c), target.get("head", h), target.get("var", g)), device_id_type=MESH,
        )

    halo_low = make(seq.at[:, pl.ds(tokens - DIL, DIL)], low, 0, {"ctx": lax.rem(c + 1, n)})
    halo_high = make(seq.at[:, pl.ds(0, DIL)], high, 1, {"ctx": lax.rem(c + 7, n)})
    halo_low.start()
    halo_high.start()
    shared = []
    for k in (4, 3, 5, 2, 6, 1, 7):
        to = lax.rem(c + k, n)
        made = make(moved.at[to], landed.at[k - 1], 1 + k, {"ctx": to})
        made.start()
        shared.append(made)

    def head_ring(buf, base):
        return HeadRing(make, buf, buf.shape[1], base, h, dn_h, up_h, far_h, sib, sib_of,
                        {"head": dn_h}, {"head": up_h}, {"head": sib})

    def token_ring(buf, base, to_mate):
        return TokenRing(make, buf, buf.shape[1], base, c, dn_c, up_c, far_c, xp, other,
                         {"ctx": dn_c}, {"ctx": up_c}, to_mate)

    ring_b0, ring_b1, ring_m, ring_p = (head_ring(buf, 10 + 9 * i) for i, buf in enumerate((gb0, gb1, gm, wp)))
    cross = {"ctx": xp, "var": 1 - g}
    ring_k0, ring_k1 = token_ring(kv0, 46, cross), token_ring(kv1, 55, cross)
    ring_o = token_ring(mkv, 73, {"ctx": xp})

    at = lax.broadcasted_iota(jnp.int32, (1, DIL), 1) + c * tokens
    wide = lambda k: jnp.concatenate([cols[k], cols[k]], axis=1)

    def trunk(half, first, length):
        def kept(x, shift, inside=None):
            d = at + (half * DIL + shift) - first
            keep = jnp.logical_or(d < 0, d >= length)
            if inside is not None:
                keep = jnp.logical_and(keep, inside)
            return jnp.where(keep, x.astype(jnp.float32), 0.0)

        here = kept(seq[:, half * DIL : (half + 1) * DIL], 0)
        if half == 0:
            before, after = kept(low[...], -DIL, c != 0), kept(seq[:, DIL:], DIL)
        else:
            before, after = kept(seq[:, :DIL], -DIL), kept(high[...], DIL, c != n - 1)
        conv = wide(0) * before + wide(1) * here + wide(2) * after + wide(3)
        return (here + jax.nn.gelu(conv, approximate=True)).astype(bf)

    ring_p.begin()
    ring_p.relay()
    halo_low.wait()
    gb0[h] = trunk(0, 0, 0)
    ring_b0.begin()
    halo_high.wait()
    gb1[h] = trunk(1, 0, 0)
    ring_b1.begin()

    pool = (
        lax.broadcasted_iota(jnp.int32, (tokens // POOL, tokens), 1) // POOL
        == lax.broadcasted_iota(jnp.int32, (tokens // POOL, tokens), 0)
    ).astype(bf)

    def project(x):
        return jnp.dot(w_ref[...], x, preferred_element_type=jnp.float32).T

    def place(kv, x, count):
        kv[c, :count] = x[:count, HD : 2 * HD].astype(bf)
        kv[c, count:] = pack(x[:count, 2 * HD :].astype(bf))

    ring_p.end()
    ring_b0.relay()
    ring_b1.relay()
    for made in fetch:
        made.wait()
    ring_b0.end()
    x = project(gb0[...].reshape(n * width, DIL))
    place(kv0, x, DIL)
    ring_k0.begin()
    queries[:DIL] = (x[:, :HD] * QSCALE).astype(bf)
    ring_b1.end()
    x = project(gb1[...].reshape(n * width, DIL))
    place(kv1, x, DIL)
    ring_k1.begin()
    queries[DIL:] = (x[:, :HD] * QSCALE).astype(bf)

    total = moved[c].astype(jnp.float32)
    for made in shared:
        made.wait_recv()
    for k in range(1, n):
        total = total + landed[k - 1].astype(jnp.float32)
    runs = [total[:, i * run : (i + 1) * run] for i in range(4)]
    nil = jnp.zeros((width, run), jnp.float32)
    t0, t1, t2, t3 = (cols[k, :, :run] for k in range(4))
    made_rows = []
    for before, here, after in ((runs[0], runs[1], nil), (runs[1], nil, runs[2]), (nil, runs[2], runs[3])):
        conv = t0 * before + t1 * here + t2 * after + t3
        made_rows.append((here + jax.nn.gelu(conv, approximate=True)).astype(bf))
    tail = made_rows[2]
    gm[h, :width] = jnp.concatenate(made_rows[:2], axis=1)
    gm[h, width:] = jnp.concatenate([tail[: width // 2], tail[width // 2 :]], axis=1)
    ring_m.begin()
    ring_k0.cross()
    ring_k0.relay()
    ring_m.relay()
    ring_m.end()
    zero = jnp.zeros((1, 128), bf)
    for k in range(n):
        flat[k * width : (k + 1) * width, :128] = gm[k, :width]
        flat[k * width : (k + 1) * width, 128:] = unpack_tail(gm[k, width:], zero)
    x = project(flat[...])
    mq[c] = (x[:share, :HD] * QSCALE).astype(bf)
    asked = []
    for k in (4, 3, 5, 2, 6, 1, 7):
        made = make(mq.at[c], mq.at[c], 64 + k, {"ctx": lax.rem(c + k, n)})
        made.start()
        asked.append(made)
    place(mkv, x, share)
    ring_o.begin()
    ring_k1.cross()
    ring_k1.relay()

    def variant(v, _):
        first = dels[0, v]
        length = dels[1, v] - first
        own = jnp.concatenate([trunk(0, first, length), trunk(1, first, length)], axis=1)
        mean = lax.dot_general(pool, own, (((1,), (1,)), ((), ())), preferred_element_type=jnp.float32)
        pooled[v] = (mean * (1.0 / POOL)).astype(bf)
        return 0

    lax.fori_loop(0, variants, variant, 0)
    total = jnp.zeros((wo_ref.shape[0], 2 * C), jnp.float32)
    for k in range(0, n, 2):
        two = jnp.concatenate([wp[k], wp[k + 1]], axis=0)
        total = total + jnp.dot(wo_ref[:, k * width : (k + 2) * width], two, preferred_element_type=jnp.float32)
    mix[...] = total.astype(bf)
    ring_k0.far_block()
    for k in range(1, n):
        source = lax.rem(c + n - k, n)
        make(mq.at[source], mq.at[source], 64 + k, {"ctx": lax.rem(c + k, n)}).wait_recv()

    lane = lax.broadcasted_iota(jnp.int32, (1, 128), 1)
    first = jnp.zeros((1, 128), jnp.int32)
    length = jnp.zeros((1, 128), jnp.int32)
    for v in range(variants):
        first = jnp.where(lane == v, dels[0, v], first)
        length = jnp.where(lane == v, dels[1, v] - dels[0, v], length)
    col = lax.broadcasted_iota(jnp.int32, (tokens, per), 1)
    col_step = col // share * (DEL // 2) + col % (DEL // 2)
    col_offset = (col % share // (DEL // 2) - 1) * DIL + col_step
    qpos = lax.broadcasted_iota(jnp.int32, (tokens, per), 0) + c * tokens

    def aim(v, _):
        s0 = dels[0, v]
        count = dels[1, v] - s0
        spot = jnp.logical_and(qpos - col_offset == s0, col_step < count).astype(bf)
        source = jnp.concatenate([mq[2 * v], mq[2 * v + 1]], axis=0)
        moved_q = jnp.dot(spot, source, preferred_element_type=jnp.float32)
        is_mod = changed(qpos[:, :128] - s0, count)
        q_aug[v, :, :HD] = jnp.where(is_mod, moved_q, queries[...].astype(jnp.float32)).astype(bf)
        q_aug[v, :, HD:] = jnp.broadcast_to(jnp.where(lane == v, 1.0, 0.0), (tokens, 128)).astype(bf)
        top[v] = jnp.full((tokens, 128), -3e38, jnp.float32)
        acc[v] = jnp.zeros((tokens, 256), jnp.float32)
        return 0

    lax.fori_loop(0, variants, aim, 0)
    ones = jnp.where(lane == VD - 128, 1.0, 0.0).astype(bf)

    def unit(v, keys, values):
        s = lax.dot_general(q_aug[v], keys, (((1,), (1,)), ((), ())), preferred_element_type=jnp.float32)
        old = top[v]
        new = jnp.maximum(old, jnp.broadcast_to(s.max(1, keepdims=True), old.shape))
        w = jnp.exp2(s - jnp.concatenate([new] * (keys.shape[0] // 128), axis=1)).astype(bf)
        shrink = jnp.exp2(old - new)
        top[v] = new
        acc[v] = acc[v] * jnp.concatenate([shrink, shrink], axis=1) + jnp.dot(
            w, values, preferred_element_type=jnp.float32
        )

    def attend(step, _):
        look = lambda table: sum((step == i).astype(jnp.int32) * t for i, t in enumerate(table) if t)
        away = look((0, 3, 1, 0, 2, 3, 1, 2))
        across = look((0, 0, 0, 1, 0, 1, 1, 1))
        side = x0 + across * (4 - 2 * x0)
        block = side + lax.rem(y0 + away, 4)
        for i, kv in enumerate((kv0, kv1)):
            rows = slice(i * DIL, (i + 1) * DIL)
            ka[rows, :HD] = kv[block, :DIL]
            pos = lax.broadcasted_iota(jnp.int32, (DIL, 128), 0) + (block * tokens + i * DIL)
            ka[rows, HD:] = jnp.where(changed(pos - first, length), BIG, 0.0).astype(bf)
            va[rows, :128] = kv[block, DIL : 2 * DIL]
            va[rows, 128:] = unpack_tail(kv[block, 2 * DIL :], ones)
        for v in range(variants):
            unit(v, ka[...], va[...])
        return 0

    lax.fori_loop(0, 1, attend, 0)
    ring_o.cross()
    ring_o.relay()
    ring_k1.far_block()
    lax.fori_loop(1, 4, attend, 0)
    ring_o.far_block()
    ring_k0.end()
    ring_k1.end()
    lax.fori_loop(4, n, attend, 0)
    for ring in (ring_b0, ring_b1, ring_m, ring_p, ring_k0, ring_k1):
        ring.drain()
    for made in shared + asked:
        made.wait_send()
    ring_o.end()

    row = lax.broadcasted_iota(jnp.int32, (per, 128), 0)
    step = row // share * (DEL // 2) + row % (DEL // 2)
    row_offset = (row % share // (DEL // 2) - 1) * DIL + step
    count = tokens // POOL // 2
    first_sent = []
    for v in range(variants):
        token = dels[0, v] + row_offset
        valid = (step < dels[1, v] - dels[0, v]) & (token >= 0) & (token < n * tokens)
        ka[:per, HD:] = jnp.where(valid, 0.0, BIG).astype(bf)
        for i in range(2):
            rows = slice(i * share, (i + 1) * share)
            ka[rows, :HD] = mkv[2 * v + i, :share]
            va[rows, :128] = mkv[2 * v + i, share : 2 * share]
            va[rows, 128:] = unpack_tail(mkv[2 * v + i, 2 * share :], ones)
        unit(v, ka[:per], va[:per])
        out = (acc[v, :, :VD] / acc[v, :, VD : VD + 1]).astype(bf)
        mean = jnp.dot(pool, out, preferred_element_type=jnp.float32) * (1.0 / POOL)
        part = jnp.dot(mean.astype(bf), mix[...], preferred_element_type=jnp.float32) + jnp.dot(
            pooled[v], wp_ref[...], preferred_element_type=jnp.float32
        )
        for i in range(2):
            to = 2 * v + i
            mine[to] = part[i * count : (i + 1) * count].astype(bf)
            made = make(mine.at[to], arrived.at[h], 82 + to, {"head": to}, 82 + h)
            first_sent.append(made)

            @pl.when(h != to)
            def _():
                made.start()

            @pl.when(h == to)
            def _():
                arrived[h] = mine[to]

    for k in range(n):
        @pl.when(h != k)
        def _():
            make(mine.at[k], arrived.at[k], 82 + k, {"head": k}).wait_recv()

    total = arrived[0].astype(jnp.float32)
    for k in range(1, n):
        total = total + arrived[k].astype(jnp.float32)
    feats[0] = total[:, :C].astype(bf)
    feats[1] = total[:, C:].astype(bf)
    rows_buf[h] = feats[0]
    for k in range(n):
        to = lax.rem(c + k, n)

        @pl.when(jnp.logical_or(c != h, k != 0))
        def _():
            make(feats.at[1], cols_buf.at[h], 98 + k, {"ctx": to, "head": c}, 98 + h).start()

        @pl.when(jnp.logical_and(c == h, k == 0))
        def _():
            cols_buf[h] = feats[1]

    for k in range(1, n):
        make(feats.at[0], rows_buf.at[h], 90 + k, {"head": lax.rem(h + k, n)}).start()
    ring_o.drain()
    for k, made in enumerate(first_sent):
        @pl.when(h != k)
        def _():
            made.wait_send()

    for k in range(1, n):
        source = lax.rem(h + n - k, n)
        made = make(feats.at[0], rows_buf.at[source], 90 + k, {"head": lax.rem(h + k, n)})
        made.wait_recv()
        made.wait_send()
    for k in range(n):
        @pl.when(jnp.logical_or(c != h, k != h))
        def _():
            make(feats.at[1], cols_buf.at[k], 98 + k, {"head": lax.rem(h + 1, n)}).wait_recv()

        @pl.when(jnp.logical_or(c != h, k != 0))
        def _():
            make(feats.at[1], cols_buf.at[h], 98 + k, {"head": lax.rem(h + 1, n)}).wait_send()
    row_out[...] = rows_buf[...]
    col_out[...] = cols_buf[...]


def features(sequence, deletions, conv_taps, conv_bias, w_proj, w_out, w_pair):
    tokens, width = sequence.shape
    variants = deletions.shape[0]
    n = 8
    share = SEGS * DEL // 2
    vm = pl.BlockSpec(memory_space=pltpu.VMEM)
    bf, f32 = jnp.bfloat16, jnp.float32
    part = variants * tokens // POOL // n
    scratch = [
        ((width, DIL), bf),
        ((width, DIL), bf),
        ((4, width, 128), f32),
        ((n, width, DIL), bf),
        ((n, width, DIL), bf),
        ((n, share * 3 // 2, 128), bf),
        ((n, width, 2 * C), bf),
        ((n, width, 2 * DEL), bf),
        ((n - 1, width, 2 * DEL), bf),
        ((n * width, 256), bf),
        ((n, DIL * 5 // 2, 128), bf),
        ((n, DIL * 5 // 2, 128), bf),
        ((n, share, 128), bf),
        ((n, share * 5 // 2, 128), bf),
        ((tokens, HD), bf),
        ((variants, tokens, 256), bf),
        ((variants, tokens, 128), f32),
        ((variants, tokens, 256), f32),
        ((tokens, 256), bf),
        ((tokens, 256), bf),
        ((variants, tokens // POOL, width), bf),
        ((w_out.shape[0], 2 * C), bf),
        ((n, part, 2 * C), bf),
        ((n, part, 2 * C), bf),
        ((n, part, C), bf),
        ((n, part, C), bf),
        ((2, part, C), bf),
        ((w_proj.shape[1], w_proj.shape[0]), bf),
        (w_out.shape, bf),
    ]
    return pl.pallas_call(
        features_kernel,
        out_shape=(jax.ShapeDtypeStruct((n, part, C), bf),) * 2,
        in_specs=[pl.BlockSpec(memory_space=pltpu.SMEM)] + [vm] * 3 + [pl.BlockSpec(memory_space=pl.ANY)] * 2 + [vm],
        out_specs=(vm, vm),
        scratch_shapes=[pltpu.VMEM(shape, kind) for shape, kind in scratch]
        + [pltpu.SemaphoreType.DMA((106,)), pltpu.SemaphoreType.DMA((106,)), pltpu.SemaphoreType.DMA((2,))],
        compiler_params=pltpu.CompilerParams(
            collective_id=0, has_side_effects=True, vmem_limit_bytes=56 * 2**20
        ),
    )(deletions.T, sequence.T, conv_taps, conv_bias.reshape(1, width), w_proj.T, w_out, w_pair)


def local(sequence, deletions, conv_taps, conv_bias, w_proj, w_out, w_pair, dist_table):
    variants = deletions.shape[0]
    row_feats, col_feats = features(sequence, deletions, conv_taps, conv_bias, w_proj, w_out, w_pair)
    shape = (variants, sequence.shape[0] // POOL, C)
    return pair_map(row_feats.reshape(shape), col_feats.reshape(shape), dist_table)


def solution(mesh):
    in_specs = (
        P("ctx", "head"),
        P("var", None),
        P(None, "head"),
        P("head"),
        P(None, "head"),
        P("head", None),
        P("head", None),
        P(),
    )
    out_specs = P("var", "ctx", "head", None)
    return jax.shard_map(local, mesh=mesh, in_specs=in_specs, out_specs=out_specs, check_vma=False)
```

```python
import functools
import math

import jax
import jax.numpy as jnp
from jax import lax
from jax.experimental import pallas as pl
from jax.experimental.pallas import tpu as pltpu
from jax.sharding import PartitionSpec as P

HD = 128
VD = 192
C = 128
NB = 16
POOL = 4
DIL = 256
DEL = 128
SEGS = 3
BIG = -1e30
QSCALE = math.log2(math.e) / math.sqrt(HD)


def changed(delta, length):
    hit = jnp.logical_and(delta >= 0, delta < length)
    for shift in (-DIL, DIL):
        moved = delta + shift
        hit = jnp.logical_or(hit, jnp.logical_and(moved >= 0, moved < length))
    return hit


def pair_kernel(per, row_ref, col_ref, table_ref, out_ref, rel, rows, cols, made, sem):
    span = col_ref.shape[1]
    row_count = row_ref.shape[1]
    base = lax.axis_index("head") * span - lax.axis_index("ctx") * row_count - (row_count - 1)
    dist = jnp.abs(lax.broadcasted_iota(jnp.int32, rel.shape, 0) + base)
    value = jnp.broadcast_to(table_ref[0:1, :], rel.shape)
    for k in range(NB - 1):
        value = jnp.where(dist >= 2**k, table_ref[k + 1 : k + 2, :], value)
    rel[...] = value
    rows[...] = row_ref[...].astype(jnp.float32)
    cols[...] = col_ref[...].astype(jnp.float32)

    def copy(group):
        at = pl.ds(pl.multiple_of(group * per, per), per)
        return pltpu.make_async_copy(made.at[:, at], out_ref.at[:, at], sem.at[group])

    def one_group(group, _):
        def one(i, _):
            row = group * per + i
            shifted = rel[pl.ds(row_count - 1 - row, span), :]
            for v in range(row_ref.shape[0]):
                made[v, row] = (rows[v, pl.ds(row, 1), :] + (cols[v] + shifted)).astype(made.dtype)
            return 0

        lax.fori_loop(0, per, one, 0, unroll=4)
        copy(group).start()
        return 0

    def done(group, _):
        copy(group).wait()
        return 0

    lax.fori_loop(0, row_count // per, one_group, 0)
    lax.fori_loop(0, row_count // per, done, 0)


def pair_map(row_feats, col_feats, table):
    variants, rows, _ = row_feats.shape
    cols = col_feats.shape[1]
    per = 8
    vm = pl.BlockSpec(memory_space=pltpu.VMEM)
    shape = (variants, rows, cols, C)
    return pl.pallas_call(
        functools.partial(pair_kernel, per),
        out_shape=jax.ShapeDtypeStruct(shape, jnp.bfloat16),
        in_specs=[vm, vm, vm],
        out_specs=pl.BlockSpec(memory_space=pl.ANY),
        scratch_shapes=[
            pltpu.VMEM((rows + cols, C), jnp.float32),
            pltpu.VMEM((variants, rows, C), jnp.float32),
            pltpu.VMEM((variants, cols, C), jnp.float32),
            pltpu.VMEM(shape, jnp.bfloat16),
            pltpu.SemaphoreType.DMA((rows // per,)),
        ],
        compiler_params=pltpu.CompilerParams(vmem_limit_bytes=60 * 2**20),
    )(row_feats, col_feats, table)


MESH = pl.DeviceIdType.MESH


def pack(x):
    half = x.shape[0] // 2
    tail = jnp.concatenate([x[:half, 128:], x[half:, 128:]], axis=1)
    return jnp.concatenate([x[:, :128], tail], axis=0)


class Ring:
    def __init__(self, make, buf, rows, base, me, dn, up, far, mate, mate_of, to_dn, to_up, to_mate):
        half = rows // 2
        self.full, self.lo, self.hi = pl.ds(0, rows), pl.ds(0, half), pl.ds(half, half)
        self.make, self.buf, self.base = make, buf, base
        self.me, self.dn, self.up, self.far, self.mate, self.mate_of = me, dn, up, far, mate, mate_of
        self.to_dn, self.to_up, self.to_mate = to_dn, to_up, to_mate
        self.sent = []

    def copy(self, slot, rows, index, target):
        ref = self.buf.at[slot, rows]
        return self.make(ref, ref, self.base + index, target)

    def send(self, slot, rows, index, target):
        made = self.copy(slot, rows, index, target)
        made.start()
        self.sent.append(made)

    def got(self, slot, rows, index):
        self.copy(slot, rows, index, self.to_up).wait_recv()


class HeadRing(Ring):
    def begin(self):
        self.send(self.me, self.full, 0, self.to_up)
        self.send(self.me, self.full, 1, self.to_dn)
        self.send(self.me, self.full, 2, self.to_mate)

    def relay(self):
        self.got(self.dn, self.full, 0)
        self.send(self.dn, self.lo, 3, self.to_up)
        self.send(self.dn, self.full, 4, self.to_mate)
        self.got(self.up, self.full, 1)
        self.send(self.up, self.hi, 5, self.to_dn)
        self.send(self.up, self.full, 6, self.to_mate)

    def end(self):
        self.got(self.far, self.lo, 3)
        self.send(self.far, self.lo, 7, self.to_mate)
        self.got(self.far, self.hi, 5)
        self.send(self.far, self.hi, 8, self.to_mate)
        self.got(self.mate, self.full, 2)
        self.got(self.mate_of(self.dn), self.full, 4)
        self.got(self.mate_of(self.up), self.full, 6)
        self.got(self.mate_of(self.far), self.lo, 7)
        self.got(self.mate_of(self.far), self.hi, 8)

    def drain(self):
        for made in self.sent:
            made.wait_send()


class TokenRing(Ring):
    def begin(self):
        self.send(self.me, self.full, 2, self.to_mate)
        self.send(self.me, self.full, 0, self.to_up)
        self.send(self.me, self.full, 1, self.to_dn)

    def cross(self):
        self.got(self.mate, self.full, 2)
        self.send(self.mate, self.full, 4, self.to_up)
        self.send(self.mate, self.full, 6, self.to_dn)

    def relay(self):
        self.got(self.dn, self.full, 0)
        self.send(self.dn, self.lo, 3, self.to_up)
        self.got(self.up, self.full, 1)
        self.send(self.up, self.hi, 5, self.to_dn)

    def far_block(self):
        self.got(self.far, self.lo, 3)
        self.send(self.far, self.lo, 7, self.to_mate)
        self.got(self.far, self.hi, 5)
        self.send(self.far, self.hi, 8, self.to_mate)

    def end(self):
        self.got(self.mate_of(self.dn), self.full, 4)
        self.got(self.mate_of(self.up), self.full, 6)
        self.got(self.mate_of(self.far), self.lo, 7)
        self.got(self.mate_of(self.far), self.hi, 8)

    def drain(self):
        for made in self.sent:
            made.wait_send()


def swap_lanes(x):
    return jnp.concatenate([x[:, 64:], x[:, :64]], axis=1)


def unpack_tail(tail, fill):
    both = jnp.concatenate([tail, swap_lanes(tail)], axis=0)
    keep = lax.broadcasted_iota(jnp.int32, both.shape, 1) < 64
    return jnp.where(keep, both, jnp.broadcast_to(fill, both.shape))


def features_kernel(dels, seq, taps, bias, w_hbm, wo_hbm, wp_ref, row_out, col_out,
                    low, high, cols, gb0, gb1, gm, wp, moved, landed, flat, kv0, kv1, mq, mkv,
                    queries, q_aug, top, acc, ka, va, pooled, mix, mine, arrived, rows_buf, cols_buf, feats, w_ref, wo_ref,
                    send, recv, fetched):
    width, tokens = seq.shape
    variants = dels.shape[1]
    share = SEGS * DEL // 2
    per = 2 * share
    n = 8
    bf = jnp.bfloat16
    c, h, g = lax.axis_index("ctx"), lax.axis_index("head"), lax.axis_index("var")
    dn_h, up_h, far_h = lax.rem(h + 6, n), lax.rem(h + 2, n), lax.rem(h + 4, n)
    sib = h + 1 - 2 * lax.rem(h, 2)
    x0, y0 = c // 4 * 4, lax.rem(c, 4)
    up_c, dn_c, far_c = x0 + lax.rem(y0 + 1, 4), x0 + lax.rem(y0 + 3, 4), x0 + lax.rem(y0 + 2, 4)
    other = lambda t: lax.rem(t + 4, n)
    xp = other(c)
    sib_of = lambda t: t + 1 - 2 * lax.rem(t, 2)

    fetch = [
        pltpu.make_async_copy(w_hbm, w_ref, fetched.at[0]),
        pltpu.make_async_copy(wo_hbm, wo_ref, fetched.at[1]),
    ]
    for made in fetch:
        made.start()
    barrier = pltpu.get_barrier_semaphore()
    peers = [{"ctx": lax.rem(c + k, n)} for k in range(1, n)]
    peers += [{"head": lax.rem(h + k, n)} for k in range(1, n)]
    peers += [{"ctx": xp, "var": 1 - g}]
    for peer in peers:
        pl.semaphore_signal(barrier, inc=1, device_id=peer, device_id_type=MESH)
    for k in range(n):
        source = lax.rem(h + k, n)

        @pl.when(jnp.logical_or(c != h, k != 0))
        def _():
            pl.semaphore_signal(barrier, inc=1, device_id={"ctx": h, "head": source}, device_id_type=MESH)

    for k in range(4):
        line = bias[...] if k == 3 else taps[k : k + 1, :]
        cols[k] = jnp.broadcast_to(line, (128, width)).T
    wp[h] = wp_ref[...]
    run = DEL // 2
    r = lax.broadcasted_iota(jnp.int32, (tokens, 4 * run), 1)
    offset = (r // run - 2) * DIL + (r // (2 * run)) * DIL + r % run
    local_token = lax.broadcasted_iota(jnp.int32, (tokens, 4 * run), 0) + c * tokens - offset

    def gather_runs(v, _):
        for half in range(2):
            pick = (local_token == dels[0, v] + half * run).astype(bf)
            moved[2 * v + half] = jnp.dot(seq[...], pick, preferred_element_type=jnp.float32).astype(bf)
        return 0

    lax.fori_loop(0, variants, gather_runs, 0)
    pl.semaphore_wait(barrier, len(peers) + n - (c == h).astype(jnp.int32))

    def make(src, dst, index, target, arrival=None):
        return pltpu.make_async_remote_copy(
            src_ref=src, dst_ref=dst, send_sem=send.at[index],
            recv_sem=recv.at[index if arrival is None else arrival],
            device_id=(target.get("ctx", c), target.get("head", h), target.get("var", g)), device_id_type=MESH,
        )

    halo_low = make(seq.at[:, pl.ds(tokens - DIL, DIL)], low, 0, {"ctx": lax.rem(c + 1, n)})
    halo_high = make(seq.at[:, pl.ds(0, DIL)], high, 1, {"ctx": lax.rem(c + 7, n)})
    halo_low.start()
    halo_high.start()
    shared = []
    for k in (4, 3, 5, 2, 6, 1, 7):
        to = lax.rem(c + k, n)
        made = make(moved.at[to], landed.at[k - 1], 1 + k, {"ctx": to})
        made.start()
        shared.append(made)

    def head_ring(buf, base):
        return HeadRing(make, buf, buf.shape[1], base, h, dn_h, up_h, far_h, sib, sib_of,
                        {"head": dn_h}, {"head": up_h}, {"head": sib})

    def token_ring(buf, base, to_mate):
        return TokenRing(make, buf, buf.shape[1], base, c, dn_c, up_c, far_c, xp, other,
                         {"ctx": dn_c}, {"ctx": up_c}, to_mate)

    ring_b0, ring_b1, ring_m, ring_p = (head_ring(buf, 10 + 9 * i) for i, buf in enumerate((gb0, gb1, gm, wp)))
    cross = {"ctx": xp, "var": 1 - g}
    ring_k0, ring_k1 = token_ring(kv0, 46, cross), token_ring(kv1, 55, cross)
    ring_o = token_ring(mkv, 73, {"ctx": xp})

    at = lax.broadcasted_iota(jnp.int32, (1, DIL), 1) + c * tokens
    wide = lambda k: jnp.concatenate([cols[k], cols[k]], axis=1)

    def trunk(half, first, length):
        def kept(x, shift, inside=None):
            d = at + (half * DIL + shift) - first
            keep = jnp.logical_or(d < 0, d >= length)
            if inside is not None:
                keep = jnp.logical_and(keep, inside)
            return jnp.where(keep, x.astype(jnp.float32), 0.0)

        here = kept(seq[:, half * DIL : (half + 1) * DIL], 0)
        if half == 0:
            before, after = kept(low[...], -DIL, c != 0), kept(seq[:, DIL:], DIL)
        else:
            before, after = kept(seq[:, :DIL], -DIL), kept(high[...], DIL, c != n - 1)
        conv = wide(0) * before + wide(1) * here + wide(2) * after + wide(3)
        return (here + jax.nn.gelu(conv, approximate=True)).astype(bf)

    ring_p.begin()
    ring_p.relay()
    halo_low.wait()
    gb0[h] = trunk(0, 0, 0)
    ring_b0.begin()
    halo_high.wait()
    gb1[h] = trunk(1, 0, 0)
    ring_b1.begin()

    pool = (
        lax.broadcasted_iota(jnp.int32, (tokens // POOL, tokens), 1) // POOL
        == lax.broadcasted_iota(jnp.int32, (tokens // POOL, tokens), 0)
    ).astype(bf)

    def project(x):
        return jnp.dot(w_ref[...], x, preferred_element_type=jnp.float32).T

    def place(kv, x, count):
        kv[c, :count] = x[:count, HD : 2 * HD].astype(bf)
        kv[c, count:] = pack(x[:count, 2 * HD :].astype(bf))

    ring_p.end()
    ring_b0.relay()
    ring_b1.relay()
    for made in fetch:
        made.wait()
    ring_b0.end()
    x = project(gb0[...].reshape(n * width, DIL))
    place(kv0, x, DIL)
    ring_k0.begin()
    queries[:DIL] = (x[:, :HD] * QSCALE).astype(bf)
    ring_b1.end()
    x = project(gb1[...].reshape(n * width, DIL))
    place(kv1, x, DIL)
    ring_k1.begin()
    queries[DIL:] = (x[:, :HD] * QSCALE).astype(bf)

    total = moved[c].astype(jnp.float32)
    for made in shared:
        made.wait_recv()
    for k in range(1, n):
        total = total + landed[k - 1].astype(jnp.float32)
    runs = [total[:, i * run : (i + 1) * run] for i in range(4)]
    nil = jnp.zeros((width, run), jnp.float32)
    t0, t1, t2, t3 = (cols[k, :, :run] for k in range(4))
    made_rows = []
    for before, here, after in ((runs[0], runs[1], nil), (runs[1], nil, runs[2]), (nil, runs[2], runs[3])):
        conv = t0 * before + t1 * here + t2 * after + t3
        made_rows.append((here + jax.nn.gelu(conv, approximate=True)).astype(bf))
    tail = made_rows[2]
    gm[h, :width] = jnp.concatenate(made_rows[:2], axis=1)
    gm[h, width:] = jnp.concatenate([tail[: width // 2], tail[width // 2 :]], axis=1)
    ring_m.begin()
    ring_k0.cross()
    ring_k0.relay()
    ring_m.relay()
    ring_m.end()
    zero = jnp.zeros((1, 128), bf)
    for k in range(n):
        flat[k * width : (k + 1) * width, :128] = gm[k, :width]
        flat[k * width : (k + 1) * width, 128:] = unpack_tail(gm[k, width:], zero)
    x = project(flat[...])
    mq[c] = (x[:share, :HD] * QSCALE).astype(bf)
    asked = []
    for k in (4, 3, 5, 2, 6, 1, 7):
        made = make(mq.at[c], mq.at[c], 64 + k, {"ctx": lax.rem(c + k, n)})
        made.start()
        asked.append(made)
    place(mkv, x, share)
    ring_o.begin()
    ring_k1.cross()
    ring_k1.relay()

    def variant(v, _):
        first = dels[0, v]
        length = dels[1, v] - first
        own = jnp.concatenate([trunk(0, first, length), trunk(1, first, length)], axis=1)
        mean = lax.dot_general(pool, own, (((1,), (1,)), ((), ())), preferred_element_type=jnp.float32)
        pooled[v] = (mean * (1.0 / POOL)).astype(bf)
        return 0

    lax.fori_loop(0, variants, variant, 0)
    total = jnp.zeros((wo_ref.shape[0], 2 * C), jnp.float32)
    for k in range(0, n, 2):
        two = jnp.concatenate([wp[k], wp[k + 1]], axis=0)
        total = total + jnp.dot(wo_ref[:, k * width : (k + 2) * width], two, preferred_element_type=jnp.float32)
    mix[...] = total.astype(bf)
    ring_k0.far_block()
    for k in range(1, n):
        source = lax.rem(c + n - k, n)
        make(mq.at[source], mq.at[source], 64 + k, {"ctx": lax.rem(c + k, n)}).wait_recv()

    lane = lax.broadcasted_iota(jnp.int32, (1, 128), 1)
    first = jnp.zeros((1, 128), jnp.int32)
    length = jnp.zeros((1, 128), jnp.int32)
    for v in range(variants):
        first = jnp.where(lane == v, dels[0, v], first)
        length = jnp.where(lane == v, dels[1, v] - dels[0, v], length)
    col = lax.broadcasted_iota(jnp.int32, (tokens, per), 1)
    col_step = col // share * (DEL // 2) + col % (DEL // 2)
    col_offset = (col % share // (DEL // 2) - 1) * DIL + col_step
    qpos = lax.broadcasted_iota(jnp.int32, (tokens, per), 0) + c * tokens

    def aim(v, _):
        s0 = dels[0, v]
        count = dels[1, v] - s0
        spot = jnp.logical_and(qpos - col_offset == s0, col_step < count).astype(bf)
        source = jnp.concatenate([mq[2 * v], mq[2 * v + 1]], axis=0)
        moved_q = jnp.dot(spot, source, preferred_element_type=jnp.float32)
        is_mod = changed(qpos[:, :128] - s0, count)
        q_aug[v, :, :HD] = jnp.where(is_mod, moved_q, queries[...].astype(jnp.float32)).astype(bf)
        q_aug[v, :, HD:] = jnp.broadcast_to(jnp.where(lane == v, 1.0, 0.0), (tokens, 128)).astype(bf)
        top[v] = jnp.full((tokens, 128), -3e38, jnp.float32)
        acc[v] = jnp.zeros((tokens, 256), jnp.float32)
        return 0

    lax.fori_loop(0, variants, aim, 0)
    ones = jnp.where(lane == VD - 128, 1.0, 0.0).astype(bf)

    def unit(v, keys, values):
        s = lax.dot_general(q_aug[v], keys, (((1,), (1,)), ((), ())), preferred_element_type=jnp.float32)
        old = top[v]
        new = jnp.maximum(old, jnp.broadcast_to(s.max(1, keepdims=True), old.shape))
        w = jnp.exp2(s - jnp.concatenate([new] * (keys.shape[0] // 128), axis=1)).astype(bf)
        shrink = jnp.exp2(old - new)
        top[v] = new
        acc[v] = acc[v] * jnp.concatenate([shrink, shrink], axis=1) + jnp.dot(
            w, values, preferred_element_type=jnp.float32
        )

    def attend(step, _):
        look = lambda table: sum((step == i).astype(jnp.int32) * t for i, t in enumerate(table) if t)
        away = look((0, 3, 1, 0, 2, 3, 1, 2))
        across = look((0, 0, 0, 1, 0, 1, 1, 1))
        side = x0 + across * (4 - 2 * x0)
        block = side + lax.rem(y0 + away, 4)
        for i, kv in enumerate((kv0, kv1)):
            rows = slice(i * DIL, (i + 1) * DIL)
            ka[rows, :HD] = kv[block, :DIL]
            pos = lax.broadcasted_iota(jnp.int32, (DIL, 128), 0) + (block * tokens + i * DIL)
            ka[rows, HD:] = jnp.where(changed(pos - first, length), BIG, 0.0).astype(bf)
            va[rows, :128] = kv[block, DIL : 2 * DIL]
            va[rows, 128:] = unpack_tail(kv[block, 2 * DIL :], ones)
        for v in range(variants):
            unit(v, ka[...], va[...])
        return 0

    lax.fori_loop(0, 2, attend, 0)
    ring_k1.far_block()
    ring_o.cross()
    ring_o.relay()
    lax.fori_loop(2, 5, attend, 0)
    ring_k0.end()
    ring_k1.end()
    ring_o.far_block()
    lax.fori_loop(5, n, attend, 0)
    ring_o.end()

    row = lax.broadcasted_iota(jnp.int32, (per, 128), 0)
    step = row // share * (DEL // 2) + row % (DEL // 2)
    row_offset = (row % share // (DEL // 2) - 1) * DIL + step
    count = tokens // POOL // 2
    first_sent = []
    for v in range(variants):
        token = dels[0, v] + row_offset
        valid = (step < dels[1, v] - dels[0, v]) & (token >= 0) & (token < n * tokens)
        ka[:per, HD:] = jnp.where(valid, 0.0, BIG).astype(bf)
        for i in range(2):
            rows = slice(i * share, (i + 1) * share)
            ka[rows, :HD] = mkv[2 * v + i, :share]
            va[rows, :128] = mkv[2 * v + i, share : 2 * share]
            va[rows, 128:] = unpack_tail(mkv[2 * v + i, 2 * share :], ones)
        unit(v, ka[:per], va[:per])
        out = (acc[v, :, :VD] / acc[v, :, VD : VD + 1]).astype(bf)
        mean = jnp.dot(pool, out, preferred_element_type=jnp.float32) * (1.0 / POOL)
        part = jnp.dot(mean.astype(bf), mix[...], preferred_element_type=jnp.float32) + jnp.dot(
            pooled[v], wp_ref[...], preferred_element_type=jnp.float32
        )
        for i in range(2):
            to = 2 * v + i
            mine[to] = part[i * count : (i + 1) * count].astype(bf)
            made = make(mine.at[to], arrived.at[h], 82 + to, {"head": to}, 82 + h)
            first_sent.append(made)

            @pl.when(h != to)
            def _():
                made.start()

            @pl.when(h == to)
            def _():
                arrived[h] = mine[to]

    for k in range(n):
        @pl.when(h != k)
        def _():
            make(mine.at[k], arrived.at[k], 82 + k, {"head": k}).wait_recv()

    total = arrived[0].astype(jnp.float32)
    for k in range(1, n):
        total = total + arrived[k].astype(jnp.float32)
    feats[0] = total[:, :C].astype(bf)
    feats[1] = total[:, C:].astype(bf)
    rows_buf[h] = feats[0]
    for k in range(n):
        to = lax.rem(c + k, n)

        @pl.when(jnp.logical_or(c != h, k != 0))
        def _():
            make(feats.at[1], cols_buf.at[h], 98 + k, {"ctx": to, "head": c}, 98 + h).start()

        @pl.when(jnp.logical_and(c == h, k == 0))
        def _():
            cols_buf[h] = feats[1]

    for k in range(1, n):
        make(feats.at[0], rows_buf.at[h], 90 + k, {"head": lax.rem(h + k, n)}).start()
    for ring in (ring_b0, ring_b1, ring_m, ring_p, ring_k0, ring_k1, ring_o):
        ring.drain()
    for made in shared + asked:
        made.wait_send()
    for k, made in enumerate(first_sent):
        @pl.when(h != k)
        def _():
            made.wait_send()

    for k in range(1, n):
        source = lax.rem(h + n - k, n)
        made = make(feats.at[0], rows_buf.at[source], 90 + k, {"head": lax.rem(h + k, n)})
        made.wait_recv()
        made.wait_send()
    for k in range(n):
        @pl.when(jnp.logical_or(c != h, k != h))
        def _():
            make(feats.at[1], cols_buf.at[k], 98 + k, {"head": lax.rem(h + 1, n)}).wait_recv()

        @pl.when(jnp.logical_or(c != h, k != 0))
        def _():
            make(feats.at[1], cols_buf.at[h], 98 + k, {"head": lax.rem(h + 1, n)}).wait_send()
    row_out[...] = rows_buf[...]
    col_out[...] = cols_buf[...]


def features(sequence, deletions, conv_taps, conv_bias, w_proj, w_out, w_pair):
    tokens, width = sequence.shape
    variants = deletions.shape[0]
    n = 8
    share = SEGS * DEL // 2
    vm = pl.BlockSpec(memory_space=pltpu.VMEM)
    bf, f32 = jnp.bfloat16, jnp.float32
    part = variants * tokens // POOL // n
    scratch = [
        ((width, DIL), bf),
        ((width, DIL), bf),
        ((4, width, 128), f32),
        ((n, width, DIL), bf),
        ((n, width, DIL), bf),
        ((n, share * 3 // 2, 128), bf),
        ((n, width, 2 * C), bf),
        ((n, width, 2 * DEL), bf),
        ((n - 1, width, 2 * DEL), bf),
        ((n * width, 256), bf),
        ((n, DIL * 5 // 2, 128), bf),
        ((n, DIL * 5 // 2, 128), bf),
        ((n, share, 128), bf),
        ((n, share * 5 // 2, 128), bf),
        ((tokens, HD), bf),
        ((variants, tokens, 256), bf),
        ((variants, tokens, 128), f32),
        ((variants, tokens, 256), f32),
        ((tokens, 256), bf),
        ((tokens, 256), bf),
        ((variants, tokens // POOL, width), bf),
        ((w_out.shape[0], 2 * C), bf),
        ((n, part, 2 * C), bf),
        ((n, part, 2 * C), bf),
        ((n, part, C), bf),
        ((n, part, C), bf),
        ((2, part, C), bf),
        ((w_proj.shape[1], w_proj.shape[0]), bf),
        (w_out.shape, bf),
    ]
    return pl.pallas_call(
        features_kernel,
        out_shape=(jax.ShapeDtypeStruct((n, part, C), bf),) * 2,
        in_specs=[pl.BlockSpec(memory_space=pltpu.SMEM)] + [vm] * 3 + [pl.BlockSpec(memory_space=pl.ANY)] * 2 + [vm],
        out_specs=(vm, vm),
        scratch_shapes=[pltpu.VMEM(shape, kind) for shape, kind in scratch]
        + [pltpu.SemaphoreType.DMA((106,)), pltpu.SemaphoreType.DMA((106,)), pltpu.SemaphoreType.DMA((2,))],
        compiler_params=pltpu.CompilerParams(
            collective_id=0, has_side_effects=True, vmem_limit_bytes=56 * 2**20
        ),
    )(deletions.T, sequence.T, conv_taps, conv_bias.reshape(1, width), w_proj.T, w_out, w_pair)


def local(sequence, deletions, conv_taps, conv_bias, w_proj, w_out, w_pair, dist_table):
    variants = deletions.shape[0]
    row_feats, col_feats = features(sequence, deletions, conv_taps, conv_bias, w_proj, w_out, w_pair)
    shape = (variants, sequence.shape[0] // POOL, C)
    return pair_map(row_feats.reshape(shape), col_feats.reshape(shape), dist_table)


def solution(mesh):
    in_specs = (
        P("ctx", "head"),
        P("var", None),
        P(None, "head"),
        P("head"),
        P(None, "head"),
        P("head", None),
        P("head", None),
        P(),
    )
    out_specs = P("var", "ctx", "head", None)
    return jax.shard_map(local, mesh=mesh, in_specs=in_specs, out_specs=out_specs, check_vma=False)
```

```python
import functools
import math

import jax
import jax.numpy as jnp
from jax import lax
from jax.experimental import pallas as pl
from jax.experimental.pallas import tpu as pltpu
from jax.sharding import PartitionSpec as P

HD = 128
VD = 192
C = 128
NB = 16
POOL = 4
DIL = 256
DEL = 128
SEGS = 3
BIG = -1e30
QSCALE = math.log2(math.e) / math.sqrt(HD)


def changed(delta, length):
    hit = jnp.logical_and(delta >= 0, delta < length)
    for shift in (-DIL, DIL):
        moved = delta + shift
        hit = jnp.logical_or(hit, jnp.logical_and(moved >= 0, moved < length))
    return hit


def pair_kernel(per, row_ref, col_ref, table_ref, out_ref, rel, rows, cols, made, sem):
    span = col_ref.shape[1]
    row_count = row_ref.shape[1]
    base = lax.axis_index("head") * span - lax.axis_index("ctx") * row_count - (row_count - 1)
    dist = jnp.abs(lax.broadcasted_iota(jnp.int32, rel.shape, 0) + base)
    value = jnp.broadcast_to(table_ref[0:1, :], rel.shape)
    for k in range(NB - 1):
        value = jnp.where(dist >= 2**k, table_ref[k + 1 : k + 2, :], value)
    rel[...] = value
    rows[...] = row_ref[...].astype(jnp.float32)
    cols[...] = col_ref[...].astype(jnp.float32)

    def copy(group):
        at = pl.ds(pl.multiple_of(group * per, per), per)
        return pltpu.make_async_copy(made.at[:, at], out_ref.at[:, at], sem.at[group])

    def one_group(group, _):
        def one(i, _):
            row = group * per + i
            shifted = rel[pl.ds(row_count - 1 - row, span), :]
            for v in range(row_ref.shape[0]):
                made[v, row] = (rows[v, pl.ds(row, 1), :] + (cols[v] + shifted)).astype(made.dtype)
            return 0

        lax.fori_loop(0, per, one, 0, unroll=4)
        copy(group).start()
        return 0

    def done(group, _):
        copy(group).wait()
        return 0

    lax.fori_loop(0, row_count // per, one_group, 0)
    lax.fori_loop(0, row_count // per, done, 0)


def pair_map(row_feats, col_feats, table):
    variants, rows, _ = row_feats.shape
    cols = col_feats.shape[1]
    per = 8
    vm = pl.BlockSpec(memory_space=pltpu.VMEM)
    shape = (variants, rows, cols, C)
    return pl.pallas_call(
        functools.partial(pair_kernel, per),
        out_shape=jax.ShapeDtypeStruct(shape, jnp.bfloat16),
        in_specs=[vm, vm, vm],
        out_specs=pl.BlockSpec(memory_space=pl.ANY),
        scratch_shapes=[
            pltpu.VMEM((rows + cols, C), jnp.float32),
            pltpu.VMEM((variants, rows, C), jnp.float32),
            pltpu.VMEM((variants, cols, C), jnp.float32),
            pltpu.VMEM(shape, jnp.bfloat16),
            pltpu.SemaphoreType.DMA((rows // per,)),
        ],
        compiler_params=pltpu.CompilerParams(vmem_limit_bytes=60 * 2**20),
    )(row_feats, col_feats, table)


MESH = pl.DeviceIdType.MESH


def pack(x):
    half = x.shape[0] // 2
    tail = jnp.concatenate([x[:half, 128:], x[half:, 128:]], axis=1)
    return jnp.concatenate([x[:, :128], tail], axis=0)


class Ring:
    def __init__(self, make, buf, rows, base, me, dn, up, far, mate, mate_of, to_dn, to_up, to_mate):
        half = rows // 2
        self.full, self.lo, self.hi = pl.ds(0, rows), pl.ds(0, half), pl.ds(half, half)
        self.make, self.buf, self.base = make, buf, base
        self.me, self.dn, self.up, self.far, self.mate, self.mate_of = me, dn, up, far, mate, mate_of
        self.to_dn, self.to_up, self.to_mate = to_dn, to_up, to_mate
        self.sent = []

    def copy(self, slot, rows, index, target):
        ref = self.buf.at[slot, rows]
        return self.make(ref, ref, self.base + index, target)

    def send(self, slot, rows, index, target):
        made = self.copy(slot, rows, index, target)
        made.start()
        self.sent.append(made)

    def got(self, slot, rows, index):
        self.copy(slot, rows, index, self.to_up).wait_recv()


class HeadRing(Ring):
    def begin(self):
        self.send(self.me, self.full, 0, self.to_up)
        self.send(self.me, self.full, 1, self.to_dn)
        self.send(self.me, self.full, 2, self.to_mate)

    def relay(self):
        self.got(self.dn, self.full, 0)
        self.send(self.dn, self.lo, 3, self.to_up)
        self.send(self.dn, self.full, 4, self.to_mate)
        self.got(self.up, self.full, 1)
        self.send(self.up, self.hi, 5, self.to_dn)
        self.send(self.up, self.full, 6, self.to_mate)

    def end(self):
        self.got(self.far, self.lo, 3)
        self.send(self.far, self.lo, 7, self.to_mate)
        self.got(self.far, self.hi, 5)
        self.send(self.far, self.hi, 8, self.to_mate)
        self.got(self.mate, self.full, 2)
        self.got(self.mate_of(self.dn), self.full, 4)
        self.got(self.mate_of(self.up), self.full, 6)
        self.got(self.mate_of(self.far), self.lo, 7)
        self.got(self.mate_of(self.far), self.hi, 8)

    def drain(self):
        for made in self.sent:
            made.wait_send()


class TokenRing(Ring):
    def begin(self):
        self.send(self.me, self.full, 2, self.to_mate)
        self.send(self.me, self.full, 0, self.to_up)
        self.send(self.me, self.full, 1, self.to_dn)

    def cross(self):
        self.got(self.mate, self.full, 2)
        self.send(self.mate, self.full, 4, self.to_up)
        self.send(self.mate, self.full, 6, self.to_dn)

    def relay(self):
        self.got(self.dn, self.full, 0)
        self.send(self.dn, self.lo, 3, self.to_up)
        self.got(self.up, self.full, 1)
        self.send(self.up, self.hi, 5, self.to_dn)

    def far_block(self):
        self.got(self.far, self.lo, 3)
        self.send(self.far, self.lo, 7, self.to_mate)
        self.got(self.far, self.hi, 5)
        self.send(self.far, self.hi, 8, self.to_mate)

    def end(self):
        self.got(self.mate_of(self.dn), self.full, 4)
        self.got(self.mate_of(self.up), self.full, 6)
        self.got(self.mate_of(self.far), self.lo, 7)
        self.got(self.mate_of(self.far), self.hi, 8)

    def drain(self):
        for made in self.sent:
            made.wait_send()


def swap_lanes(x):
    return jnp.concatenate([x[:, 64:], x[:, :64]], axis=1)


def unpack_tail(tail, fill):
    both = jnp.concatenate([tail, swap_lanes(tail)], axis=0)
    keep = lax.broadcasted_iota(jnp.int32, both.shape, 1) < 64
    return jnp.where(keep, both, jnp.broadcast_to(fill, both.shape))


def features_kernel(dels, seq, taps, bias, w_hbm, wo_hbm, wp_ref, row_out, col_out,
                    low, high, cols, gb0, gb1, gm, wp, moved, landed, flat, kv0, kv1, mq, mkv,
                    queries, q_aug, top, acc, ka, va, pooled, mix, mine, arrived, rows_buf, cols_buf, feats, w_ref, wo_ref,
                    send, recv, fetched):
    width, tokens = seq.shape
    variants = dels.shape[1]
    share = SEGS * DEL // 2
    per = 2 * share
    n = 8
    bf = jnp.bfloat16
    c, h, g = lax.axis_index("ctx"), lax.axis_index("head"), lax.axis_index("var")
    dn_h, up_h, far_h = lax.rem(h + 6, n), lax.rem(h + 2, n), lax.rem(h + 4, n)
    sib = h + 1 - 2 * lax.rem(h, 2)
    x0, y0 = c // 4 * 4, lax.rem(c, 4)
    up_c, dn_c, far_c = x0 + lax.rem(y0 + 1, 4), x0 + lax.rem(y0 + 3, 4), x0 + lax.rem(y0 + 2, 4)
    other = lambda t: lax.rem(t + 4, n)
    xp = other(c)
    sib_of = lambda t: t + 1 - 2 * lax.rem(t, 2)

    fetch = [
        pltpu.make_async_copy(w_hbm, w_ref, fetched.at[0]),
        pltpu.make_async_copy(wo_hbm, wo_ref, fetched.at[1]),
    ]
    for made in fetch:
        made.start()
    barrier = pltpu.get_barrier_semaphore()
    peers = [{"ctx": lax.rem(c + k, n)} for k in range(1, n)]
    peers += [{"head": lax.rem(h + k, n)} for k in range(1, n)]
    peers += [{"ctx": xp, "var": 1 - g}]
    for peer in peers:
        pl.semaphore_signal(barrier, inc=1, device_id=peer, device_id_type=MESH)
    for k in range(n):
        source = lax.rem(h + k, n)

        @pl.when(jnp.logical_or(c != h, k != 0))
        def _():
            pl.semaphore_signal(barrier, inc=1, device_id={"ctx": h, "head": source}, device_id_type=MESH)

    for k in range(4):
        line = bias[...] if k == 3 else taps[k : k + 1, :]
        cols[k] = jnp.broadcast_to(line, (128, width)).T
    wp[h] = wp_ref[...]
    run = DEL // 2
    r = lax.broadcasted_iota(jnp.int32, (tokens, 4 * run), 1)
    offset = (r // run - 2) * DIL + (r // (2 * run)) * DIL + r % run
    local_token = lax.broadcasted_iota(jnp.int32, (tokens, 4 * run), 0) + c * tokens - offset

    def gather_runs(v, _):
        for half in range(2):
            pick = (local_token == dels[0, v] + half * run).astype(bf)
            moved[2 * v + half] = jnp.dot(seq[...], pick, preferred_element_type=jnp.float32).astype(bf)
        return 0

    lax.fori_loop(0, variants, gather_runs, 0)
    pl.semaphore_wait(barrier, len(peers) + n - (c == h).astype(jnp.int32))

    def make(src, dst, index, target, arrival=None):
        return pltpu.make_async_remote_copy(
            src_ref=src, dst_ref=dst, send_sem=send.at[index],
            recv_sem=recv.at[index if arrival is None else arrival],
            device_id=(target.get("ctx", c), target.get("head", h), target.get("var", g)), device_id_type=MESH,
        )

    halo_low = make(seq.at[:, pl.ds(tokens - DIL, DIL)], low, 0, {"ctx": lax.rem(c + 1, n)})
    halo_high = make(seq.at[:, pl.ds(0, DIL)], high, 1, {"ctx": lax.rem(c + 7, n)})
    halo_low.start()
    halo_high.start()
    shared = []
    for k in (4, 3, 5, 2, 6, 1, 7):
        to = lax.rem(c + k, n)
        made = make(moved.at[to], landed.at[k - 1], 1 + k, {"ctx": to})
        made.start()
        shared.append(made)

    def head_ring(buf, base):
        return HeadRing(make, buf, buf.shape[1], base, h, dn_h, up_h, far_h, sib, sib_of,
                        {"head": dn_h}, {"head": up_h}, {"head": sib})

    def token_ring(buf, base, to_mate):
        return TokenRing(make, buf, buf.shape[1], base, c, dn_c, up_c, far_c, xp, other,
                         {"ctx": dn_c}, {"ctx": up_c}, to_mate)

    ring_b0, ring_b1, ring_m, ring_p = (head_ring(buf, 10 + 9 * i) for i, buf in enumerate((gb0, gb1, gm, wp)))
    cross = {"ctx": xp, "var": 1 - g}
    ring_k0, ring_k1 = token_ring(kv0, 46, cross), token_ring(kv1, 55, cross)
    ring_o = token_ring(mkv, 73, {"ctx": xp})

    at = lax.broadcasted_iota(jnp.int32, (1, DIL), 1) + c * tokens
    wide = lambda k: jnp.concatenate([cols[k], cols[k]], axis=1)

    def trunk(half, first, length):
        def kept(x, shift, inside=None):
            d = at + (half * DIL + shift) - first
            keep = jnp.logical_or(d < 0, d >= length)
            if inside is not None:
                keep = jnp.logical_and(keep, inside)
            return jnp.where(keep, x.astype(jnp.float32), 0.0)

        here = kept(seq[:, half * DIL : (half + 1) * DIL], 0)
        if half == 0:
            before, after = kept(low[...], -DIL, c != 0), kept(seq[:, DIL:], DIL)
        else:
            before, after = kept(seq[:, :DIL], -DIL), kept(high[...], DIL, c != n - 1)
        conv = wide(0) * before + wide(1) * here + wide(2) * after + wide(3)
        return (here + jax.nn.gelu(conv, approximate=True)).astype(bf)

    ring_p.begin()
    ring_p.relay()
    halo_low.wait()
    gb0[h] = trunk(0, 0, 0)
    ring_b0.begin()
    halo_high.wait()
    gb1[h] = trunk(1, 0, 0)
    ring_b1.begin()

    pool = (
        lax.broadcasted_iota(jnp.int32, (tokens // POOL, tokens), 1) // POOL
        == lax.broadcasted_iota(jnp.int32, (tokens // POOL, tokens), 0)
    ).astype(bf)

    def project(x):
        return jnp.dot(w_ref[...], x, preferred_element_type=jnp.float32).T

    def place(kv, x, count):
        kv[c, :count] = x[:count, HD : 2 * HD].astype(bf)
        kv[c, count:] = pack(x[:count, 2 * HD :].astype(bf))

    ring_p.end()
    ring_b0.relay()
    ring_b1.relay()
    for made in fetch:
        made.wait()
    ring_b0.end()
    x = project(gb0[...].reshape(n * width, DIL))
    place(kv0, x, DIL)
    ring_k0.begin()
    queries[:DIL] = (x[:, :HD] * QSCALE).astype(bf)
    ring_b1.end()
    x = project(gb1[...].reshape(n * width, DIL))
    place(kv1, x, DIL)
    ring_k1.begin()
    queries[DIL:] = (x[:, :HD] * QSCALE).astype(bf)

    total = moved[c].astype(jnp.float32)
    for made in shared:
        made.wait_recv()
    for k in range(1, n):
        total = total + landed[k - 1].astype(jnp.float32)
    runs = [total[:, i * run : (i + 1) * run] for i in range(4)]
    nil = jnp.zeros((width, run), jnp.float32)
    t0, t1, t2, t3 = (cols[k, :, :run] for k in range(4))
    made_rows = []
    for before, here, after in ((runs[0], runs[1], nil), (runs[1], nil, runs[2]), (nil, runs[2], runs[3])):
        conv = t0 * before + t1 * here + t2 * after + t3
        made_rows.append((here + jax.nn.gelu(conv, approximate=True)).astype(bf))
    tail = made_rows[2]
    gm[h, :width] = jnp.concatenate(made_rows[:2], axis=1)
    gm[h, width:] = jnp.concatenate([tail[: width // 2], tail[width // 2 :]], axis=1)
    ring_m.begin()
    ring_k0.cross()
    ring_k0.relay()
    ring_m.relay()
    ring_m.end()
    zero = jnp.zeros((1, 128), bf)
    for k in range(n):
        flat[k * width : (k + 1) * width, :128] = gm[k, :width]
        flat[k * width : (k + 1) * width, 128:] = unpack_tail(gm[k, width:], zero)
    x = project(flat[...])
    mq[c] = (x[:share, :HD] * QSCALE).astype(bf)
    asked = []
    for k in (4, 3, 5, 2, 6, 1, 7):
        made = make(mq.at[c], mq.at[c], 64 + k, {"ctx": lax.rem(c + k, n)})
        made.start()
        asked.append(made)
    place(mkv, x, share)
    ring_o.begin()
    ring_k1.cross()
    ring_k1.relay()

    def variant(v, _):
        first = dels[0, v]
        length = dels[1, v] - first
        own = jnp.concatenate([trunk(0, first, length), trunk(1, first, length)], axis=1)
        mean = lax.dot_general(pool, own, (((1,), (1,)), ((), ())), preferred_element_type=jnp.float32)
        pooled[v] = (mean * (1.0 / POOL)).astype(bf)
        return 0

    lax.fori_loop(0, variants, variant, 0)
    total = jnp.zeros((wo_ref.shape[0], 2 * C), jnp.float32)
    for k in range(0, n, 2):
        two = jnp.concatenate([wp[k], wp[k + 1]], axis=0)
        total = total + jnp.dot(wo_ref[:, k * width : (k + 2) * width], two, preferred_element_type=jnp.float32)
    mix[...] = total.astype(bf)
    ring_k0.far_block()
    for k in range(1, n):
        source = lax.rem(c + n - k, n)
        make(mq.at[source], mq.at[source], 64 + k, {"ctx": lax.rem(c + k, n)}).wait_recv()

    lane = lax.broadcasted_iota(jnp.int32, (1, 128), 1)
    first = jnp.zeros((1, 128), jnp.int32)
    length = jnp.zeros((1, 128), jnp.int32)
    for v in range(variants):
        first = jnp.where(lane == v, dels[0, v], first)
        length = jnp.where(lane == v, dels[1, v] - dels[0, v], length)
    col = lax.broadcasted_iota(jnp.int32, (tokens, per), 1)
    col_step = col // share * (DEL // 2) + col % (DEL // 2)
    col_offset = (col % share // (DEL // 2) - 1) * DIL + col_step
    qpos = lax.broadcasted_iota(jnp.int32, (tokens, per), 0) + c * tokens

    def aim(v, _):
        s0 = dels[0, v]
        count = dels[1, v] - s0
        spot = jnp.logical_and(qpos - col_offset == s0, col_step < count).astype(bf)
        source = jnp.concatenate([mq[2 * v], mq[2 * v + 1]], axis=0)
        moved_q = jnp.dot(spot, source, preferred_element_type=jnp.float32)
        is_mod = changed(qpos[:, :128] - s0, count)
        q_aug[v, :, :HD] = jnp.where(is_mod, moved_q, queries[...].astype(jnp.float32)).astype(bf)
        q_aug[v, :, HD:] = jnp.broadcast_to(jnp.where(lane == v, 1.0, 0.0), (tokens, 128)).astype(bf)
        top[v] = jnp.full((tokens, 128), -3e38, jnp.float32)
        acc[v] = jnp.zeros((tokens, 256), jnp.float32)
        return 0

    lax.fori_loop(0, variants, aim, 0)
    ones = jnp.where(lane == VD - 128, 1.0, 0.0).astype(bf)

    def unit(v, keys, values):
        s = lax.dot_general(q_aug[v], keys, (((1,), (1,)), ((), ())), preferred_element_type=jnp.float32)
        old = top[v]
        new = jnp.maximum(old, jnp.broadcast_to(s.max(1, keepdims=True), old.shape))
        w = jnp.exp2(s - jnp.concatenate([new] * (keys.shape[0] // 128), axis=1)).astype(bf)
        shrink = jnp.exp2(old - new)
        top[v] = new
        acc[v] = acc[v] * jnp.concatenate([shrink, shrink], axis=1) + jnp.dot(
            w, values, preferred_element_type=jnp.float32
        )

    def attend(step, _):
        look = lambda table: sum((step == i).astype(jnp.int32) * t for i, t in enumerate(table) if t)
        away = look((0, 3, 1, 0, 2, 3, 1, 2))
        across = look((0, 0, 0, 1, 0, 1, 1, 1))
        side = x0 + across * (4 - 2 * x0)
        block = side + lax.rem(y0 + away, 4)
        for i, kv in enumerate((kv0, kv1)):
            rows = slice(i * DIL, (i + 1) * DIL)
            ka[rows, :HD] = kv[block, :DIL]
            pos = lax.broadcasted_iota(jnp.int32, (DIL, 128), 0) + (block * tokens + i * DIL)
            ka[rows, HD:] = jnp.where(changed(pos - first, length), BIG, 0.0).astype(bf)
            va[rows, :128] = kv[block, DIL : 2 * DIL]
            va[rows, 128:] = unpack_tail(kv[block, 2 * DIL :], ones)
        for v in range(variants):
            unit(v, ka[...], va[...])
        return 0

    lax.fori_loop(0, 2, attend, 0)
    ring_k1.far_block()
    ring_o.cross()
    ring_o.relay()
    lax.fori_loop(2, 5, attend, 0)
    ring_k0.end()
    ring_k1.end()
    ring_o.far_block()
    lax.fori_loop(5, n, attend, 0)
    for ring in (ring_b0, ring_b1, ring_m, ring_p, ring_k0, ring_k1):
        ring.drain()
    for made in shared + asked:
        made.wait_send()
    ring_o.end()

    row = lax.broadcasted_iota(jnp.int32, (per, 128), 0)
    step = row // share * (DEL // 2) + row % (DEL // 2)
    row_offset = (row % share // (DEL // 2) - 1) * DIL + step
    count = tokens // POOL // 2
    first_sent = []
    for v in range(variants):
        token = dels[0, v] + row_offset
        valid = (step < dels[1, v] - dels[0, v]) & (token >= 0) & (token < n * tokens)
        ka[:per, HD:] = jnp.where(valid, 0.0, BIG).astype(bf)
        for i in range(2):
            rows = slice(i * share, (i + 1) * share)
            ka[rows, :HD] = mkv[2 * v + i, :share]
            va[rows, :128] = mkv[2 * v + i, share : 2 * share]
            va[rows, 128:] = unpack_tail(mkv[2 * v + i, 2 * share :], ones)
        unit(v, ka[:per], va[:per])
        out = (acc[v, :, :VD] / acc[v, :, VD : VD + 1]).astype(bf)
        mean = jnp.dot(pool, out, preferred_element_type=jnp.float32) * (1.0 / POOL)
        part = jnp.dot(mean.astype(bf), mix[...], preferred_element_type=jnp.float32) + jnp.dot(
            pooled[v], wp_ref[...], preferred_element_type=jnp.float32
        )
        for i in range(2):
            to = 2 * v + i
            mine[to] = part[i * count : (i + 1) * count].astype(bf)
            made = make(mine.at[to], arrived.at[h], 82 + to, {"head": to}, 82 + h)
            first_sent.append(made)

            @pl.when(h != to)
            def _():
                made.start()

            @pl.when(h == to)
            def _():
                arrived[h] = mine[to]

    for k in range(n):
        @pl.when(h != k)
        def _():
            make(mine.at[k], arrived.at[k], 82 + k, {"head": k}).wait_recv()

    total = arrived[0].astype(jnp.float32)
    for k in range(1, n):
        total = total + arrived[k].astype(jnp.float32)
    feats[0] = total[:, :C].astype(bf)
    feats[1] = total[:, C:].astype(bf)
    rows_buf[h] = feats[0]
    for k in range(n):
        to = lax.rem(c + k, n)

        @pl.when(jnp.logical_or(c != h, k != 0))
        def _():
            make(feats.at[1], cols_buf.at[h], 98 + k, {"ctx": to, "head": c}, 98 + h).start()

        @pl.when(jnp.logical_and(c == h, k == 0))
        def _():
            cols_buf[h] = feats[1]

    for k in range(1, n):
        make(feats.at[0], rows_buf.at[h], 90 + k, {"head": lax.rem(h + k, n)}).start()
    ring_o.drain()
    for k, made in enumerate(first_sent):
        @pl.when(h != k)
        def _():
            made.wait_send()

    for k in range(1, n):
        source = lax.rem(h + n - k, n)
        made = make(feats.at[0], rows_buf.at[source], 90 + k, {"head": lax.rem(h + k, n)})
        made.wait_recv()
        made.wait_send()
    for k in range(n):
        @pl.when(jnp.logical_or(c != h, k != h))
        def _():
            make(feats.at[1], cols_buf.at[k], 98 + k, {"head": lax.rem(h + 1, n)}).wait_recv()

        @pl.when(jnp.logical_or(c != h, k != 0))
        def _():
            make(feats.at[1], cols_buf.at[h], 98 + k, {"head": lax.rem(h + 1, n)}).wait_send()
    row_out[...] = rows_buf[...]
    col_out[...] = cols_buf[...]


def features(sequence, deletions, conv_taps, conv_bias, w_proj, w_out, w_pair):
    tokens, width = sequence.shape
    variants = deletions.shape[0]
    n = 8
    share = SEGS * DEL // 2
    vm = pl.BlockSpec(memory_space=pltpu.VMEM)
    bf, f32 = jnp.bfloat16, jnp.float32
    part = variants * tokens // POOL // n
    scratch = [
        ((width, DIL), bf),
        ((width, DIL), bf),
        ((4, width, 128), f32),
        ((n, width, DIL), bf),
        ((n, width, DIL), bf),
        ((n, share * 3 // 2, 128), bf),
        ((n, width, 2 * C), bf),
        ((n, width, 2 * DEL), bf),
        ((n - 1, width, 2 * DEL), bf),
        ((n * width, 256), bf),
        ((n, DIL * 5 // 2, 128), bf),
        ((n, DIL * 5 // 2, 128), bf),
        ((n, share, 128), bf),
        ((n, share * 5 // 2, 128), bf),
        ((tokens, HD), bf),
        ((variants, tokens, 256), bf),
        ((variants, tokens, 128), f32),
        ((variants, tokens, 256), f32),
        ((tokens, 256), bf),
        ((tokens, 256), bf),
        ((variants, tokens // POOL, width), bf),
        ((w_out.shape[0], 2 * C), bf),
        ((n, part, 2 * C), bf),
        ((n, part, 2 * C), bf),
        ((n, part, C), bf),
        ((n, part, C), bf),
        ((2, part, C), bf),
        ((w_proj.shape[1], w_proj.shape[0]), bf),
        (w_out.shape, bf),
    ]
    return pl.pallas_call(
        features_kernel,
        out_shape=(jax.ShapeDtypeStruct((n, part, C), bf),) * 2,
        in_specs=[pl.BlockSpec(memory_space=pltpu.SMEM)] + [vm] * 3 + [pl.BlockSpec(memory_space=pl.ANY)] * 2 + [vm],
        out_specs=(vm, vm),
        scratch_shapes=[pltpu.VMEM(shape, kind) for shape, kind in scratch]
        + [pltpu.SemaphoreType.DMA((106,)), pltpu.SemaphoreType.DMA((106,)), pltpu.SemaphoreType.DMA((2,))],
        compiler_params=pltpu.CompilerParams(
            collective_id=0, has_side_effects=True, vmem_limit_bytes=56 * 2**20
        ),
    )(deletions.T, sequence.T, conv_taps, conv_bias.reshape(1, width), w_proj.T, w_out, w_pair)


def local(sequence, deletions, conv_taps, conv_bias, w_proj, w_out, w_pair, dist_table):
    variants = deletions.shape[0]
    row_feats, col_feats = features(sequence, deletions, conv_taps, conv_bias, w_proj, w_out, w_pair)
    shape = (variants, sequence.shape[0] // POOL, C)
    return pair_map(row_feats.reshape(shape), col_feats.reshape(shape), dist_table)


def solution(mesh):
    in_specs = (
        P("ctx", "head"),
        P("var", None),
        P(None, "head"),
        P("head"),
        P(None, "head"),
        P("head", None),
        P("head", None),
        P(),
    )
    out_specs = P("var", "ctx", "head", None)
    return jax.shard_map(local, mesh=mesh, in_specs=in_specs, out_specs=out_specs, check_vma=False)
```
